32 devices in a mesh: seq: 4 (over y, core), items: 8 (over z, x).
Axes of the slice: x: 2, y: 2, z: 4, core: 2. Of those that a mesh axis runs over, the one named last changes fastest.
Arguments:
- block_in: bfloat16 [16, 640, 768], P('items', 'seq'), may hold values from -6 to 6
- lengths: int32 [16], P('items'), may hold values from 257 to 577, as said below
- gain_attn: float32 [768], replicated, may hold values from 0.5 to 1.5
- w_query: bfloat16 [768, 768], replicated, may hold values from -0.21875 to 0.21875
- w_key: bfloat16 [768, 768], replicated, may hold values from -0.21875 to 0.21875
- w_value: bfloat16 [768, 768], replicated, may hold values from -0.21875 to 0.21875
- w_out: bfloat16 [768, 768], replicated, may hold values from -1.75 to 1.75
- gain_ffn: float32 [768], replicated, may hold values from 0.5 to 1.5
- w_gate: bfloat16 [768, 2048], replicated, may hold values from -0.21875 to 0.21875
- w_up: bfloat16 [768, 2048], replicated, may hold values from -0.21875 to 0.21875
- w_down: bfloat16 [2048, 768], replicated, may hold values from -0.125 to 0.125
- cotangent: bfloat16 [16, 640, 768], P('items', 'seq'), may hold values from -6 to 6
Outputs:
- block_out: bfloat16 [16, 640, 768], P('items', 'seq')
- grad_input: bfloat16 [16, 640, 768], P('items', 'seq')
- grad_gain_attn: float32 [768], P('items')
- grad_w_query: float32 [768, 768], P('items')
- grad_w_key: float32 [768, 768], P('items')
- grad_w_value: float32 [768, 768], P('items')
- grad_w_out: float32 [768, 768], P('items')
- grad_gain_ffn: float32 [768], P('items')
- grad_w_gate: float32 [768, 2048], P('items')
- grad_w_up: float32 [768, 2048], P('items')
- grad_w_down: float32 [2048, 768], P('items')
The draws below stay inside these ranges and needn't reach their ends.
Inputs may be any that keep to these rules, and one draw needn't show every extreme that they name: `lengths`: each item's length is 257 or 577; in each aligned block of 2 items at least one has 577.
All inputs are finite; a program needn't handle non-finite values.
Results may differ from the reference program's by a relative error of at most 0.02.
Values may be sent and summed in bfloat16 or wider, within the bound.
A program may use at most 128 MiB of HBM per device.

```python
import jax
import jax.numpy as jnp
from jax import lax

D = 768
H = 12
HD = 64
FF = 2048
SIDE_S = 16
SIDE_L = 24
SHORT = 257
LONG = 577
PAD = 640
ITEMS_DEV = 2
ITEMS = 16


def draw_lengths(key, part):
    key = jax.random.fold_in(key, 7)
    coin_key, pick_key = jax.random.split(key)
    coins = jax.random.randint(coin_key, (ITEMS,), 0, 2)
    blocks = ITEMS // ITEMS_DEV
    picks = jax.random.randint(pick_key, (blocks,), 0, ITEMS_DEV)
    forced = (jnp.arange(ITEMS_DEV)[None, :] == picks[:, None]).reshape(ITEMS).astype(jnp.int32)
    longer = jnp.maximum(coins, forced)
    return jnp.where(longer == 1, LONG, SHORT).astype(jnp.int32)


def level_of(rng, dims, cuts, low, high):
    factor_of, own = 1.0, jax.random.fold_in(rng, 6)
    for dim, blocks in cuts:
        heights = jnp.exp(jax.random.uniform(jax.random.fold_in(own, dim), (blocks,), jnp.float32, low / len(cuts), high / len(cuts)))
        factor_of = factor_of * jnp.repeat(heights, dims[dim] // blocks).reshape([-1 if axis == dim else 1 for axis in range(len(dims))])
    return factor_of


def noise(key, shape, scale, most, cuts=(), kind=jnp.bfloat16):
    gain = level_of(key, shape, cuts, -0.22, 0.18) if cuts else 1.0
    result = jax.random.normal(key, shape, jnp.float32) * scale * gain
    return jnp.minimum(jnp.maximum(result, -most), most).astype(kind)


def setup_inputs(seed: int = 0) -> dict:
    key_of = jax.random.split(jax.random.key(seed), 13)
    block_in = noise(key_of[0], (ITEMS, PAD, D), 1.0, 6.0, ((0, 8), (1, 4)))
    lengths = draw_lengths(jax.random.fold_in(key_of[12], 71), 0)
    gain_attn = jnp.clip(1.0 + 0.1 * jax.random.normal(key_of[2], (D,), jnp.float32), 0.5, 1.5)
    w_query = noise(key_of[3], (D, D), D ** -0.5, 0.21875)
    w_key = noise(key_of[4], (D, D), D ** -0.5, 0.21875)
    w_value = noise(key_of[5], (D, D), D ** -0.5, 0.21875)
    w_out = noise(key_of[6], (D, D), (max(D // 64, 1)) ** -0.5, 1.75)
    gain_ffn = jnp.clip(1.0 + 0.1 * jax.random.normal(key_of[7], (D,), jnp.float32), 0.5, 1.5)
    w_gate = noise(key_of[8], (D, FF), D ** -0.5, 0.21875)
    w_up = noise(key_of[9], (D, FF), D ** -0.5, 0.21875)
    w_down = noise(key_of[10], (FF, D), FF ** -0.5, 0.125)
    cotangent = noise(key_of[11], (ITEMS, PAD, D), 1.0, 6.0, ((0, 8), (1, 4)))
    return {"block_in": block_in, "lengths": lengths, "gain_attn": gain_attn, "w_query": w_query, "w_key": w_key, "w_value": w_value, "w_out": w_out, "gain_ffn": gain_ffn, "w_gate": w_gate, "w_up": w_up, "w_down": w_down, "cotangent": cotangent}


@jax.custom_vjp
def low(v):
    return lax.optimization_barrier(v.astype(jnp.bfloat16)).astype(jnp.float32)

@jax.custom_vjp
def low_back(v):
    return v

def low_keep(v):
    return (low(v), None)

def low_pass(kept, grad):
    return (grad,)

def back_keep(v):
    return (v, None)

def back_low(kept, grad):
    return (low(grad),)
low.defvjp(low_keep, low_pass)
low_back.defvjp(back_keep, back_low)
highest = lax.Precision.HIGHEST
epsilon = 1e-05

def grid_places(lengths, rows):
    side = jnp.where(lengths == LONG, SIDE_L, SIDE_S).astype(jnp.int32)[:, None]
    place = rows[None, :] - 1
    valid = (place >= 0) & (rows[None, :] < lengths[:, None])
    place = jnp.where(valid, place, 0).astype(jnp.int32)
    return ((place // side).astype(jnp.int32), (place % side).astype(jnp.int32))

def rotary_tables(lengths, rows):
    grid_row, grid_col = grid_places(lengths, rows)
    quarter = HD // 4
    freq = 10000.0 ** (-jnp.arange(quarter, dtype=jnp.float32) / quarter)
    angle_row = grid_row[..., None].astype(jnp.float32) * freq
    angle_col = grid_col[..., None].astype(jnp.float32) * freq
    cosine = jnp.concatenate([jnp.cos(angle_row), jnp.cos(angle_row), jnp.cos(angle_col), jnp.cos(angle_col)], -1)
    sine = jnp.concatenate([jnp.sin(angle_row), jnp.sin(angle_row), jnp.sin(angle_col), jnp.sin(angle_col)], -1)
    return (cosine, sine)

def turn(values):
    quarter = HD // 4
    first = values[..., 0:quarter]
    second = values[..., quarter:2 * quarter]
    third = values[..., 2 * quarter:3 * quarter]
    fourth = values[..., 3 * quarter:]
    return jnp.concatenate([-second, first, -fourth, third], -1)

def rotate(values, cosine, sine):
    return values * cosine[:, :, None, :] + turn(values) * sine[:, :, None, :]

def project(left, right):
    return jnp.einsum('bpd,de->bpe', left, right, precision=highest)

def forward(block, gain_attn, w_query, w_key, w_value, w_out, gain_ffn, w_gate, w_up, w_down, cosine, sine, allowed):
    batch, length = (block.shape[0], block.shape[1])
    normed = low(block * lax.rsqrt(lax.optimization_barrier(jnp.mean(block * block, -1, keepdims=True)) + epsilon) * gain_attn)
    query = low_back(project(normed, w_query)).reshape(batch, length, H, HD)
    keys = low_back(project(normed, w_key)).reshape(batch, length, H, HD)
    query = low(rotate(query, cosine, sine))
    keys = low(rotate(keys, cosine, sine))
    values = low(low_back(project(normed, w_value))).reshape(batch, length, H, HD)
    scores = low_back(HD ** (-0.5) * jnp.einsum('bqhe,bkhe->bhqk', query, keys, precision=highest))
    scores = jnp.where(allowed[:, None], scores, -1e+30)
    top = lax.optimization_barrier(jnp.max(scores, -1, keepdims=True))
    expo = jnp.exp(scores - top)
    chance = low(expo / lax.optimization_barrier(jnp.sum(expo, -1, keepdims=True)))
    mixed = jnp.einsum('bhqk,bkhe->bqhe', chance, values, precision=highest)
    mixed = low(low_back(mixed)).reshape(batch, length, H * HD)
    middle = block + low_back(project(mixed, w_out))
    normed_ffn = low(middle * lax.rsqrt(lax.optimization_barrier(jnp.mean(middle * middle, -1, keepdims=True)) + epsilon) * gain_ffn)
    gate = low_back(project(normed_ffn, w_gate))
    up = low_back(project(normed_ffn, w_up))
    hidden = low(jax.nn.silu(gate) * up)
    return middle + low_back(project(hidden, w_down))

def reference(block_in, lengths, gain_attn, w_query, w_key, w_value, w_out, gain_ffn, w_gate, w_up, w_down, cotangent):
    group = 4
    rows = jnp.arange(PAD, dtype=jnp.int32)
    params = (gain_attn.astype(jnp.float32), w_query.astype(jnp.float32), w_key.astype(jnp.float32), w_value.astype(jnp.float32), w_out.astype(jnp.float32), gain_ffn.astype(jnp.float32), w_gate.astype(jnp.float32), w_up.astype(jnp.float32), w_down.astype(jnp.float32))
    inputs = block_in.reshape(ITEMS // group, group, PAD, D)
    cotans = cotangent.reshape(ITEMS // group, group, PAD, D)
    groups_len = lengths.reshape(ITEMS // group, group)

    def one_group(totals, pieces):
        part_in, part_cot, part_len = pieces
        cosine, sine = rotary_tables(part_len, rows)
        allowed = (rows[None, :] <= rows[:, None])[None] & (rows[None, None, :] < part_len[:, None, None])

        def apply(block, *weights):
            return forward(block, *weights, cosine, sine, allowed)
        output, pullback = jax.vjp(apply, part_in.astype(jnp.float32), *params)
        grads = pullback(part_cot.astype(jnp.float32))
        totals = tuple((total + grad for total, grad in zip(totals, grads[1:])))
        return (totals, (output.astype(jnp.bfloat16), grads[0].astype(jnp.bfloat16)))
    init = tuple((jnp.zeros_like(param) for param in params))
    totals, (outputs, input_grads) = lax.scan(one_group, init, (inputs, cotans, groups_len))
    return (outputs.reshape(ITEMS, PAD, D), input_grads.reshape(ITEMS, PAD, D), totals[0], totals[1], totals[2], totals[3], totals[4], totals[5], totals[6], totals[7], totals[8])
```

```python
import functools

import jax
import jax.numpy as jnp
import numpy as np
from jax import lax
from jax.experimental import pallas as pl
from jax.experimental.pallas import tpu as pltpu
from jax.sharding import PartitionSpec as P

HD = 64
SIDE_S = 16
SIDE_L = 24
LONG = 577


epsilon = 1e-05


def grid_places(lengths, rows):
    side = jnp.where(lengths == LONG, SIDE_L, SIDE_S).astype(jnp.int32)[:, None]
    place = rows[None, :] - 1
    valid = (place >= 0) & (rows[None, :] < lengths[:, None])
    place = jnp.where(valid, place, 0)
    return (place // side, place % side)


def rotary_tables(lengths, rows):
    grid_row, grid_col = grid_places(lengths, rows)
    quarter = HD // 4
    freq = 10000.0 ** (-jnp.arange(quarter, dtype=jnp.float32) / quarter)
    angle_row = grid_row[..., None].astype(jnp.float32) * freq
    angle_col = grid_col[..., None].astype(jnp.float32) * freq
    cosine = jnp.concatenate(
        [jnp.cos(angle_row), jnp.cos(angle_row), jnp.cos(angle_col), jnp.cos(angle_col)], -1
    )
    sine = jnp.concatenate(
        [jnp.sin(angle_row), jnp.sin(angle_row), jnp.sin(angle_col), jnp.sin(angle_col)], -1
    )
    return (cosine[:, :, None, :], sine[:, :, None, :])


def turn(values):
    quarter = HD // 4
    first = values[..., 0:quarter]
    second = values[..., quarter : 2 * quarter]
    third = values[..., 2 * quarter : 3 * quarter]
    fourth = values[..., 3 * quarter :]
    return jnp.concatenate([-second, first, -fourth, third], -1)


def project(left, right):
    return jnp.einsum("ird,de->ire", left, right, preferred_element_type=jnp.float32)


def back_project(grad, weight):
    return jnp.einsum("ire,de->ird", grad, weight, preferred_element_type=jnp.float32)


def weight_grad(left, right):
    return jnp.einsum("ird,ire->de", left, right, preferred_element_type=jnp.float32)


def norm_back(grad_normed, unit, scale, gain):
    scaled = grad_normed * gain
    return scale * (scaled - unit * jnp.mean(scaled * unit, -1, keepdims=True))


def body(
    block_in,
    lengths,
    gain_attn,
    w_query,
    w_key,
    w_value,
    w_out,
    gain_ffn,
    w_gate,
    w_up,
    w_down,
    cotangent,
):
    count, rows_here, width = block_in.shape
    heads = width // HD
    length_all = rows_here * lax.axis_size("seq")
    factor = HD ** (-0.5)
    query_rows = lax.axis_index("seq") * rows_here + jnp.arange(rows_here, dtype=jnp.int32)
    key_rows = jnp.arange(length_all, dtype=jnp.int32)
    cosine, sine = rotary_tables(lengths, query_rows)
    allowed = (key_rows[None, None, :] <= query_rows[None, :, None]) & (
        key_rows[None, None, :] < lengths[:, None, None]
    )

    def heads_of(array):
        return array.reshape(array.shape[0], array.shape[1], heads, HD)

    def attention_scores(query, keys_all):
        raw = (
            jnp.einsum(
                "irhe,iphe->ihrp", query, heads_of(keys_all), preferred_element_type=jnp.float32
            )
            * factor
        )
        return jnp.where(allowed[:, None], raw, -1e30)

    source = block_in.astype(jnp.float32)
    scale_attn = lax.rsqrt(jnp.mean(source * source, -1, keepdims=True) + epsilon)
    unit_attn = source * scale_attn
    normed = (unit_attn * gain_attn).astype(jnp.bfloat16)
    query_pre = heads_of(project(normed, w_query))
    keys_pre = heads_of(project(normed, w_key))
    query = (query_pre * cosine + turn(query_pre) * sine).astype(jnp.bfloat16)
    keys = (
        (keys_pre * cosine + turn(keys_pre) * sine)
        .astype(jnp.bfloat16)
        .reshape(count, rows_here, width)
    )
    values = project(normed, w_value).astype(jnp.bfloat16)
    keys_all, values_all = (
        lax.all_gather(keys, "seq", axis=1, tiled=True),
        lax.all_gather(values, "seq", axis=1, tiled=True),
    )
    scores = attention_scores(query, keys_all)
    top = jnp.max(scores, -1, keepdims=True)
    expo = jnp.exp(scores - top)
    summed = jnp.sum(expo, -1, keepdims=True)
    chance = expo / summed
    log_total = top + jnp.log(summed)
    mixed = (
        jnp.einsum(
            "ihrp,iphe->irhe",
            chance.astype(jnp.bfloat16),
            heads_of(values_all),
            preferred_element_type=jnp.float32,
        )
        .reshape(count, rows_here, width)
        .astype(jnp.bfloat16)
    )
    middle = source + project(mixed, w_out)
    scale_ffn = lax.rsqrt(jnp.mean(middle * middle, -1, keepdims=True) + epsilon)
    unit_ffn = middle * scale_ffn
    normed_ffn = (unit_ffn * gain_ffn).astype(jnp.bfloat16)
    gate = project(normed_ffn, w_gate)
    up = project(normed_ffn, w_up)
    sigma = jax.nn.sigmoid(gate)
    hidden = (gate * sigma * up).astype(jnp.bfloat16)
    block_out = (middle + project(hidden, w_down)).astype(jnp.bfloat16)
    incoming = cotangent.astype(jnp.float32)
    grad_w_down = weight_grad(hidden, cotangent)
    grad_hidden = back_project(cotangent, w_down)
    grad_gate = (grad_hidden * up * sigma * (1.0 + gate * (1.0 - sigma))).astype(jnp.bfloat16)
    grad_up = (grad_hidden * gate * sigma).astype(jnp.bfloat16)
    grad_w_gate = weight_grad(normed_ffn, grad_gate)
    grad_w_up = weight_grad(normed_ffn, grad_up)
    grad_normed_ffn = back_project(grad_gate, w_gate) + back_project(grad_up, w_up)
    grad_gain_ffn = jnp.sum(grad_normed_ffn * unit_ffn, axis=(0, 1))
    grad_middle = incoming + norm_back(grad_normed_ffn, unit_ffn, scale_ffn, gain_ffn)
    grad_branch = grad_middle.astype(jnp.bfloat16)
    grad_w_out = weight_grad(mixed, grad_branch)
    grad_mixed = heads_of(back_project(grad_branch, w_out)).astype(jnp.bfloat16)
    keys_back, values_back = (keys_all, values_all)
    chance_back = jnp.exp(attention_scores(query, keys_back) - log_total)
    grad_chance = jnp.einsum(
        "irhe,iphe->ihrp", grad_mixed, heads_of(values_back), preferred_element_type=jnp.float32
    )
    inner = jnp.sum(grad_chance * chance_back, -1, keepdims=True)
    grad_scores = (chance_back * (grad_chance - inner)).astype(jnp.bfloat16)
    grad_query = (
        jnp.einsum(
            "ihrp,iphe->irhe", grad_scores, heads_of(keys_back), preferred_element_type=jnp.float32
        )
        * factor
    )
    grad_values_sum = jnp.einsum(
        "ihrp,irhe->iphe",
        chance_back.astype(jnp.bfloat16),
        grad_mixed,
        preferred_element_type=jnp.float32,
    )
    grad_keys_sum = (
        jnp.einsum("ihrp,irhe->iphe", grad_scores, query, preferred_element_type=jnp.float32)
        * factor
    )
    grad_keys, grad_values = (
        lax.psum_scatter(
            grad_keys_sum.reshape(count, length_all, width).astype(jnp.bfloat16),
            "seq",
            scatter_dimension=1,
            tiled=True,
        ).astype(jnp.float32),
        lax.psum_scatter(
            grad_values_sum.reshape(count, length_all, width).astype(jnp.bfloat16),
            "seq",
            scatter_dimension=1,
            tiled=True,
        ).astype(jnp.float32),
    )
    grad_query_pre = (
        (grad_query * cosine - turn(grad_query * sine))
        .reshape(count, rows_here, width)
        .astype(jnp.bfloat16)
    )
    grad_keys_heads = heads_of(grad_keys)
    grad_keys_pre = (
        (grad_keys_heads * cosine - turn(grad_keys_heads * sine))
        .reshape(count, rows_here, width)
        .astype(jnp.bfloat16)
    )
    grad_values_pre = grad_values.astype(jnp.bfloat16)
    grad_w_query = weight_grad(normed, grad_query_pre)
    grad_w_key = weight_grad(normed, grad_keys_pre)
    grad_w_value = weight_grad(normed, grad_values_pre)
    grad_normed = (
        back_project(grad_query_pre, w_query)
        + back_project(grad_keys_pre, w_key)
        + back_project(grad_values_pre, w_value)
    )
    grad_gain_attn = jnp.sum(grad_normed * unit_attn, axis=(0, 1))
    grad_input = (grad_middle + norm_back(grad_normed, unit_attn, scale_attn, gain_attn)).astype(
        jnp.bfloat16
    )
    shares = (
        lax.psum_scatter(
            grad_gain_attn.astype(jnp.bfloat16), "items", scatter_dimension=0, tiled=True
        ).astype(jnp.float32),
        lax.psum_scatter(
            grad_w_query.astype(jnp.bfloat16), "items", scatter_dimension=0, tiled=True
        ).astype(jnp.float32),
        lax.psum_scatter(
            grad_w_key.astype(jnp.bfloat16), "items", scatter_dimension=0, tiled=True
        ).astype(jnp.float32),
        lax.psum_scatter(
            grad_w_value.astype(jnp.bfloat16), "items", scatter_dimension=0, tiled=True
        ).astype(jnp.float32),
        lax.psum_scatter(
            grad_w_out.astype(jnp.bfloat16), "items", scatter_dimension=0, tiled=True
        ).astype(jnp.float32),
        lax.psum_scatter(
            grad_gain_ffn.astype(jnp.bfloat16), "items", scatter_dimension=0, tiled=True
        ).astype(jnp.float32),
        lax.psum_scatter(
            grad_w_gate.astype(jnp.bfloat16), "items", scatter_dimension=0, tiled=True
        ).astype(jnp.float32),
        lax.psum_scatter(
            grad_w_up.astype(jnp.bfloat16), "items", scatter_dimension=0, tiled=True
        ).astype(jnp.float32),
        lax.psum_scatter(
            grad_w_down.astype(jnp.bfloat16), "items", scatter_dimension=0, tiled=True
        ).astype(jnp.float32),
    )
    summed = (
        lax.psum(shares[0].astype(jnp.bfloat16), "seq").astype(jnp.float32),
        lax.psum(shares[1].astype(jnp.bfloat16), "seq").astype(jnp.float32),
        lax.psum(shares[2].astype(jnp.bfloat16), "seq").astype(jnp.float32),
        lax.psum(shares[3].astype(jnp.bfloat16), "seq").astype(jnp.float32),
        lax.psum(shares[4].astype(jnp.bfloat16), "seq").astype(jnp.float32),
        lax.psum(shares[5].astype(jnp.bfloat16), "seq").astype(jnp.float32),
        lax.psum(shares[6].astype(jnp.bfloat16), "seq").astype(jnp.float32),
        lax.psum(shares[7].astype(jnp.bfloat16), "seq").astype(jnp.float32),
        lax.psum(shares[8].astype(jnp.bfloat16), "seq").astype(jnp.float32),
    )
    return (
        block_out,
        grad_input,
        summed[0],
        summed[1],
        summed[2],
        summed[3],
        summed[4],
        summed[5],
        summed[6],
        summed[7],
        summed[8],
    )


MESH = pl.DeviceIdType.MESH
WIDE = 256
LOW = jnp.bfloat16
F32 = jnp.float32
NEVER = -1e30


def dot(left, right):
    return lax.dot_general(left, right, (((1,), (0,)), ((), ())), preferred_element_type=F32)


def dot_nt(left, right):
    return lax.dot_general(left, right, (((1,), (1,)), ((), ())), preferred_element_type=F32)


def dot_tn(left, right):
    return lax.dot_general(left, right, (((0,), (0,)), ((), ())), preferred_element_type=F32)


def rope_constants(rows):
    quarter = HD // 4
    freq = 10000.0 ** (-np.arange(quarter) / quarter)
    tables = []
    for side, length in ((SIDE_S, SIDE_S * SIDE_S + 1), (SIDE_L, SIDE_L * SIDE_L + 1)):
        place = np.arange(rows) - 1
        place = np.where((place >= 0) & (place < length - 1), place, 0)
        row = (place // side)[:, None] * freq
        col = (place % side)[:, None] * freq
        cosine = np.concatenate([np.cos(row), np.cos(row), np.cos(col), np.cos(col)], -1)
        sine = np.concatenate([-np.sin(row), np.sin(row), -np.sin(col), np.sin(col)], -1)
        tables += [np.concatenate([cosine, cosine], -1), np.concatenate([sine, sine], -1)]
    return np.stack(tables).astype(np.float32)


def swap_quarters(values):
    lane = lax.broadcasted_iota(jnp.int32, values.shape, 1)
    first = (lane % (HD // 2)) < HD // 4
    return jnp.where(
        first, pltpu.roll(values, 2 * HD - HD // 4, 1), pltpu.roll(values, HD // 4, 1)
    )


def fused(geo, *refs):
    rows_here, width, hidden_all = geo
    (
        lens, gain_a, gain_f, x_hbm, cot_hbm, tab_hbm,
        wq, wk, wv, wo, wg, wu, wd,
        bo_hbm, gi_hbm, fa_hbm, fd_hbm, fq_hbm, gain_hbm,
        x4, cot4, tab, wqkv_v, wo_v, wg_v, wu_v, wd_v,
        nrm, nrm_t, qkv, chance, mix_own, mix_in, mix, mix_t,
        mid, nf, nf_t, hid, hid_t, gg, gu, big,
        gnf_out, gnf_in, sb, rb, bo, bo_in, gb, gmx, ds_s, gqkv, sb2, rb2, gi, gi_in,
        gain_s, gain_x, gain_y, gain_z, gain_c,
        pa, r1a, r2a, r3a, fa, pd, r1d, r2d, r3d, fd, pq, r1q, r2q, r3q, fq,
        sem_w, sem_in_s, sem_in_r, sem_core_s, sem_core_r, sem_gain_s, sem_gain_r, sem_o,
        sa_s, sa_r, sd_s, sd_r, sq_s, sq_r,
    ) = refs
    s = lax.axis_index("seq")
    i = lax.axis_index("items")
    y, c = s // 2, s % 2
    z, x = i // 2, i % 2
    rows = 4 * rows_here
    half = width // 2
    ff = hidden_all // 2
    pairs = half // 128
    step = 32
    per = rows_here // step
    blocks = [(r0, min(256, rows - r0)) for r0 in range(0, rows, 256)]

    def device(y_to, c_to, z_to, x_to):
        return (y_to * 2 + c_to, z_to * 2 + x_to)

    sibling = device(y, 1 - c, z, x)
    y_dev = device(1 - y, c, z, x)
    x_dev = device(y, c, z, 1 - x)
    z_devs = [device(y, c, lax.rem(z + d, 4), x) for d in (1, 2, 3)]

    started = []

    def send(src, dst, s_sem, r_sem, to):
        return pltpu.make_async_remote_copy(
            src_ref=src, dst_ref=dst, send_sem=s_sem, recv_sem=r_sem,
            device_id=to, device_id_type=MESH,
        )

    def weight_copies():
        copies = [pltpu.make_async_copy(tab_hbm, tab, sem_w.at[0])]
        mine = pl.ds(pl.multiple_of(c * half, half), half)
        for t, w in enumerate((wq, wk, wv)):
            copies.append(
                pltpu.make_async_copy(
                    w.at[:, mine], wqkv_v.at[:, pl.ds(t * half, half)], sem_w.at[1 + t]
                )
            )
        copies.append(pltpu.make_async_copy(wo, wo_v, sem_w.at[4]))
        for b in range(ff // 128):
            far = pl.ds(pl.multiple_of(256 * b + 128 * c, 128), 128)
            near = pl.ds(128 * b, 128)
            copies.append(pltpu.make_async_copy(wg.at[:, far], wg_v.at[:, near], sem_w.at[5 + 3 * b]))
            copies.append(pltpu.make_async_copy(wu.at[:, far], wu_v.at[:, near], sem_w.at[6 + 3 * b]))
            copies.append(pltpu.make_async_copy(wd.at[far], wd_v.at[near], sem_w.at[7 + 3 * b]))
        return copies

    weights = weight_copies()
    own_x = pltpu.make_async_copy(x_hbm.at[y], x4.at[s], sem_o.at[0])
    own_cot = pltpu.make_async_copy(cot_hbm.at[y], cot4.at[s], sem_o.at[1])
    own_x.start()
    for copy in weights[:4]:
        copy.start()

    barrier = pltpu.get_barrier_semaphore()
    for to in [sibling, y_dev, x_dev] + z_devs:
        pl.semaphore_signal(barrier, inc=1, device_id=to, device_id_type=MESH)
    pl.semaphore_wait(barrier, 6)

    s_y = (1 - y) * 2 + c
    across_x = send(x_hbm.at[1 - y], x4.at[s], sem_in_s.at[0], sem_in_r.at[0], y_dev)
    beside_x = send(x_hbm.at[y], x4.at[s], sem_in_s.at[1], sem_in_r.at[1], sibling)
    across_x.start()
    beside_x.start()
    across_c = send(cot_hbm.at[1 - y], cot4.at[s], sem_in_s.at[2], sem_in_r.at[2], y_dev)
    beside_c = send(cot_hbm.at[y], cot4.at[s], sem_in_s.at[3], sem_in_r.at[3], sibling)
    across_c.start()
    beside_c.start()
    own_cot.start()
    for copy in weights[4:]:
        copy.start()
    relay_x = send(x4.at[s_y], x4.at[s_y], sem_in_s.at[4], sem_in_r.at[4], sibling)
    relay_c = send(cot4.at[s_y], cot4.at[s_y], sem_in_s.at[5], sem_in_r.at[5], sibling)

    length = lens[y]

    def norm_rows(piece):
        def one(b, carry):
            here = pl.ds(pl.multiple_of(b * step, step), step)
            values = x4[piece, here, :].astype(F32)
            scale = lax.rsqrt(jnp.mean(values * values, -1, keepdims=True) + epsilon)
            there = pl.ds(pl.multiple_of(piece * rows_here + b * step, step), step)
            nrm[there, :] = (values * scale * gain_a[...]).astype(LOW)
            return carry

        lax.fori_loop(0, per, one, 0)

    def project_rows(part):
        base = pl.multiple_of(part * 2 * rows_here, 32)
        here = pl.ds(base, 2 * rows_here)
        cosine = jnp.where(length == LONG, tab[2, here, :], tab[0, here, :])
        sine = jnp.where(length == LONG, tab[3, here, :], tab[1, here, :])
        for t in range(3):
            product = dot(nrm[here, :], wqkv_v[:, t * half : (t + 1) * half])
            for p in range(pairs):
                lanes = product[:, 128 * p : 128 * (p + 1)]
                if t < 2:
                    lanes = lanes * cosine + swap_quarters(lanes) * sine
                if t == 0:
                    lanes = lanes.astype(LOW).astype(F32) * HD ** (-0.5)
                qkv[t, here, 128 * p : 128 * (p + 1)] = lanes.astype(LOW)

    own_x.wait()
    norm_rows(s)
    beside_x.wait_recv()
    norm_rows(2 * y + 1 - c)
    for copy in weights[:4]:
        copy.wait()
    project_rows(y)
    across_x.wait_recv()
    relay_x.start()
    norm_rows(s_y)
    relay_x.wait_recv()
    norm_rows(2 * (1 - y) + 1 - c)
    project_rows(1 - y)

    lane = lax.broadcasted_iota(jnp.int32, (1, 128), 1)
    left_head = lane < HD
    masks = [(lane // HD == n).astype(F32).astype(LOW) for n in range(2)]

    def mix_copy(pair):
        return send(
            mix_own.at[pair], mix_in.at[pair], sem_core_s.at[pair], sem_core_r.at[pair], sibling
        )

    def attend(pair, carry):
        lanes = pl.ds(pl.multiple_of(pair * 128, 128), 128)
        for r0, rb in blocks:
            nk = r0 + rb
            row = r0 + lax.broadcasted_iota(jnp.int32, (rb, nk), 0)
            col = lax.broadcasted_iota(jnp.int32, (rb, nk), 1)
            allowed = (col <= row) & (col < length)
            both = []
            for n in range(2):
                query = qkv[0, r0:nk, lanes] * masks[n]
                scores = jnp.where(allowed, dot_nt(query, qkv[1, :nk, lanes]), NEVER)
                expo = jnp.exp(scores - jnp.max(scores, -1, keepdims=True))
                low = (expo * (1.0 / jnp.sum(expo, -1, keepdims=True))).astype(LOW)
                chance[pair * 2 + n, r0:nk, :nk] = low
                both.append(dot(low, qkv[2, :nk, lanes]))
            mix_own[pair, r0:nk, :] = jnp.where(left_head, both[0], both[1]).astype(LOW)
        mix_copy(pair).start()
        return carry

    lax.fori_loop(0, pairs, attend, 0)

    across_c.wait_recv()
    relay_c.start()

    def turn_rows(src, dst):
        def one(b, carry):
            here = pl.ds(pl.multiple_of(b * 128, 128), 128)
            dst[:, here] = src[here, :].T
            return carry

        lax.fori_loop(0, rows // 128, one, 0)

    def place_mix(src, at):
        def one(p, carry):
            mix[:, pl.ds(pl.multiple_of(at * half + p * 128, 128), 128)] = src[p]
            return carry

        lax.fori_loop(0, pairs, one, 0)

    place_mix(mix_own, c)
    turn_rows(nrm, nrm_t)
    for p in range(pairs):
        mix_copy(p).wait_recv()
    place_mix(mix_in, 1 - c)

    weights[4].wait()

    def chunk(n, wide=WIDE):
        return pl.ds(pl.multiple_of(n * wide, wide), wide)

    def out_project(n, carry):
        mid[:, chunk(n)] = (
            dot(mix[...], wo_v[:, chunk(n)])
            + x4[:, :, chunk(n)].reshape(rows, WIDE).astype(F32)
        )
        return carry

    lax.fori_loop(0, width // WIDE, out_project, 0)

    def second_norm(b, carry):
        here = pl.ds(pl.multiple_of(b * step, step), step)
        values = mid[here, :]
        scale = lax.rsqrt(jnp.mean(values * values, -1, keepdims=True) + epsilon)
        nf[here, :] = (values * scale * gain_f[...]).astype(LOW)
        return carry

    lax.fori_loop(0, rows // step, second_norm, 0)
    turn_rows(nf, nf_t)
    for copy in weights[5:]:
        copy.wait()
    own_cot.wait()
    beside_c.wait_recv()
    relay_c.wait_recv()

    class Group:
        def __init__(self, parts, r1, r2, r3, fin, s_sem, r_sem):
            self.parts, self.r1, self.r2, self.r3, self.fin = parts, r1, r2, r3, fin
            self.s_sem, self.r_sem = s_sem, r_sem

        def copy1(self, k, x_first):
            src = self.parts.at[k, :, 1 - x] if x_first else self.parts.at[k, :, :, 1 - y]
            to = x_dev if x_first else y_dev
            return send(src, self.r1.at[k], self.s_sem.at[k, 0], self.r_sem.at[k, 0], to)

        def copy2(self, k, x_first):
            src = self.r1.at[k, :, 1 - y] if x_first else self.r1.at[k, :, 1 - x]
            to = y_dev if x_first else x_dev
            return send(src, self.r2.at[k], self.s_sem.at[k, 1], self.r_sem.at[k, 1], to)

        def copy3(self, k, d):
            return send(
                self.r2.at[k, lax.rem(z + d, 4)], self.r3.at[k, d - 1],
                self.s_sem.at[k, 1 + d], self.r_sem.at[k, 1 + d], z_devs[d - 1],
            )

        def copy4(self, k, n):
            at = self.fin.at[k, c, y] if n < 2 else self.fin.at[k, c, 1 - y]
            to = y_dev if n == 0 else sibling
            return send(at, at, self.s_sem.at[k, 5 + n], self.r_sem.at[k, 5 + n], to)

        def step1(self, k, x_first):
            self.copy1(k, x_first).start()

        def step2(self, k, x_first):
            self.copy1(k, x_first).wait_recv()

            def add(other):
                for zz in range(4):
                    if x_first:
                        h = 1 - y if other else y
                        at, own = (k, zz, h), (k, zz, x, h)
                    else:
                        xx = 1 - x if other else x
                        at, own = (k, zz, xx), (k, zz, xx, y)
                    self.r1[at] = (self.r1[at].astype(F32) + self.parts[own].astype(F32)).astype(LOW)

            add(True)
            self.copy2(k, x_first).start()
            add(False)

        def step3(self, k, x_first):
            self.copy2(k, x_first).wait_recv()
            at = y if x_first else x
            for d in (1, 2, 3, 0):
                to = lax.rem(z + d, 4)
                self.r2[k, to] = (
                    self.r2[k, to].astype(F32) + self.r1[k, to, at].astype(F32)
                ).astype(LOW)
                if d:
                    self.copy3(k, d).start()

        def step4(self, k, x_first):
            total = self.r2[k, z].astype(F32)
            for d in (1, 2, 3):
                self.copy3(k, d).wait_recv()
                total = total + self.r3[k, d - 1].astype(F32)
            self.fin[k, c, y] = total.astype(LOW)
            self.copy4(k, 0).start()
            self.copy4(k, 1).start()

        def step5(self, k, x_first):
            self.copy4(k, 0).wait_recv()
            self.copy4(k, 2).start()

        def step6(self, k, x_first):
            self.copy4(k, 1).wait_recv()
            self.copy4(k, 2).wait_recv()

        def sent(self, k, x_first):
            self.copy1(k, x_first).wait_send()
            self.copy2(k, x_first).wait_send()
            for d in (1, 2, 3):
                self.copy3(k, d).wait_send()
            for n in range(3):
                self.copy4(k, n).wait_send()

    group_a = Group(pa, r1a, r2a, r3a, fa, sa_s, sa_r)
    group_d = Group(pd, r1d, r2d, r3d, fd, sd_s, sd_r)
    group_q = Group(pq, r1q, r2q, r3q, fq, sq_s, sq_r)
    chunks_f = ff // WIDE
    chunks_w = width // WIDE

    def feed(n, carry):
        at = chunk(n)
        big[:, 0:WIDE] = dot(nf[...], wg_v[:, at])
        big[:, WIDE : 2 * WIDE] = dot(nf[...], wu_v[:, at])
        big[:, 2 * WIDE : 3 * WIDE] = dot_nt(cot4[...].reshape(rows, width), wd_v[at, :])

        def one(b, inner):
            here = pl.ds(pl.multiple_of(b * step, step), step)
            gate = big[here, 0:WIDE]
            up = big[here, WIDE : 2 * WIDE]
            back = big[here, 2 * WIDE : 3 * WIDE]
            sigma = 0.5 * jnp.tanh(0.5 * gate) + 0.5
            silu = gate * sigma
            hid[here, at] = (silu * up).astype(LOW)
            gg[here, at] = (back * up * (sigma + silu * (1.0 - sigma))).astype(LOW)
            gu[here, at] = (back * silu).astype(LOW)
            return inner

        lax.fori_loop(0, rows // step, one, 0)
        shape = pa.shape[1:]
        pa[n] = dot(nf_t[...], gg[:, at]).reshape(shape).astype(LOW)
        group_a.step1(n, True)
        pa[n + chunks_f] = dot(nf_t[...], gu[:, at]).reshape(shape).astype(LOW)
        group_a.step1(n + chunks_f, False)
        hid_t[at, :] = hid[:, at].T
        return carry

    lax.fori_loop(0, chunks_f, feed, 0)

    def gnf_copy(n):
        return send(
            gnf_out.at[n], gnf_in.at[n], sem_core_s.at[pairs + n], sem_core_r.at[pairs + n], sibling
        )

    def back_ffn(n, carry):
        partial = dot_nt(gg[...], wg_v[chunk(n), :]) + dot_nt(gu[...], wu_v[chunk(n), :])
        big[:, chunk(n)] = partial
        gnf_out[n] = partial.astype(LOW)
        gnf_copy(n).start()
        return carry

    lax.fori_loop(0, chunks_w, back_ffn, 0)

    def down(n, carry):
        big[:, chunk(n + chunks_w)] = dot(hid[...], wd_v[:, chunk(n)])
        return carry

    lax.fori_loop(0, chunks_w, down, 0)
    n_core = pairs + chunks_w
    bo_copy = send(sb, rb, sem_core_s.at[n_core], sem_core_r.at[n_core], sibling)
    far = slice(width, 2 * width)

    def for_rows(core, fn):
        for yy in range(2):
            def one(b, carry, yy=yy):
                base = pl.multiple_of((2 * yy + core) * rows_here + b * step, step)
                fn(yy, b, pl.ds(base, step), pl.ds(pl.multiple_of(b * step, step), step))
                return carry

            lax.fori_loop(0, per, one, 0)

    def pack_bo(yy, b, here, there):
        sb[yy, there, :] = big[here, far].astype(LOW)

    for_rows(1 - c, pack_bo)
    bo_copy.start()

    d_first = [n % 2 == 0 for n in range(chunks_w)]

    for n in range(chunks_w):
        at = slice(n * WIDE, (n + 1) * WIDE)
        pd[n] = (
            dot(hid_t[...], cot4[:, :, at].reshape(rows, WIDE)).reshape(pd.shape[1:]).astype(LOW)
        )
        group_d.step1(n, d_first[n])

    bo_copy.wait_recv()

    def finish_bo(yy, b, here, there):
        bo[yy, there, :] = (mid[here, :] + big[here, far] + rb[yy, there, :].astype(F32)).astype(LOW)

    for_rows(c, finish_bo)
    bo_across = send(bo.at[1 - y], bo_in, sem_in_s.at[6], sem_in_r.at[6], y_dev)
    bo_across.start()

    for n in range(chunks_w):
        gnf_copy(n).wait_recv()

    def middle_back(b, total):
        here = pl.ds(pl.multiple_of(b * step, step), step)
        values = mid[here, :]
        grad = big[here, 0:width] + jnp.concatenate(
            [gnf_in[n, here, :].astype(F32) for n in range(chunks_w)], -1
        )
        scale = lax.rsqrt(jnp.mean(values * values, -1, keepdims=True) + epsilon)
        unit = values * scale
        total = total + (grad * unit).reshape(step // 8, 8, width).sum(0)
        scaled = grad * gain_f[...]
        inner = jnp.mean(scaled * unit, -1, keepdims=True)
        out = cot4[b // per, pl.ds(pl.multiple_of(lax.rem(b, per) * step, step), step), :].astype(F32)
        out = out + scale * (scaled - unit * inner)
        mid[here, :] = out
        gb[here, :] = out.astype(LOW)
        return total

    total_f = lax.fori_loop(0, rows // step, middle_back, jnp.zeros((8, width), F32))

    turn_rows(mix, mix_t)
    mine = pl.ds(pl.multiple_of(c * half, half), half)
    pq[0] = dot(mix_t[...], gb[:, mine]).reshape(pq.shape[1:]).astype(LOW)
    group_q.step1(0, True)
    gmx[...] = dot_nt(gb[...], wo_v[mine, :]).astype(LOW)

    def attend_back(pair, carry):
        lanes = pl.ds(pl.multiple_of(pair * 128, 128), 128)

        def keep(n, at, off, value):
            where_ = pl.ds(pl.multiple_of(off * 128, 128), 128)
            if n:
                value = jnp.where(left_head, big[at, where_], value)
            big[at, where_] = value

        for n in range(2):
            head = pair * 2 + n
            for r0, rb_ in blocks:
                nk = r0 + rb_
                grad = gmx[r0:nk, lanes] * masks[n]
                prob = chance[head, r0:nk, :nk].astype(F32)
                each = dot_nt(grad, qkv[2, :nk, lanes]) * prob
                low = (each - prob * jnp.sum(each, -1, keepdims=True)).astype(LOW)
                ds_s[r0:nk, :nk] = low
                keep(n, slice(r0, nk), 0, dot(low, qkv[1, :nk, lanes]))
            for k0, kb in blocks:
                at = slice(k0, k0 + kb)
                keep(n, at, 1, dot_tn(ds_s[k0:, at], qkv[0, k0:, lanes]))
                keep(n, at, 2, dot_tn(chance[head, k0:, at], gmx[k0:, lanes]))

        def one(b, inner):
            here = pl.ds(pl.multiple_of(b * 64, 64), 64)
            cosine = jnp.where(length == LONG, tab[2, here, :], tab[0, here, :])
            sine = jnp.where(length == LONG, tab[3, here, :], tab[1, here, :])
            for t in range(3):
                values = big[here, 128 * t : 128 * (t + 1)]
                if t == 0:
                    values = values * HD ** (-0.5)
                if t < 2:
                    values = values * cosine - swap_quarters(values) * sine
                gqkv[here, pl.ds(pl.multiple_of(t * half + pair * 128, 128), 128)] = values.astype(LOW)
            return inner

        lax.fori_loop(0, rows // 64, one, 0)
        return carry

    lax.fori_loop(0, pairs, attend_back, 0)

    q_first = [True, True, False, True]
    for t in range(3):
        pq[1 + t] = (
            dot(nrm_t[...], gqkv[:, t * half : (t + 1) * half]).reshape(pq.shape[1:]).astype(LOW)
        )
        group_q.step1(1 + t, q_first[1 + t])

    def back_attn(n, carry):
        big[:, chunk(n)] = dot_nt(gqkv[...], wqkv_v[chunk(n), :])
        return carry

    lax.fori_loop(0, chunks_w, back_attn, 0)

    def pack_gi(yy, b, here, there):
        sb2[yy, there, :] = big[here, 0:width].astype(LOW)

    for_rows(1 - c, pack_gi)
    gi_copy = send(sb2, rb2, sem_core_s.at[n_core + 1], sem_core_r.at[n_core + 1], sibling)
    gi_copy.start()

    def gain_back(b, total):
        here = pl.ds(pl.multiple_of(b * step, step), step)
        values = x4[b // per, pl.ds(pl.multiple_of(lax.rem(b, per) * step, step), step), :].astype(F32)
        scale = lax.rsqrt(jnp.mean(values * values, -1, keepdims=True) + epsilon)
        return total + (big[here, 0:width] * (values * scale)).reshape(step // 8, 8, width).sum(0)

    total_a = lax.fori_loop(0, rows // step, gain_back, jnp.zeros((8, width), F32))
    gain_s[...] = jnp.concatenate(
        [
            jnp.broadcast_to(jnp.sum(total_a, 0, keepdims=True), (8, width)),
            jnp.broadcast_to(jnp.sum(total_f, 0, keepdims=True), (8, width)),
        ],
        0,
    )
    gain_1 = send(gain_s, gain_x, sem_gain_s.at[0], sem_gain_r.at[0], x_dev)
    gain_1.start()
    gi_copy.wait_recv()

    def finish_gi(yy, b, here, there):
        values = x4[2 * yy + c, there, :].astype(F32)
        scale = lax.rsqrt(jnp.mean(values * values, -1, keepdims=True) + epsilon)
        unit = values * scale
        scaled = (big[here, 0:width] + rb2[yy, there, :].astype(F32)) * gain_a[...]
        inner = jnp.mean(scaled * unit, -1, keepdims=True)
        gi[yy, there, :] = (mid[here, :] + scale * (scaled - unit * inner)).astype(LOW)

    for_rows(c, finish_gi)
    gi_across = send(gi.at[1 - y], gi_in, sem_in_s.at[7], sem_in_r.at[7], y_dev)
    gi_across.start()

    todo = []
    for n in range(chunks_f):
        todo += [(group_a, n, True), (group_a, n + chunks_f, False)]
    todo += [(group_d, n, d_first[n]) for n in range(chunks_w)]
    todo += [(group_q, n, q_first[n]) for n in range(4)]
    lag = 4
    names = ["step2", "step3", "step4", "step5", "step6"]
    for tick in range(len(todo) + lag * (len(names) - 1)):
        for stage in range(len(names) - 1, -1, -1):
            at = tick - lag * stage
            if 0 <= at < len(todo):
                group, k, first = todo[at]
                getattr(group, names[stage])(k, first)

    gain_1.wait()
    gain_s[...] = gain_s[...] + gain_x[...]
    gain_2 = send(gain_s, gain_y, sem_gain_s.at[1], sem_gain_r.at[1], y_dev)
    gain_2.start()
    gain_2.wait()
    gain_s[...] = gain_s[...] + gain_y[...]
    gain_3 = [
        send(gain_s, gain_z.at[d], sem_gain_s.at[2 + d], sem_gain_r.at[2 + d], z_devs[d])
        for d in range(3)
    ]
    for copy in gain_3:
        copy.start()
    for copy in gain_3:
        copy.wait()
    gain_s[...] = gain_s[...] + gain_z[0] + gain_z[1] + gain_z[2]
    gain_4 = send(gain_s, gain_c, sem_gain_s.at[5], sem_gain_r.at[5], sibling)
    gain_4.start()
    gain_4.wait()
    gain_c[0:8, :] = gain_s[0:8, :] + gain_c[0:8, :]

    outs = [
        pltpu.make_async_copy(fa, fa_hbm, sem_o.at[2]),
        pltpu.make_async_copy(fd, fd_hbm, sem_o.at[3]),
        pltpu.make_async_copy(fq, fq_hbm, sem_o.at[4]),
        pltpu.make_async_copy(gain_c, gain_hbm, sem_o.at[5]),
        pltpu.make_async_copy(bo.at[y], bo_hbm.at[y], sem_o.at[6]),
        pltpu.make_async_copy(gi.at[y], gi_hbm.at[y], sem_o.at[7]),
    ]
    for copy in outs:
        copy.start()
    bo_across.wait_recv()
    gi_across.wait_recv()
    outs += [
        pltpu.make_async_copy(bo_in, bo_hbm.at[1 - y], sem_o.at[8]),
        pltpu.make_async_copy(gi_in, gi_hbm.at[1 - y], sem_o.at[9]),
    ]
    for copy in outs[6:]:
        copy.start()
    for copy in outs:
        copy.wait()

    for copy in (across_x, beside_x, across_c, beside_c, relay_x, relay_c, bo_across, gi_across):
        copy.wait_send()
    for p in range(pairs):
        mix_copy(p).wait_send()
    for n in range(chunks_w):
        gnf_copy(n).wait_send()
    bo_copy.wait_send()
    gi_copy.wait_send()
    for group, k, first in todo:
        group.sent(k, first)


def spread(chunks_f, fa, fd, fq, bo, gi, bo_out, gi_out, dq, dk, dv, do, dg, du, dd):
    bo_out[...] = bo[...]
    gi_out[...] = gi[...]
    rows = fa.shape[3]
    for core in range(2):
        for h in range(2):
            at = slice(h * rows, (h + 1) * rows)
            for n in range(chunks_f):
                for b in range(WIDE // 128):
                    far = 256 * (n * (WIDE // 128) + b) + 128 * core
                    near = slice(128 * b, 128 * (b + 1))
                    dg[at, far : far + 128] = fa[n, core, h, :, near].astype(F32)
                    du[at, far : far + 128] = fa[n + chunks_f, core, h, :, near].astype(F32)
            half = fq.shape[4]
            lanes = slice(core * half, (core + 1) * half)
            for n, ref in enumerate((do, dq, dk, dv)):
                ref[at, lanes] = fq[n, core, h].astype(F32)
            deep = fd.shape[3]
            at = slice((2 * core + h) * deep, (2 * core + h + 1) * deep)
            for n in range(fd.shape[0]):
                dd[at, WIDE * n : WIDE * (n + 1)] = fd[n, core, h].astype(F32)


def item_per_chip(
    block_in, lengths, gain_attn, w_query, w_key, w_value, w_out, gain_ffn, w_gate, w_up, w_down,
    cotangent,
):
    _, rows_here, width = block_in.shape
    hidden_all = w_gate.shape[1]
    rows = rows_here * lax.axis_size("seq")
    shares = lax.axis_size("items")
    half, ff = width // 2, hidden_all // 2
    pairs = half // 128
    chunks_f, chunks_w = ff // WIDE, width // WIDE
    thin, deep = width // shares // 2, ff // shares // 2
    tables = jnp.asarray(rope_constants(rows))
    any_ = pl.BlockSpec(memory_space=pl.ANY)
    vmem = pl.BlockSpec(memory_space=pltpu.VMEM)

    def group(n, r, w):
        return [
            pltpu.VMEM((n, 4, 2, 2, r, w), LOW),
            pltpu.VMEM((n, 4, 2, r, w), LOW),
            pltpu.VMEM((n, 4, r, w), LOW),
            pltpu.VMEM((n, 3, r, w), LOW),
            pltpu.VMEM((n, 2, 2, r, w), LOW),
        ]

    def low(*shape):
        return pltpu.VMEM(shape, LOW)

    def full(*shape):
        return pltpu.VMEM(shape, F32)

    dma = pltpu.SemaphoreType.DMA
    scratch = [
        low(4, rows_here, width), low(4, rows_here, width), full(4, rows, 128),
        low(width, 3 * half), low(width, width), low(width, ff), low(width, ff), low(ff, width),
        low(rows, width), low(width, rows), low(3, rows, half), low(2 * pairs, rows, rows),
        low(pairs, rows, 128), low(pairs, rows, 128), low(rows, width), low(width, rows),
        full(rows, width), low(rows, width), low(width, rows), low(rows, ff), low(ff, rows),
        low(rows, ff), low(rows, ff), full(rows, 2 * width),
        low(chunks_w, rows, WIDE), low(chunks_w, rows, WIDE),
        low(2, rows_here, width), low(2, rows_here, width),
        low(2, rows_here, width), low(rows_here, width),
        low(rows, width), low(rows, half), low(rows, rows), low(rows, 3 * half),
        low(2, rows_here, width), low(2, rows_here, width),
        low(2, rows_here, width), low(rows_here, width),
        full(16, width), full(16, width), full(16, width), full(3, 16, width), full(16, width),
    ]
    scratch += group(2 * chunks_f, thin, WIDE) + group(chunks_w, deep, WIDE) + group(4, thin, half)
    scratch += [
        dma((5 + 3 * (ff // 128),)), dma((8,)), dma((8,)),
        dma((pairs + chunks_w + 2,)), dma((pairs + chunks_w + 2,)), dma((6,)), dma((6,)), dma((10,)),
        dma((2 * chunks_f, 8)), dma((2 * chunks_f, 8)), dma((chunks_w, 8)), dma((chunks_w, 8)),
        dma((4, 8)), dma((4, 8)),
    ]
    shape = jax.ShapeDtypeStruct
    bo, gi, fa, fd, fq, gains = pl.pallas_call(
        functools.partial(fused, (rows_here, width, hidden_all)),
        out_shape=(
            shape(block_in.shape, LOW), shape(block_in.shape, LOW),
            shape((2 * chunks_f, 2, 2, thin, WIDE), LOW), shape((chunks_w, 2, 2, deep, WIDE), LOW),
            shape((4, 2, 2, thin, half), LOW), shape((16, width), F32),
        ),
        in_specs=[pl.BlockSpec(memory_space=pltpu.SMEM), vmem, vmem] + [any_] * 10,
        out_specs=(any_,) * 6,
        scratch_shapes=scratch,
        compiler_params=pltpu.CompilerParams(
            collective_id=0, has_side_effects=True, vmem_limit_bytes=63 * 2**20
        ),
        name="block",
    )(
        lengths, gain_attn.reshape(1, width), gain_ffn.reshape(1, width), block_in, cotangent, tables,
        w_query, w_key, w_value, w_out, w_gate, w_up, w_down,
    )
    thick = (width // shares, width)
    bo, gi, dq, dk, dv, do, dg, du, dd = pl.pallas_call(
        functools.partial(spread, chunks_f),
        out_shape=(
            shape(block_in.shape, LOW), shape(block_in.shape, LOW),
            shape(thick, F32), shape(thick, F32), shape(thick, F32), shape(thick, F32),
            shape((width // shares, hidden_all), F32), shape((width // shares, hidden_all), F32),
            shape((hidden_all // shares, width), F32),
        ),
        in_specs=[vmem] * 5,
        out_specs=(vmem,) * 9,
        compiler_params=pltpu.CompilerParams(vmem_limit_bytes=32 * 2**20),
        name="spread",
    )(fa, fd, fq, bo, gi)
    share = width // shares
    gains = lax.dynamic_slice(gains, (0, lax.axis_index("items") * share), (16, share))
    return bo, gi, gains[0], dq, dk, dv, do, gains[8], dg, du, dd


def solution(mesh):
    fits = mesh.shape["seq"] == 4 and mesh.shape["items"] == 8
    return jax.shard_map(
        item_per_chip if fits else body,
        mesh=mesh,
        in_specs=(P("items", "seq", None), P("items")) + (P(),) * 9 + (P("items", "seq", None),),
        out_specs=(
            (P("items", "seq", None),) * 2
            + (P("items"),) + (P("items", None),) * 4
            + (P("items"),) + (P("items", None),) * 3
        ),
        check_vma=False,
    )
```

```python
import functools

import jax
import jax.numpy as jnp
import numpy as np
from jax import lax
from jax.experimental import pallas as pl
from jax.experimental.pallas import tpu as pltpu
from jax.sharding import PartitionSpec as P

HD = 64
SIDE_S = 16
SIDE_L = 24
LONG = 577


epsilon = 1e-05


def grid_places(lengths, rows):
    side = jnp.where(lengths == LONG, SIDE_L, SIDE_S).astype(jnp.int32)[:, None]
    place = rows[None, :] - 1
    valid = (place >= 0) & (rows[None, :] < lengths[:, None])
    place = jnp.where(valid, place, 0)
    return (place // side, place % side)


def rotary_tables(lengths, rows):
    grid_row, grid_col = grid_places(lengths, rows)
    quarter = HD // 4
    freq = 10000.0 ** (-jnp.arange(quarter, dtype=jnp.float32) / quarter)
    angle_row = grid_row[..., None].astype(jnp.float32) * freq
    angle_col = grid_col[..., None].astype(jnp.float32) * freq
    cosine = jnp.concatenate(
        [jnp.cos(angle_row), jnp.cos(angle_row), jnp.cos(angle_col), jnp.cos(angle_col)], -1
    )
    sine = jnp.concatenate(
        [jnp.sin(angle_row), jnp.sin(angle_row), jnp.sin(angle_col), jnp.sin(angle_col)], -1
    )
    return (cosine[:, :, None, :], sine[:, :, None, :])


def turn(values):
    quarter = HD // 4
    first = values[..., 0:quarter]
    second = values[..., quarter : 2 * quarter]
    third = values[..., 2 * quarter : 3 * quarter]
    fourth = values[..., 3 * quarter :]
    return jnp.concatenate([-second, first, -fourth, third], -1)


def project(left, right):
    return jnp.einsum("ird,de->ire", left, right, preferred_element_type=jnp.float32)


def back_project(grad, weight):
    return jnp.einsum("ire,de->ird", grad, weight, preferred_element_type=jnp.float32)


def weight_grad(left, right):
    return jnp.einsum("ird,ire->de", left, right, preferred_element_type=jnp.float32)


def norm_back(grad_normed, unit, scale, gain):
    scaled = grad_normed * gain
    return scale * (scaled - unit * jnp.mean(scaled * unit, -1, keepdims=True))


def body(
    block_in,
    lengths,
    gain_attn,
    w_query,
    w_key,
    w_value,
    w_out,
    gain_ffn,
    w_gate,
    w_up,
    w_down,
    cotangent,
):
    count, rows_here, width = block_in.shape
    heads = width // HD
    length_all = rows_here * lax.axis_size("seq")
    factor = HD ** (-0.5)
    query_rows = lax.axis_index("seq") * rows_here + jnp.arange(rows_here, dtype=jnp.int32)
    key_rows = jnp.arange(length_all, dtype=jnp.int32)
    cosine, sine = rotary_tables(lengths, query_rows)
    allowed = (key_rows[None, None, :] <= query_rows[None, :, None]) & (
        key_rows[None, None, :] < lengths[:, None, None]
    )

    def heads_of(array):
        return array.reshape(array.shape[0], array.shape[1], heads, HD)

    def attention_scores(query, keys_all):
        raw = (
            jnp.einsum(
                "irhe,iphe->ihrp", query, heads_of(keys_all), preferred_element_type=jnp.float32
            )
            * factor
        )
        return jnp.where(allowed[:, None], raw, -1e30)

    source = block_in.astype(jnp.float32)
    scale_attn = lax.rsqrt(jnp.mean(source * source, -1, keepdims=True) + epsilon)
    unit_attn = source * scale_attn
    normed = (unit_attn * gain_attn).astype(jnp.bfloat16)
    query_pre = heads_of(project(normed, w_query))
    keys_pre = heads_of(project(normed, w_key))
    query = (query_pre * cosine + turn(query_pre) * sine).astype(jnp.bfloat16)
    keys = (
        (keys_pre * cosine + turn(keys_pre) * sine)
        .astype(jnp.bfloat16)
        .reshape(count, rows_here, width)
    )
    values = project(normed, w_value).astype(jnp.bfloat16)
    keys_all, values_all = (
        lax.all_gather(keys, "seq", axis=1, tiled=True),
        lax.all_gather(values, "seq", axis=1, tiled=True),
    )
    scores = attention_scores(query, keys_all)
    top = jnp.max(scores, -1, keepdims=True)
    expo = jnp.exp(scores - top)
    summed = jnp.sum(expo, -1, keepdims=True)
    chance = expo / summed
    log_total = top + jnp.log(summed)
    mixed = (
        jnp.einsum(
            "ihrp,iphe->irhe",
            chance.astype(jnp.bfloat16),
            heads_of(values_all),
            preferred_element_type=jnp.float32,
        )
        .reshape(count, rows_here, width)
        .astype(jnp.bfloat16)
    )
    middle = source + project(mixed, w_out)
    scale_ffn = lax.rsqrt(jnp.mean(middle * middle, -1, keepdims=True) + epsilon)
    unit_ffn = middle * scale_ffn
    normed_ffn = (unit_ffn * gain_ffn).astype(jnp.bfloat16)
    gate = project(normed_ffn, w_gate)
    up = project(normed_ffn, w_up)
    sigma = jax.nn.sigmoid(gate)
    hidden = (gate * sigma * up).astype(jnp.bfloat16)
    block_out = (middle + project(hidden, w_down)).astype(jnp.bfloat16)
    incoming = cotangent.astype(jnp.float32)
    grad_w_down = weight_grad(hidden, cotangent)
    grad_hidden = back_project(cotangent, w_down)
    grad_gate = (grad_hidden * up * sigma * (1.0 + gate * (1.0 - sigma))).astype(jnp.bfloat16)
    grad_up = (grad_hidden * gate * sigma).astype(jnp.bfloat16)
    grad_w_gate = weight_grad(normed_ffn, grad_gate)
    grad_w_up = weight_grad(normed_ffn, grad_up)
    grad_normed_ffn = back_project(grad_gate, w_gate) + back_project(grad_up, w_up)
    grad_gain_ffn = jnp.sum(grad_normed_ffn * unit_ffn, axis=(0, 1))
    grad_middle = incoming + norm_back(grad_normed_ffn, unit_ffn, scale_ffn, gain_ffn)
    grad_branch = grad_middle.astype(jnp.bfloat16)
    grad_w_out = weight_grad(mixed, grad_branch)
    grad_mixed = heads_of(back_project(grad_branch, w_out)).astype(jnp.bfloat16)
    keys_back, values_back = (keys_all, values_all)
    chance_back = jnp.exp(attention_scores(query, keys_back) - log_total)
    grad_chance = jnp.einsum(
        "irhe,iphe->ihrp", grad_mixed, heads_of(values_back), preferred_element_type=jnp.float32
    )
    inner = jnp.sum(grad_chance * chance_back, -1, keepdims=True)
    grad_scores = (chance_back * (grad_chance - inner)).astype(jnp.bfloat16)
    grad_query = (
        jnp.einsum(
            "ihrp,iphe->irhe", grad_scores, heads_of(keys_back), preferred_element_type=jnp.float32
        )
        * factor
    )
    grad_values_sum = jnp.einsum(
        "ihrp,irhe->iphe",
        chance_back.astype(jnp.bfloat16),
        grad_mixed,
        preferred_element_type=jnp.float32,
    )
    grad_keys_sum = (
        jnp.einsum("ihrp,irhe->iphe", grad_scores, query, preferred_element_type=jnp.float32)
        * factor
    )
    grad_keys, grad_values = (
        lax.psum_scatter(
            grad_keys_sum.reshape(count, length_all, width).astype(jnp.bfloat16),
            "seq",
            scatter_dimension=1,
            tiled=True,
        ).astype(jnp.float32),
        lax.psum_scatter(
            grad_values_sum.reshape(count, length_all, width).astype(jnp.bfloat16),
            "seq",
            scatter_dimension=1,
            tiled=True,
        ).astype(jnp.float32),
    )
    grad_query_pre = (
        (grad_query * cosine - turn(grad_query * sine))
        .reshape(count, rows_here, width)
        .astype(jnp.bfloat16)
    )
    grad_keys_heads = heads_of(grad_keys)
    grad_keys_pre = (
        (grad_keys_heads * cosine - turn(grad_keys_heads * sine))
        .reshape(count, rows_here, width)
        .astype(jnp.bfloat16)
    )
    grad_values_pre = grad_values.astype(jnp.bfloat16)
    grad_w_query = weight_grad(normed, grad_query_pre)
    grad_w_key = weight_grad(normed, grad_keys_pre)
    grad_w_value = weight_grad(normed, grad_values_pre)
    grad_normed = (
        back_project(grad_query_pre, w_query)
        + back_project(grad_keys_pre, w_key)
        + back_project(grad_values_pre, w_value)
    )
    grad_gain_attn = jnp.sum(grad_normed * unit_attn, axis=(0, 1))
    grad_input = (grad_middle + norm_back(grad_normed, unit_attn, scale_attn, gain_attn)).astype(
        jnp.bfloat16
    )
    shares = (
        lax.psum_scatter(
            grad_gain_attn.astype(jnp.bfloat16), "items", scatter_dimension=0, tiled=True
        ).astype(jnp.float32),
        lax.psum_scatter(
            grad_w_query.astype(jnp.bfloat16), "items", scatter_dimension=0, tiled=True
        ).astype(jnp.float32),
        lax.psum_scatter(
            grad_w_key.astype(jnp.bfloat16), "items", scatter_dimension=0, tiled=True
        ).astype(jnp.float32),
        lax.psum_scatter(
            grad_w_value.astype(jnp.bfloat16), "items", scatter_dimension=0, tiled=True
        ).astype(jnp.float32),
        lax.psum_scatter(
            grad_w_out.astype(jnp.bfloat16), "items", scatter_dimension=0, tiled=True
        ).astype(jnp.float32),
        lax.psum_scatter(
            grad_gain_ffn.astype(jnp.bfloat16), "items", scatter_dimension=0, tiled=True
        ).astype(jnp.float32),
        lax.psum_scatter(
            grad_w_gate.astype(jnp.bfloat16), "items", scatter_dimension=0, tiled=True
        ).astype(jnp.float32),
        lax.psum_scatter(
            grad_w_up.astype(jnp.bfloat16), "items", scatter_dimension=0, tiled=True
        ).astype(jnp.float32),
        lax.psum_scatter(
            grad_w_down.astype(jnp.bfloat16), "items", scatter_dimension=0, tiled=True
        ).astype(jnp.float32),
    )
    summed = (
        lax.psum(shares[0].astype(jnp.bfloat16), "seq").astype(jnp.float32),
        lax.psum(shares[1].astype(jnp.bfloat16), "seq").astype(jnp.float32),
        lax.psum(shares[2].astype(jnp.bfloat16), "seq").astype(jnp.float32),
        lax.psum(shares[3].astype(jnp.bfloat16), "seq").astype(jnp.float32),
        lax.psum(shares[4].astype(jnp.bfloat16), "seq").astype(jnp.float32),
        lax.psum(shares[5].astype(jnp.bfloat16), "seq").astype(jnp.float32),
        lax.psum(shares[6].astype(jnp.bfloat16), "seq").astype(jnp.float32),
        lax.psum(shares[7].astype(jnp.bfloat16), "seq").astype(jnp.float32),
        lax.psum(shares[8].astype(jnp.bfloat16), "seq").astype(jnp.float32),
    )
    return (
        block_out,
        grad_input,
        summed[0],
        summed[1],
        summed[2],
        summed[3],
        summed[4],
        summed[5],
        summed[6],
        summed[7],
        summed[8],
    )


MESH = pl.DeviceIdType.MESH
WIDE = 256
LOW = jnp.bfloat16
F32 = jnp.float32
NEVER = -1e30

ORDER = (
    (2, 42),
    (12, 52),
    (),
    (),
    (22, 62),
    (3,),
    (),
    (),
    (32, 72),
    (13, 43, 53, 82, 63),
    (23,),
    (92, 112, 33, 73, 44),
    (54, 102),
    (83, 4),
    (64,),
    (93,),
    (
        14, 24, 34, 122, 45, 55, 113, 103, 74, 132, 84, 94, 133, 142, 65, 123, 143, 104, 114, 134,
        75, 85, 95, 124, 105, 144, 135, 145,
    ),
)


def dot(left, right):
    return lax.dot_general(left, right, (((1,), (0,)), ((), ())), preferred_element_type=F32)


def dot_nt(left, right):
    return lax.dot_general(left, right, (((1,), (1,)), ((), ())), preferred_element_type=F32)


def dot_tn(left, right):
    return lax.dot_general(left, right, (((0,), (0,)), ((), ())), preferred_element_type=F32)


def rope_constants(rows):
    quarter = HD // 4
    freq = 10000.0 ** (-np.arange(quarter) / quarter)
    tables = []
    for side, length in ((SIDE_S, SIDE_S * SIDE_S + 1), (SIDE_L, SIDE_L * SIDE_L + 1)):
        place = np.arange(rows) - 1
        place = np.where((place >= 0) & (place < length - 1), place, 0)
        row = (place // side)[:, None] * freq
        col = (place % side)[:, None] * freq
        cosine = np.concatenate([np.cos(row), np.cos(row), np.cos(col), np.cos(col)], -1)
        sine = np.concatenate([-np.sin(row), np.sin(row), -np.sin(col), np.sin(col)], -1)
        tables += [np.concatenate([cosine, cosine], -1), np.concatenate([sine, sine], -1)]
    return np.stack(tables).astype(np.float32)


def swap_quarters(values):
    lane = lax.broadcasted_iota(jnp.int32, values.shape, 1)
    first = (lane % (HD // 2)) < HD // 4
    return jnp.where(
        first, pltpu.roll(values, 2 * HD - HD // 4, 1), pltpu.roll(values, HD // 4, 1)
    )


def fused(geo, *refs):
    rows_here, width, hidden_all = geo
    (
        lens, gain_a, gain_f, x_hbm, cot_hbm, tab_hbm,
        wq, wk, wv, wo, wg, wu, wd,
        bo_hbm, gi_hbm, fa_hbm, fd_hbm, fq_hbm, gain_hbm,
        x4, cot4, tab, wqkv_v, wo_v, wg_v, wu_v, wd_v,
        nrm, nrm_t, qkv, chance, mix_own, mix_in, mix, mix_t,
        mid, nf, nf_t, hid, hid_t, gg, gu, big,
        gnf_out, gnf_in, sb, rb, bo, bo_in, gb, gmx, ds_s, gqkv, sb2, rb2, gi, gi_in,
        gain_s, gain_x, gain_y, gain_z, gain_c,
        pa, r1a, r2a, r3a, fa, pd, r1d, r2d, r3d, fd, pq, r1q, r2q, r3q, fq,
        sem_w, sem_in_s, sem_in_r, sem_core_s, sem_core_r, sem_gain_s, sem_gain_r, sem_o,
        sa_s, sa_r, sd_s, sd_r, sq_s, sq_r,
    ) = refs
    s = lax.axis_index("seq")
    i = lax.axis_index("items")
    y, c = s // 2, s % 2
    z, x = i // 2, i % 2
    rows = 4 * rows_here
    half = width // 2
    ff = hidden_all // 2
    pairs = half // 128
    step = rows_here
    fine = 32
    per = rows_here // step
    blocks = [(r0, min(256, rows - r0)) for r0 in range(0, rows, 256)]

    def device(y_to, c_to, z_to, x_to):
        return (y_to * 2 + c_to, z_to * 2 + x_to)

    sibling = device(y, 1 - c, z, x)
    y_dev = device(1 - y, c, z, x)
    x_dev = device(y, c, z, 1 - x)
    z_devs = [device(y, c, lax.rem(z + d, 4), x) for d in (1, 2, 3)]

    started = []

    def send(src, dst, s_sem, r_sem, to):
        return pltpu.make_async_remote_copy(
            src_ref=src, dst_ref=dst, send_sem=s_sem, recv_sem=r_sem,
            device_id=to, device_id_type=MESH,
        )

    def weight_copies():
        copies = [pltpu.make_async_copy(tab_hbm, tab, sem_w.at[0])]
        mine = pl.ds(pl.multiple_of(c * half, half), half)
        for t, w in enumerate((wq, wk, wv)):
            copies.append(
                pltpu.make_async_copy(
                    w.at[:, mine], wqkv_v.at[:, pl.ds(t * half, half)], sem_w.at[1 + t]
                )
            )
        copies.append(pltpu.make_async_copy(wo, wo_v, sem_w.at[4]))
        for b in range(ff // 128):
            far = pl.ds(pl.multiple_of(256 * b + 128 * c, 128), 128)
            near = pl.ds(128 * b, 128)
            copies.append(pltpu.make_async_copy(wg.at[:, far], wg_v.at[:, near], sem_w.at[5 + 3 * b]))
            copies.append(pltpu.make_async_copy(wu.at[:, far], wu_v.at[:, near], sem_w.at[6 + 3 * b]))
            copies.append(pltpu.make_async_copy(wd.at[far], wd_v.at[near], sem_w.at[7 + 3 * b]))
        return copies

    weights = weight_copies()
    own_x = pltpu.make_async_copy(x_hbm.at[y], x4.at[s], sem_o.at[0])
    own_cot = pltpu.make_async_copy(cot_hbm.at[y], cot4.at[s], sem_o.at[1])
    own_x.start()
    for copy in weights[:4]:
        copy.start()

    barrier = pltpu.get_barrier_semaphore()
    for to in [sibling, y_dev, x_dev] + z_devs:
        pl.semaphore_signal(barrier, inc=1, device_id=to, device_id_type=MESH)
    pl.semaphore_wait(barrier, 6)

    s_y = (1 - y) * 2 + c
    across_x = send(x_hbm.at[1 - y], x4.at[s], sem_in_s.at[0], sem_in_r.at[0], y_dev)
    beside_x = send(x_hbm.at[y], x4.at[s], sem_in_s.at[1], sem_in_r.at[1], sibling)
    across_x.start()
    beside_x.start()
    across_c = send(cot_hbm.at[1 - y], cot4.at[s], sem_in_s.at[2], sem_in_r.at[2], y_dev)
    beside_c = send(cot_hbm.at[y], cot4.at[s], sem_in_s.at[3], sem_in_r.at[3], sibling)
    own_cot.start()
    for copy in weights[4:]:
        copy.start()
    relay_x = send(x4.at[s_y], x4.at[s_y], sem_in_s.at[4], sem_in_r.at[4], sibling)
    relay_c = send(cot4.at[s_y], cot4.at[s_y], sem_in_s.at[5], sem_in_r.at[5], sibling)

    length = lens[y]

    def norm_rows(piece):
        def one(b, carry):
            here = pl.ds(pl.multiple_of(b * step, step), step)
            values = x4[piece, here, :].astype(F32)
            scale = lax.rsqrt(jnp.mean(values * values, -1, keepdims=True) + epsilon)
            there = pl.ds(pl.multiple_of(piece * rows_here + b * step, step), step)
            nrm[there, :] = (values * scale * gain_a[...]).astype(LOW)
            return carry

        lax.fori_loop(0, per, one, 0)

    def project_rows(part):
        base = pl.multiple_of(part * 2 * rows_here, 32)
        here = pl.ds(base, 2 * rows_here)
        cosine = jnp.where(length == LONG, tab[2, here, :], tab[0, here, :])
        sine = jnp.where(length == LONG, tab[3, here, :], tab[1, here, :])
        for t in range(3):
            product = dot(nrm[here, :], wqkv_v[:, t * half : (t + 1) * half])
            for p in range(pairs):
                lanes = product[:, 128 * p : 128 * (p + 1)]
                if t < 2:
                    lanes = lanes * cosine + swap_quarters(lanes) * sine
                if t == 0:
                    lanes = lanes.astype(LOW).astype(F32) * HD ** (-0.5)
                qkv[t, here, 128 * p : 128 * (p + 1)] = lanes.astype(LOW)

    own_x.wait()
    norm_rows(s)
    beside_x.wait_recv()
    norm_rows(2 * y + 1 - c)
    for copy in weights[:4]:
        copy.wait()
    project_rows(y)
    across_x.wait_recv()
    relay_x.start()
    across_c.start()
    beside_c.start()
    norm_rows(s_y)
    relay_x.wait_recv()
    norm_rows(2 * (1 - y) + 1 - c)
    project_rows(1 - y)

    lane = lax.broadcasted_iota(jnp.int32, (1, 128), 1)
    left_head = lane < HD
    masks = [(lane // HD == n).astype(F32).astype(LOW) for n in range(2)]

    def mix_copy(pair):
        return send(
            mix_own.at[pair], mix_in.at[pair], sem_core_s.at[pair], sem_core_r.at[pair], sibling
        )

    def attend(pair, carry):
        lanes = pl.ds(pl.multiple_of(pair * 128, 128), 128)
        for r0, rb in blocks:
            nk = r0 + rb
            row = r0 + lax.broadcasted_iota(jnp.int32, (rb, nk), 0)
            col = lax.broadcasted_iota(jnp.int32, (rb, nk), 1)
            allowed = (col <= row) & (col < length)
            both = []
            for n in range(2):
                query = qkv[0, r0:nk, lanes] * masks[n]
                scores = jnp.where(allowed, dot_nt(query, qkv[1, :nk, lanes]), NEVER)
                expo = jnp.exp(scores - jnp.max(scores, -1, keepdims=True))
                low = (expo * (1.0 / jnp.sum(expo, -1, keepdims=True))).astype(LOW)
                chance[pair * 2 + n, r0:nk, :nk] = low
                both.append(dot(low, qkv[2, :nk, lanes]))
            mix_own[pair, r0:nk, :] = jnp.where(left_head, both[0], both[1]).astype(LOW)
        mix_copy(pair).start()
        return carry

    lax.fori_loop(0, pairs, attend, 0)

    across_c.wait_recv()
    relay_c.start()

    def turn_rows(src, dst):
        def one(b, carry):
            here = pl.ds(pl.multiple_of(b * 128, 128), 128)
            dst[:, here] = src[here, :].T
            return carry

        lax.fori_loop(0, rows // 128, one, 0)

    def place_mix(src, at):
        def one(p, carry):
            mix[:, pl.ds(pl.multiple_of(at * half + p * 128, 128), 128)] = src[p]
            return carry

        lax.fori_loop(0, pairs, one, 0)

    place_mix(mix_own, c)
    turn_rows(nrm, nrm_t)
    for p in range(pairs):
        mix_copy(p).wait_recv()
    place_mix(mix_in, 1 - c)

    weights[4].wait()

    def chunk(n, wide=WIDE):
        return pl.ds(pl.multiple_of(n * wide, wide), wide)

    def out_project(n, carry):
        mid[:, chunk(n)] = (
            dot(mix[...], wo_v[:, chunk(n)])
            + x4[:, :, chunk(n)].reshape(rows, WIDE).astype(F32)
        )
        return carry

    lax.fori_loop(0, width // WIDE, out_project, 0)

    def second_norm(b, carry):
        here = pl.ds(pl.multiple_of(b * step, step), step)
        values = mid[here, :]
        scale = lax.rsqrt(jnp.mean(values * values, -1, keepdims=True) + epsilon)
        nf[here, :] = (values * scale * gain_f[...]).astype(LOW)
        return carry

    lax.fori_loop(0, rows // step, second_norm, 0)
    turn_rows(nf, nf_t)
    for copy in weights[5:]:
        copy.wait()
    own_cot.wait()
    beside_c.wait_recv()
    relay_c.wait_recv()

    class Group:
        def __init__(self, parts, r1, r2, r3, fin, s_sem, r_sem):
            self.parts, self.r1, self.r2, self.r3, self.fin = parts, r1, r2, r3, fin
            self.s_sem, self.r_sem = s_sem, r_sem

        def copy(self, k, n, src, dst, to):
            return send(src, dst, self.s_sem.at[k, n], self.r_sem.at[k, n], to)

        def add(self, k, to, own):
            self.r1[to] = (self.r1[to].astype(F32) + self.parts[own].astype(F32)).astype(LOW)

    class ByX(Group):
        def first(self, k):
            return self.copy(k, 0, self.parts.at[k, :, 1 - x], self.r1.at[k], x_dev)

        def along_z(self, k, d):
            return self.copy(
                k, d, self.r1.at[k, lax.rem(z + d, 4)], self.r2.at[k, pl.ds(2 * d - 2, 2)], z_devs[d - 1]
            )

        def over_y(self, k):
            return self.copy(k, 4, self.r1.at[k, z], self.r3.at[k, pl.ds(0, 2)], y_dev)

        def to_core(self, k):
            return self.copy(k, 5, self.fin.at[k, c], self.fin.at[k, c], sibling)

        def step1(self, k):
            self.first(k).start()

        def step2(self, k):
            self.first(k).wait_recv()
            for d in (1, 2, 3, 0):
                to = lax.rem(z + d, 4)
                for h in range(2):
                    self.add(k, (k, to, h), (k, to, x, h))
                if d:
                    self.along_z(k, d).start()

        def step3(self, k):
            for d in (1, 2, 3):
                self.along_z(k, d).wait_recv()
            for h in range(2):
                total = self.r1[k, z, h].astype(F32)
                for d in (1, 2, 3):
                    total = total + self.r2[k, 2 * d - 2 + h].astype(F32)
                self.r1[k, z, h] = total.astype(LOW)
            self.over_y(k).start()

        def step4(self, k):
            self.over_y(k).wait_recv()
            for h in range(2):
                total = self.r1[k, z, h].astype(F32) + self.r3[k, h].astype(F32)
                self.fin[k, c, h] = total.astype(LOW)
            self.to_core(k).start()

        def end(self, k):
            self.to_core(k).wait_recv()

        def sent(self, k):
            self.first(k).wait_send()
            for d in (1, 2, 3):
                self.along_z(k, d).wait_send()
            self.over_y(k).wait_send()
            self.to_core(k).wait_send()

    class ByY(Group):
        def first(self, k):
            return self.copy(k, 0, self.parts.at[k, :, :, 1 - y], self.r1.at[k], y_dev)

        def second(self, k):
            return self.copy(k, 1, self.r1.at[k, :, 1 - x], self.r2.at[k, pl.ds(0, 4)], x_dev)

        def along_z(self, k, d):
            return self.copy(
                k, 1 + d, self.r2.at[k, lax.rem(z + d, 4)], self.r3.at[k, d - 1], z_devs[d - 1]
            )

        def copies_out(self, k, n):
            at = self.fin.at[k, c, y] if n < 2 else self.fin.at[k, c, 1 - y]
            return self.copy(k, 5 + n, at, at, y_dev if n == 0 else sibling)

        def step1(self, k):
            self.first(k).start()

        def step2(self, k):
            self.first(k).wait_recv()
            for zz in range(4):
                self.add(k, (k, zz, 1 - x), (k, zz, 1 - x, y))
            self.second(k).start()
            for zz in range(4):
                self.add(k, (k, zz, x), (k, zz, x, y))

        def step3(self, k):
            self.second(k).wait_recv()
            for d in (1, 2, 3, 0):
                to = lax.rem(z + d, 4)
                self.r2[k, to] = (
                    self.r2[k, to].astype(F32) + self.r1[k, to, x].astype(F32)
                ).astype(LOW)
                if d:
                    self.along_z(k, d).start()

        def step4(self, k):
            total = self.r2[k, z].astype(F32)
            for d in (1, 2, 3):
                self.along_z(k, d).wait_recv()
                total = total + self.r3[k, d - 1].astype(F32)
            self.fin[k, c, y] = total.astype(LOW)
            self.copies_out(k, 0).start()
            self.copies_out(k, 1).start()

        def step5(self, k):
            self.copies_out(k, 0).wait_recv()
            self.copies_out(k, 2).start()

        def end(self, k):
            self.copies_out(k, 1).wait_recv()
            self.copies_out(k, 2).wait_recv()

        def sent(self, k):
            self.first(k).wait_send()
            self.second(k).wait_send()
            for d in (1, 2, 3):
                self.along_z(k, d).wait_send()
            for n in range(3):
                self.copies_out(k, n).wait_send()

    buffers_a = (pa, r1a, r2a, r3a, fa, sa_s, sa_r)
    buffers_d = (pd, r1d, r2d, r3d, fd, sd_s, sd_r)
    buffers_q = (pq, r1q, r2q, r3q, fq, sq_s, sq_r)
    chunks = [(ByX(*buffers_a), n) for n in range(4)] + [(ByY(*buffers_a), n + 4) for n in range(4)]
    chunks += [(plan(*buffers_d), n) for n, plan in enumerate((ByY, ByY, ByY))]
    chunks += [(plan(*buffers_q), n) for n, plan in enumerate((ByX, ByX, ByY, ByY))]
    slots = iter(ORDER)

    def first(chunk):
        group, k = chunks[chunk]
        group.step1(k)

    def turn():
        for code in next(slots):
            group, k = chunks[code // 10]
            getattr(group, f"step{code % 10}")(k)

    chunks_f = ff // WIDE
    chunks_w = width // WIDE

    def feed(n, carry):
        at = chunk(n)
        big[:, 0:WIDE] = dot(nf[...], wg_v[:, at])
        big[:, WIDE : 2 * WIDE] = dot(nf[...], wu_v[:, at])
        big[:, 2 * WIDE : 3 * WIDE] = dot_nt(cot4[...].reshape(rows, width), wd_v[at, :])

        def one(b, inner):
            here = pl.ds(pl.multiple_of(b * fine, fine), fine)
            gate = big[here, 0:WIDE]
            up = big[here, WIDE : 2 * WIDE]
            back = big[here, 2 * WIDE : 3 * WIDE]
            sigma = 0.5 * jnp.tanh(0.5 * gate) + 0.5
            silu = gate * sigma
            hid[here, at] = (silu * up).astype(LOW)
            gg[here, at] = (back * up * (sigma + silu * (1.0 - sigma))).astype(LOW)
            gu[here, at] = (back * silu).astype(LOW)
            return inner

        lax.fori_loop(0, rows // fine, one, 0, unroll=5)
        shape = pa.shape[1:]
        pa[n] = dot(nf_t[...], gg[:, at]).reshape(shape).astype(LOW)
        chunks[0][0].step1(n)
        pa[n + chunks_f] = dot(nf_t[...], gu[:, at]).reshape(shape).astype(LOW)
        chunks[4][0].step1(n + chunks_f)
        hid_t[at, :] = hid[:, at].T
        return carry

    lax.fori_loop(0, chunks_f, feed, 0)
    turn()

    def gnf_copy(n):
        return send(
            gnf_out.at[n], gnf_in.at[n], sem_core_s.at[pairs + n], sem_core_r.at[pairs + n], sibling
        )

    def back_ffn(n, carry):
        partial = dot_nt(gg[...], wg_v[chunk(n), :]) + dot_nt(gu[...], wu_v[chunk(n), :])
        big[:, chunk(n)] = partial
        gnf_out[n] = partial.astype(LOW)
        gnf_copy(n).start()
        return carry

    lax.fori_loop(0, chunks_w, back_ffn, 0)
    turn()

    def down(n, carry):
        big[:, chunk(n + chunks_w)] = dot(hid[...], wd_v[:, chunk(n)])
        return carry

    lax.fori_loop(0, chunks_w, down, 0)
    n_core = pairs + chunks_w
    bo_copy = send(sb, rb, sem_core_s.at[n_core], sem_core_r.at[n_core], sibling)
    far = slice(width, 2 * width)

    def for_rows(core, fn):
        for yy in range(2):
            def one(b, carry, yy=yy):
                base = pl.multiple_of((2 * yy + core) * rows_here + b * step, step)
                fn(yy, b, pl.ds(base, step), pl.ds(pl.multiple_of(b * step, step), step))
                return carry

            lax.fori_loop(0, per, one, 0)

    def pack_bo(yy, b, here, there):
        sb[yy, there, :] = big[here, far].astype(LOW)

    for_rows(1 - c, pack_bo)
    bo_copy.start()

    for n in range(chunks_w):
        turn()
        at = slice(n * WIDE, (n + 1) * WIDE)
        pd[n] = (
            dot(hid_t[...], cot4[:, :, at].reshape(rows, WIDE)).reshape(pd.shape[1:]).astype(LOW)
        )
        first(8 + n)

    turn()
    bo_copy.wait_recv()

    def finish_bo(yy, b, here, there):
        bo[yy, there, :] = (mid[here, :] + big[here, far] + rb[yy, there, :].astype(F32)).astype(LOW)

    for_rows(c, finish_bo)
    bo_across = send(bo.at[1 - y], bo_in, sem_in_s.at[6], sem_in_r.at[6], y_dev)
    bo_across.start()

    turn()
    for n in range(chunks_w):
        gnf_copy(n).wait_recv()

    def middle_back(b, total):
        here = pl.ds(pl.multiple_of(b * step, step), step)
        values = mid[here, :]
        grad = big[here, 0:width] + jnp.concatenate(
            [gnf_in[n, here, :].astype(F32) for n in range(chunks_w)], -1
        )
        scale = lax.rsqrt(jnp.mean(values * values, -1, keepdims=True) + epsilon)
        unit = values * scale
        total = total + (grad * unit).reshape(step // 8, 8, width).sum(0)
        scaled = grad * gain_f[...]
        inner = jnp.mean(scaled * unit, -1, keepdims=True)
        out = cot4[b // per, pl.ds(pl.multiple_of(lax.rem(b, per) * step, step), step), :].astype(F32)
        out = out + scale * (scaled - unit * inner)
        mid[here, :] = out
        gb[here, :] = out.astype(LOW)
        return total

    total_f = lax.fori_loop(0, rows // step, middle_back, jnp.zeros((8, width), F32))

    turn()
    turn_rows(mix, mix_t)
    mine = pl.ds(pl.multiple_of(c * half, half), half)
    pq[0] = dot(mix_t[...], gb[:, mine]).reshape(pq.shape[1:]).astype(LOW)
    first(11)
    gmx[...] = dot_nt(gb[...], wo_v[mine, :]).astype(LOW)

    def attend_back(pair, carry):
        lanes = slice(pair * 128, pair * 128 + 128)

        def keep(n, at, off, value):
            where_ = slice(off * 128, off * 128 + 128)
            if n:
                value = jnp.where(left_head, big[at, where_], value)
            big[at, where_] = value

        for n in range(2):
            head = pair * 2 + n
            for r0, rb_ in blocks:
                nk = r0 + rb_
                grad = gmx[r0:nk, lanes] * masks[n]
                prob = chance[head, r0:nk, :nk].astype(F32)
                each = dot_nt(grad, qkv[2, :nk, lanes]) * prob
                low = (each - prob * jnp.sum(each, -1, keepdims=True)).astype(LOW)
                ds_s[r0:nk, :nk] = low
                keep(n, slice(r0, nk), 0, dot(low, qkv[1, :nk, lanes]))
            for k0, kb in blocks:
                at = slice(k0, k0 + kb)
                keep(n, at, 1, dot_tn(ds_s[k0:, at], qkv[0, k0:, lanes]))
                keep(n, at, 2, dot_tn(chance[head, k0:, at], gmx[k0:, lanes]))

        def one(b, inner):
            here = pl.ds(pl.multiple_of(b * 64, 64), 64)
            cosine = jnp.where(length == LONG, tab[2, here, :], tab[0, here, :])
            sine = jnp.where(length == LONG, tab[3, here, :], tab[1, here, :])
            for t in range(3):
                values = big[here, 128 * t : 128 * (t + 1)]
                if t == 0:
                    values = values * HD ** (-0.5)
                if t < 2:
                    values = values * cosine - swap_quarters(values) * sine
                gqkv[here, t * half + pair * 128 : t * half + pair * 128 + 128] = values.astype(LOW)
            return inner

        lax.fori_loop(0, rows // 64, one, 0)
        return carry

    for pair in range(pairs):
        turn()
        attend_back(pair, 0)

    for t in range(3):
        turn()
        pq[1 + t] = (
            dot(nrm_t[...], gqkv[:, t * half : (t + 1) * half]).reshape(pq.shape[1:]).astype(LOW)
        )
        first(12 + t)

    turn()

    def back_attn(n, carry):
        big[:, chunk(n)] = dot_nt(gqkv[...], wqkv_v[chunk(n), :])
        return carry

    lax.fori_loop(0, chunks_w, back_attn, 0)
    turn()

    def pack_gi(yy, b, here, there):
        sb2[yy, there, :] = big[here, 0:width].astype(LOW)

    for_rows(1 - c, pack_gi)
    gi_copy = send(sb2, rb2, sem_core_s.at[n_core + 1], sem_core_r.at[n_core + 1], sibling)
    gi_copy.start()

    def gain_back(b, total):
        here = pl.ds(pl.multiple_of(b * step, step), step)
        values = x4[b // per, pl.ds(pl.multiple_of(lax.rem(b, per) * step, step), step), :].astype(F32)
        scale = lax.rsqrt(jnp.mean(values * values, -1, keepdims=True) + epsilon)
        return total + (big[here, 0:width] * (values * scale)).reshape(step // 8, 8, width).sum(0)

    total_a = lax.fori_loop(0, rows // step, gain_back, jnp.zeros((8, width), F32))
    gain_s[...] = jnp.concatenate(
        [
            jnp.broadcast_to(jnp.sum(total_a, 0, keepdims=True), (8, width)),
            jnp.broadcast_to(jnp.sum(total_f, 0, keepdims=True), (8, width)),
        ],
        0,
    )
    gain_1 = send(gain_s, gain_x, sem_gain_s.at[0], sem_gain_r.at[0], x_dev)
    gain_2 = send(gain_x, gain_y, sem_gain_s.at[1], sem_gain_r.at[1], y_dev)
    gain_3 = [
        send(gain_y, gain_z.at[d], sem_gain_s.at[2 + d], sem_gain_r.at[2 + d], z_devs[d])
        for d in range(3)
    ]
    gain_4 = send(gain_s, gain_c, sem_gain_s.at[5], sem_gain_r.at[5], sibling)
    gain_1.start()

    def gains_2():
        gain_1.wait()
        gain_x[...] = gain_s[...] + gain_x[...]
        gain_2.start()

    def gains_3():
        gain_2.wait()
        gain_y[...] = gain_x[...] + gain_y[...]
        for copy in gain_3:
            copy.start()

    def gains_4():
        for copy in gain_3:
            copy.wait()
        gain_s[...] = gain_y[...] + gain_z[0] + gain_z[1] + gain_z[2]
        gain_4.start()

    def gains_5():
        gain_4.wait()
        gain_c[0:8, :] = gain_s[0:8, :] + gain_c[0:8, :]
        gain_c[...] = pltpu.roll(gain_c[...], lax.rem(8 - i, 8) * (width // 8), 1)

    gi_copy.wait_recv()

    def finish_gi(yy, b, here, there):
        values = x4[2 * yy + c, there, :].astype(F32)
        scale = lax.rsqrt(jnp.mean(values * values, -1, keepdims=True) + epsilon)
        unit = values * scale
        scaled = (big[here, 0:width] + rb2[yy, there, :].astype(F32)) * gain_a[...]
        inner = jnp.mean(scaled * unit, -1, keepdims=True)
        gi[yy, there, :] = (mid[here, :] + scale * (scaled - unit * inner)).astype(LOW)

    for_rows(c, finish_gi)
    gi_across = send(gi.at[1 - y], gi_in, sem_in_s.at[7], sem_in_r.at[7], y_dev)
    gi_across.start()

    tail = next(slots)
    gains_at = dict(zip((4, 10, 16, 22), (gains_2, gains_3, gains_4, gains_5)))
    for n, code in enumerate(tail):
        if n in gains_at:
            gains_at[n]()
        group, k = chunks[code // 10]
        getattr(group, f"step{code % 10}")(k)
    for group, k in chunks:
        group.end(k)

    outs = [
        pltpu.make_async_copy(fa, fa_hbm, sem_o.at[2]),
        pltpu.make_async_copy(fd, fd_hbm, sem_o.at[3]),
        pltpu.make_async_copy(fq, fq_hbm, sem_o.at[4]),
        pltpu.make_async_copy(gain_c, gain_hbm, sem_o.at[5]),
        pltpu.make_async_copy(bo.at[y], bo_hbm.at[y], sem_o.at[6]),
        pltpu.make_async_copy(gi.at[y], gi_hbm.at[y], sem_o.at[7]),
    ]
    for copy in outs:
        copy.start()
    bo_across.wait_recv()
    gi_across.wait_recv()
    outs += [
        pltpu.make_async_copy(bo_in, bo_hbm.at[1 - y], sem_o.at[8]),
        pltpu.make_async_copy(gi_in, gi_hbm.at[1 - y], sem_o.at[9]),
    ]
    for copy in outs[6:]:
        copy.start()
    for copy in outs:
        copy.wait()

    for copy in (across_x, beside_x, across_c, beside_c, relay_x, relay_c, bo_across, gi_across):
        copy.wait_send()
    for p in range(pairs):
        mix_copy(p).wait_send()
    for n in range(chunks_w):
        gnf_copy(n).wait_send()
    bo_copy.wait_send()
    gi_copy.wait_send()
    for group, k in chunks:
        group.sent(k)


def spread(chunks_f, share, *refs):
    far, refs = refs[:6], refs[6:]
    outs, near, sem = refs[:11], refs[11:17], refs[17]
    bo_out, gi_out, da, dq, dk, dv, do, df, dg, du, dd = outs
    copies = [pltpu.make_async_copy(a, b, sem.at[n]) for n, (a, b) in enumerate(zip(far, near))]
    for copy in copies:
        copy.start()
    fa, fd, fq, bo, gi, gains = near
    for copy in copies:
        copy.wait()
    bo_out[...] = bo[...]
    gi_out[...] = gi[...]
    da[...] = gains[0, 0:share]
    df[...] = gains[8, 0:share]
    rows = fa.shape[3]
    for core in range(2):
        for h in range(2):
            at = slice(h * rows, (h + 1) * rows)
            for n in range(chunks_f):
                for b in range(WIDE // 128):
                    far = 256 * (n * (WIDE // 128) + b) + 128 * core
                    near = slice(128 * b, 128 * (b + 1))
                    dg[at, far : far + 128] = fa[n, core, h, :, near].astype(F32)
                    du[at, far : far + 128] = fa[n + chunks_f, core, h, :, near].astype(F32)
            half = fq.shape[4]
            lanes = slice(core * half, (core + 1) * half)
            for n, ref in enumerate((do, dq, dk, dv)):
                ref[at, lanes] = fq[n, core, h].astype(F32)
            deep = fd.shape[3]
            at = slice((2 * core + h) * deep, (2 * core + h + 1) * deep)
            for n in range(fd.shape[0]):
                dd[at, WIDE * n : WIDE * (n + 1)] = fd[n, core, h].astype(F32)


def item_per_chip(
    block_in, lengths, gain_attn, w_query, w_key, w_value, w_out, gain_ffn, w_gate, w_up, w_down,
    cotangent,
):
    _, rows_here, width = block_in.shape
    hidden_all = w_gate.shape[1]
    rows = rows_here * lax.axis_size("seq")
    shares = lax.axis_size("items")
    half, ff = width // 2, hidden_all // 2
    pairs = half // 128
    chunks_f, chunks_w = ff // WIDE, width // WIDE
    thin, deep = width // shares // 2, ff // shares // 2
    tables = jnp.asarray(rope_constants(rows))
    any_ = pl.BlockSpec(memory_space=pl.ANY)
    vmem = pl.BlockSpec(memory_space=pltpu.VMEM)

    def group(n, r, w):
        return [
            pltpu.VMEM((n, 4, 2, 2, r, w), LOW),
            pltpu.VMEM((n, 4, 2, r, w), LOW),
            pltpu.VMEM((n, 6, r, w), LOW),
            pltpu.VMEM((n, 3, r, w), LOW),
            pltpu.VMEM((n, 2, 2, r, w), LOW),
        ]

    def low(*shape):
        return pltpu.VMEM(shape, LOW)

    def full(*shape):
        return pltpu.VMEM(shape, F32)

    dma = pltpu.SemaphoreType.DMA
    scratch = [
        low(4, rows_here, width), low(4, rows_here, width), full(4, rows, 128),
        low(width, 3 * half), low(width, width), low(width, ff), low(width, ff), low(ff, width),
        low(rows, width), low(width, rows), low(3, rows, half), low(2 * pairs, rows, rows),
        low(pairs, rows, 128), low(pairs, rows, 128), low(rows, width), low(width, rows),
        full(rows, width), low(rows, width), low(width, rows), low(rows, ff), low(ff, rows),
        low(rows, ff), low(rows, ff), full(rows, 2 * width),
        low(chunks_w, rows, WIDE), low(chunks_w, rows, WIDE),
        low(2, rows_here, width), low(2, rows_here, width),
        low(2, rows_here, width), low(rows_here, width),
        low(rows, width), low(rows, half), low(rows, rows), low(rows, 3 * half),
        low(2, rows_here, width), low(2, rows_here, width),
        low(2, rows_here, width), low(rows_here, width),
        full(16, width), full(16, width), full(16, width), full(3, 16, width), full(16, width),
    ]
    scratch += group(2 * chunks_f, thin, WIDE) + group(chunks_w, deep, WIDE) + group(4, thin, half)
    scratch += [
        dma((5 + 3 * (ff // 128),)), dma((8,)), dma((8,)),
        dma((pairs + chunks_w + 2,)), dma((pairs + chunks_w + 2,)), dma((6,)), dma((6,)), dma((10,)),
        dma((2 * chunks_f, 8)), dma((2 * chunks_f, 8)), dma((chunks_w, 8)), dma((chunks_w, 8)),
        dma((4, 8)), dma((4, 8)),
    ]
    shape = jax.ShapeDtypeStruct
    bo, gi, fa, fd, fq, gains = pl.pallas_call(
        functools.partial(fused, (rows_here, width, hidden_all)),
        out_shape=(
            shape(block_in.shape, LOW), shape(block_in.shape, LOW),
            shape((2 * chunks_f, 2, 2, thin, WIDE), LOW), shape((chunks_w, 2, 2, deep, WIDE), LOW),
            shape((4, 2, 2, thin, half), LOW), shape((16, width), F32),
        ),
        in_specs=[pl.BlockSpec(memory_space=pltpu.SMEM), vmem, vmem] + [any_] * 10,
        out_specs=(any_,) * 6,
        scratch_shapes=scratch,
        compiler_params=pltpu.CompilerParams(
            collective_id=0, has_side_effects=True, vmem_limit_bytes=63 * 2**20
        ),
        name="block",
    )(
        lengths, gain_attn, gain_ffn, block_in, cotangent, tables,
        w_query, w_key, w_value, w_out, w_gate, w_up, w_down,
    )
    thick = (width // shares, width)
    made = (fa, fd, fq, bo, gi, gains)
    share = width // shares
    bo, gi, da, dq, dk, dv, do, df, dg, du, dd = pl.pallas_call(
        functools.partial(spread, chunks_f, share),
        out_shape=(
            shape(block_in.shape, LOW), shape(block_in.shape, LOW), shape((share,), F32),
            shape(thick, F32), shape(thick, F32), shape(thick, F32), shape(thick, F32),
            shape((share,), F32),
            shape((width // shares, hidden_all), F32), shape((width // shares, hidden_all), F32),
            shape((hidden_all // shares, width), F32),
        ),
        in_specs=[any_] * 6,
        out_specs=(vmem,) * 11,
        scratch_shapes=[pltpu.VMEM(a.shape, a.dtype) for a in made] + [dma((6,))],
        compiler_params=pltpu.CompilerParams(vmem_limit_bytes=60 * 2**20),
        name="spread",
    )(*made)
    return bo, gi, da, dq, dk, dv, do, df, dg, du, dd


def solution(mesh):
    fits = mesh.shape["seq"] == 4 and mesh.shape["items"] == 8
    return jax.shard_map(
        item_per_chip if fits else body,
        mesh=mesh,
        in_specs=(P("items", "seq", None), P("items")) + (P(),) * 9 + (P("items", "seq", None),),
        out_specs=(
            (P("items", "seq", None),) * 2
            + (P("items"),) + (P("items", None),) * 4
            + (P("items"),) + (P("items", None),) * 3
        ),
        check_vma=False,
    )
```

```python
import functools

import jax
import jax.numpy as jnp
import numpy as np
from jax import lax
from jax.experimental import pallas as pl
from jax.experimental.pallas import tpu as pltpu
from jax.sharding import PartitionSpec as P

HD = 64
SIDE_S = 16
SIDE_L = 24
LONG = 577


epsilon = 1e-05


def grid_places(lengths, rows):
    side = jnp.where(lengths == LONG, SIDE_L, SIDE_S).astype(jnp.int32)[:, None]
    place = rows[None, :] - 1
    valid = (place >= 0) & (rows[None, :] < lengths[:, None])
    place = jnp.where(valid, place, 0)
    return (place // side, place % side)


def rotary_tables(lengths, rows):
    grid_row, grid_col = grid_places(lengths, rows)
    quarter = HD // 4
    freq = 10000.0 ** (-jnp.arange(quarter, dtype=jnp.float32) / quarter)
    angle_row = grid_row[..., None].astype(jnp.float32) * freq
    angle_col = grid_col[..., None].astype(jnp.float32) * freq
    cosine = jnp.concatenate(
        [jnp.cos(angle_row), jnp.cos(angle_row), jnp.cos(angle_col), jnp.cos(angle_col)], -1
    )
    sine = jnp.concatenate(
        [jnp.sin(angle_row), jnp.sin(angle_row), jnp.sin(angle_col), jnp.sin(angle_col)], -1
    )
    return (cosine[:, :, None, :], sine[:, :, None, :])


def turn(values):
    quarter = HD // 4
    first = values[..., 0:quarter]
    second = values[..., quarter : 2 * quarter]
    third = values[..., 2 * quarter : 3 * quarter]
    fourth = values[..., 3 * quarter :]
    return jnp.concatenate([-second, first, -fourth, third], -1)


def project(left, right):
    return jnp.einsum("ird,de->ire", left, right, preferred_element_type=jnp.float32)


def back_project(grad, weight):
    return jnp.einsum("ire,de->ird", grad, weight, preferred_element_type=jnp.float32)


def weight_grad(left, right):
    return jnp.einsum("ird,ire->de", left, right, preferred_element_type=jnp.float32)


def norm_back(grad_normed, unit, scale, gain):
    scaled = grad_normed * gain
    return scale * (scaled - unit * jnp.mean(scaled * unit, -1, keepdims=True))


def body(
    block_in,
    lengths,
    gain_attn,
    w_query,
    w_key,
    w_value,
    w_out,
    gain_ffn,
    w_gate,
    w_up,
    w_down,
    cotangent,
):
    count, rows_here, width = block_in.shape
    heads = width // HD
    length_all = rows_here * lax.axis_size("seq")
    factor = HD ** (-0.5)
    query_rows = lax.axis_index("seq") * rows_here + jnp.arange(rows_here, dtype=jnp.int32)
    key_rows = jnp.arange(length_all, dtype=jnp.int32)
    cosine, sine = rotary_tables(lengths, query_rows)
    allowed = (key_rows[None, None, :] <= query_rows[None, :, None]) & (
        key_rows[None, None, :] < lengths[:, None, None]
    )

    def heads_of(array):
        return array.reshape(array.shape[0], array.shape[1], heads, HD)

    def attention_scores(query, keys_all):
        raw = (
            jnp.einsum(
                "irhe,iphe->ihrp", query, heads_of(keys_all), preferred_element_type=jnp.float32
            )
            * factor
        )
        return jnp.where(allowed[:, None], raw, -1e30)

    source = block_in.astype(jnp.float32)
    scale_attn = lax.rsqrt(jnp.mean(source * source, -1, keepdims=True) + epsilon)
    unit_attn = source * scale_attn
    normed = (unit_attn * gain_attn).astype(jnp.bfloat16)
    query_pre = heads_of(project(normed, w_query))
    keys_pre = heads_of(project(normed, w_key))
    query = (query_pre * cosine + turn(query_pre) * sine).astype(jnp.bfloat16)
    keys = (
        (keys_pre * cosine + turn(keys_pre) * sine)
        .astype(jnp.bfloat16)
        .reshape(count, rows_here, width)
    )
    values = project(normed, w_value).astype(jnp.bfloat16)
    keys_all, values_all = (
        lax.all_gather(keys, "seq", axis=1, tiled=True),
        lax.all_gather(values, "seq", axis=1, tiled=True),
    )
    scores = attention_scores(query, keys_all)
    top = jnp.max(scores, -1, keepdims=True)
    expo = jnp.exp(scores - top)
    summed = jnp.sum(expo, -1, keepdims=True)
    chance = expo / summed
    log_total = top + jnp.log(summed)
    mixed = (
        jnp.einsum(
            "ihrp,iphe->irhe",
            chance.astype(jnp.bfloat16),
            heads_of(values_all),
            preferred_element_type=jnp.float32,
        )
        .reshape(count, rows_here, width)
        .astype(jnp.bfloat16)
    )
    middle = source + project(mixed, w_out)
    scale_ffn = lax.rsqrt(jnp.mean(middle * middle, -1, keepdims=True) + epsilon)
    unit_ffn = middle * scale_ffn
    normed_ffn = (unit_ffn * gain_ffn).astype(jnp.bfloat16)
    gate = project(normed_ffn, w_gate)
    up = project(normed_ffn, w_up)
    sigma = jax.nn.sigmoid(gate)
    hidden = (gate * sigma * up).astype(jnp.bfloat16)
    block_out = (middle + project(hidden, w_down)).astype(jnp.bfloat16)
    incoming = cotangent.astype(jnp.float32)
    grad_w_down = weight_grad(hidden, cotangent)
    grad_hidden = back_project(cotangent, w_down)
    grad_gate = (grad_hidden * up * sigma * (1.0 + gate * (1.0 - sigma))).astype(jnp.bfloat16)
    grad_up = (grad_hidden * gate * sigma).astype(jnp.bfloat16)
    grad_w_gate = weight_grad(normed_ffn, grad_gate)
    grad_w_up = weight_grad(normed_ffn, grad_up)
    grad_normed_ffn = back_project(grad_gate, w_gate) + back_project(grad_up, w_up)
    grad_gain_ffn = jnp.sum(grad_normed_ffn * unit_ffn, axis=(0, 1))
    grad_middle = incoming + norm_back(grad_normed_ffn, unit_ffn, scale_ffn, gain_ffn)
    grad_branch = grad_middle.astype(jnp.bfloat16)
    grad_w_out = weight_grad(mixed, grad_branch)
    grad_mixed = heads_of(back_project(grad_branch, w_out)).astype(jnp.bfloat16)
    keys_back, values_back = (keys_all, values_all)
    chance_back = jnp.exp(attention_scores(query, keys_back) - log_total)
    grad_chance = jnp.einsum(
        "irhe,iphe->ihrp", grad_mixed, heads_of(values_back), preferred_element_type=jnp.float32
    )
    inner = jnp.sum(grad_chance * chance_back, -1, keepdims=True)
    grad_scores = (chance_back * (grad_chance - inner)).astype(jnp.bfloat16)
    grad_query = (
        jnp.einsum(
            "ihrp,iphe->irhe", grad_scores, heads_of(keys_back), preferred_element_type=jnp.float32
        )
        * factor
    )
    grad_values_sum = jnp.einsum(
        "ihrp,irhe->iphe",
        chance_back.astype(jnp.bfloat16),
        grad_mixed,
        preferred_element_type=jnp.float32,
    )
    grad_keys_sum = (
        jnp.einsum("ihrp,irhe->iphe", grad_scores, query, preferred_element_type=jnp.float32)
        * factor
    )
    grad_keys, grad_values = (
        lax.psum_scatter(
            grad_keys_sum.reshape(count, length_all, width).astype(jnp.bfloat16),
            "seq",
            scatter_dimension=1,
            tiled=True,
        ).astype(jnp.float32),
        lax.psum_scatter(
            grad_values_sum.reshape(count, length_all, width).astype(jnp.bfloat16),
            "seq",
            scatter_dimension=1,
            tiled=True,
        ).astype(jnp.float32),
    )
    grad_query_pre = (
        (grad_query * cosine - turn(grad_query * sine))
        .reshape(count, rows_here, width)
        .astype(jnp.bfloat16)
    )
    grad_keys_heads = heads_of(grad_keys)
    grad_keys_pre = (
        (grad_keys_heads * cosine - turn(grad_keys_heads * sine))
        .reshape(count, rows_here, width)
        .astype(jnp.bfloat16)
    )
    grad_values_pre = grad_values.astype(jnp.bfloat16)
    grad_w_query = weight_grad(normed, grad_query_pre)
    grad_w_key = weight_grad(normed, grad_keys_pre)
    grad_w_value = weight_grad(normed, grad_values_pre)
    grad_normed = (
        back_project(grad_query_pre, w_query)
        + back_project(grad_keys_pre, w_key)
        + back_project(grad_values_pre, w_value)
    )
    grad_gain_attn = jnp.sum(grad_normed * unit_attn, axis=(0, 1))
    grad_input = (grad_middle + norm_back(grad_normed, unit_attn, scale_attn, gain_attn)).astype(
        jnp.bfloat16
    )
    shares = (
        lax.psum_scatter(
            grad_gain_attn.astype(jnp.bfloat16), "items", scatter_dimension=0, tiled=True
        ).astype(jnp.float32),
        lax.psum_scatter(
            grad_w_query.astype(jnp.bfloat16), "items", scatter_dimension=0, tiled=True
        ).astype(jnp.float32),
        lax.psum_scatter(
            grad_w_key.astype(jnp.bfloat16), "items", scatter_dimension=0, tiled=True
        ).astype(jnp.float32),
        lax.psum_scatter(
            grad_w_value.astype(jnp.bfloat16), "items", scatter_dimension=0, tiled=True
        ).astype(jnp.float32),
        lax.psum_scatter(
            grad_w_out.astype(jnp.bfloat16), "items", scatter_dimension=0, tiled=True
        ).astype(jnp.float32),
        lax.psum_scatter(
            grad_gain_ffn.astype(jnp.bfloat16), "items", scatter_dimension=0, tiled=True
        ).astype(jnp.float32),
        lax.psum_scatter(
            grad_w_gate.astype(jnp.bfloat16), "items", scatter_dimension=0, tiled=True
        ).astype(jnp.float32),
        lax.psum_scatter(
            grad_w_up.astype(jnp.bfloat16), "items", scatter_dimension=0, tiled=True
        ).astype(jnp.float32),
        lax.psum_scatter(
            grad_w_down.astype(jnp.bfloat16), "items", scatter_dimension=0, tiled=True
        ).astype(jnp.float32),
    )
    summed = (
        lax.psum(shares[0].astype(jnp.bfloat16), "seq").astype(jnp.float32),
        lax.psum(shares[1].astype(jnp.bfloat16), "seq").astype(jnp.float32),
        lax.psum(shares[2].astype(jnp.bfloat16), "seq").astype(jnp.float32),
        lax.psum(shares[3].astype(jnp.bfloat16), "seq").astype(jnp.float32),
        lax.psum(shares[4].astype(jnp.bfloat16), "seq").astype(jnp.float32),
        lax.psum(shares[5].astype(jnp.bfloat16), "seq").astype(jnp.float32),
        lax.psum(shares[6].astype(jnp.bfloat16), "seq").astype(jnp.float32),
        lax.psum(shares[7].astype(jnp.bfloat16), "seq").astype(jnp.float32),
        lax.psum(shares[8].astype(jnp.bfloat16), "seq").astype(jnp.float32),
    )
    return (
        block_out,
        grad_input,
        summed[0],
        summed[1],
        summed[2],
        summed[3],
        summed[4],
        summed[5],
        summed[6],
        summed[7],
        summed[8],
    )


MESH = pl.DeviceIdType.MESH
WIDE = 256
LOW = jnp.bfloat16
F32 = jnp.float32
NEVER = -1e30

PLANS = "yxxzxzyyyyxxxyy"
ORDER = (
    (),
    (),
    (),
    (),
    (2, 42),
    (52, 12, 62),
    (),
    (32,),
    (),
    (22,),
    (72,),
    (3, 43),
    (),
    (63, 53, 82, 13),
    (102, 33, 92, 73),
    (23, 4, 44, 64),
    (14,),
    (),
    (112,),
    (45, 54, 103, 15),
    (74,),
    (
        24, 83, 5, 34, 65, 93, 132, 113, 104, 75, 84, 94, 122, 142, 152, 55, 114, 85, 95, 133,
        123, 143, 25, 134, 6, 35, 66, 105, 124, 76, 153, 144, 135, 115, 154, 86, 96, 145, 125,
        155, 136, 146,
    ),
)


def dot(left, right):
    return lax.dot_general(left, right, (((1,), (0,)), ((), ())), preferred_element_type=F32)


def dot_nt(left, right):
    return lax.dot_general(left, right, (((1,), (1,)), ((), ())), preferred_element_type=F32)


def dot_tn(left, right):
    return lax.dot_general(left, right, (((0,), (0,)), ((), ())), preferred_element_type=F32)


def rope_constants(rows):
    quarter = HD // 4
    freq = 10000.0 ** (-np.arange(quarter) / quarter)
    tables = []
    for side, length in ((SIDE_S, SIDE_S * SIDE_S + 1), (SIDE_L, SIDE_L * SIDE_L + 1)):
        place = np.arange(rows) - 1
        place = np.where((place >= 0) & (place < length - 1), place, 0)
        row = (place // side)[:, None] * freq
        col = (place % side)[:, None] * freq
        cosine = np.concatenate([np.cos(row), np.cos(row), np.cos(col), np.cos(col)], -1)
        sine = np.concatenate([-np.sin(row), np.sin(row), -np.sin(col), np.sin(col)], -1)
        tables += [np.concatenate([cosine, cosine], -1), np.concatenate([sine, sine], -1)]
    return np.stack(tables).astype(np.float32)


def swap_quarters(values):
    lane = lax.broadcasted_iota(jnp.int32, values.shape, 1)
    first = (lane % (HD // 2)) < HD // 4
    return jnp.where(
        first, pltpu.roll(values, 2 * HD - HD // 4, 1), pltpu.roll(values, HD // 4, 1)
    )


def fused(geo, *refs):
    rows_here, width, hidden_all = geo
    (
        lens, gain_a, gain_f, x_hbm, cot_hbm, tab_hbm,
        wq, wk, wv, wo, wg, wu, wd,
        bo_hbm, gi_hbm, fa_hbm, fd_hbm, fq_hbm, gain_hbm,
        x4, cot4, tab, wqkv_v, wo_v, wg_v, wu_v, wd_v,
        nrm, nrm_t, qkv, chance, mix_own, mix_in, mix, mix_t,
        mid, nf, nf_t, hid, hid_t, gg, gu, big,
        gnf_out, gnf_in, sb, rb, bo, bo_in, gb, gmx, ds_s, gqkv, sb2, rb2, gi, gi_in,
        gain_s, gain_x, gain_y, gain_z, gain_f_z, gain_c,
        pa, r1a, r2a, r3a, fa, pd, r1d, r2d, r3d, fd, pq, r1q, r2q, r3q, fq,
        sem_w, sem_in_s, sem_in_r, sem_core_s, sem_core_r, sem_gain_s, sem_gain_r, sem_o,
        sa_s, sa_r, sd_s, sd_r, sq_s, sq_r,
    ) = refs
    s = lax.axis_index("seq")
    i = lax.axis_index("items")
    y, c = s // 2, s % 2
    z, x = i // 2, i % 2
    rows = 4 * rows_here
    half = width // 2
    ff = hidden_all // 2
    pairs = half // 128
    step = rows_here
    fine = 32
    per = rows_here // step
    blocks = [(r0, min(256, rows - r0)) for r0 in range(0, rows, 256)]

    def device(y_to, c_to, z_to, x_to):
        return (y_to * 2 + c_to, z_to * 2 + x_to)

    sibling = device(y, 1 - c, z, x)
    y_dev = device(1 - y, c, z, x)
    x_dev = device(y, c, z, 1 - x)
    z_hi, z_lo = z // 2, z % 2
    near_z = device(y, c, z + 1 - 2 * z_lo, x)
    far_z = device(y, c, z + 2 - 4 * z_hi, x)

    started = []

    def send(src, dst, s_sem, r_sem, to):
        return pltpu.make_async_remote_copy(
            src_ref=src, dst_ref=dst, send_sem=s_sem, recv_sem=r_sem,
            device_id=to, device_id_type=MESH,
        )

    def weight_copies():
        copies = [pltpu.make_async_copy(tab_hbm, tab, sem_w.at[0])]
        mine = pl.ds(pl.multiple_of(c * half, half), half)
        for t, w in enumerate((wq, wk, wv)):
            copies.append(
                pltpu.make_async_copy(
                    w.at[:, mine], wqkv_v.at[:, pl.ds(t * half, half)], sem_w.at[1 + t]
                )
            )
        copies.append(pltpu.make_async_copy(wo, wo_v, sem_w.at[4]))
        for b in range(ff // 128):
            far = pl.ds(pl.multiple_of(256 * b + 128 * c, 128), 128)
            near = pl.ds(128 * b, 128)
            copies.append(pltpu.make_async_copy(wg.at[:, far], wg_v.at[:, near], sem_w.at[5 + 3 * b]))
            copies.append(pltpu.make_async_copy(wu.at[:, far], wu_v.at[:, near], sem_w.at[6 + 3 * b]))
            copies.append(pltpu.make_async_copy(wd.at[far], wd_v.at[near], sem_w.at[7 + 3 * b]))
        return copies

    weights = weight_copies()
    own_x = pltpu.make_async_copy(x_hbm.at[y], x4.at[s], sem_o.at[0])
    own_cot = pltpu.make_async_copy(cot_hbm.at[y], cot4.at[s], sem_o.at[1])
    own_x.start()
    for copy in weights[:4]:
        copy.start()

    barrier = pltpu.get_barrier_semaphore()
    for to in (sibling, y_dev, x_dev, near_z, far_z):
        pl.semaphore_signal(barrier, inc=1, device_id=to, device_id_type=MESH)
    pl.semaphore_wait(barrier, 5)

    s_y = (1 - y) * 2 + c
    across_x = send(x_hbm.at[1 - y], x4.at[s], sem_in_s.at[0], sem_in_r.at[0], y_dev)
    beside_x = send(x_hbm.at[y], x4.at[s], sem_in_s.at[1], sem_in_r.at[1], sibling)
    across_x.start()
    beside_x.start()
    across_c = send(cot_hbm.at[1 - y], cot4.at[s], sem_in_s.at[2], sem_in_r.at[2], y_dev)
    beside_c = send(cot_hbm.at[y], cot4.at[s], sem_in_s.at[3], sem_in_r.at[3], sibling)
    own_cot.start()
    for copy in weights[4:]:
        copy.start()
    relay_x = send(x4.at[s_y], x4.at[s_y], sem_in_s.at[4], sem_in_r.at[4], sibling)
    relay_c = send(cot4.at[s_y], cot4.at[s_y], sem_in_s.at[5], sem_in_r.at[5], sibling)

    length = lens[y]

    def norm_rows(piece):
        def one(b, carry):
            here = pl.ds(pl.multiple_of(b * step, step), step)
            values = x4[piece, here, :].astype(F32)
            scale = lax.rsqrt(jnp.mean(values * values, -1, keepdims=True) + epsilon)
            there = pl.ds(pl.multiple_of(piece * rows_here + b * step, step), step)
            nrm[there, :] = (values * scale * gain_a[...]).astype(LOW)
            return carry

        lax.fori_loop(0, per, one, 0)

    def project_rows(part):
        base = pl.multiple_of(part * 2 * rows_here, 32)
        here = pl.ds(base, 2 * rows_here)
        cosine = jnp.where(length == LONG, tab[2, here, :], tab[0, here, :])
        sine = jnp.where(length == LONG, tab[3, here, :], tab[1, here, :])
        for t in range(3):
            product = dot(nrm[here, :], wqkv_v[:, t * half : (t + 1) * half])
            for p in range(pairs):
                lanes = product[:, 128 * p : 128 * (p + 1)]
                if t < 2:
                    lanes = lanes * cosine + swap_quarters(lanes) * sine
                if t == 0:
                    lanes = lanes.astype(LOW).astype(F32) * HD ** (-0.5)
                qkv[t, here, 128 * p : 128 * (p + 1)] = lanes.astype(LOW)

    own_x.wait()
    norm_rows(s)
    beside_x.wait_recv()
    norm_rows(2 * y + 1 - c)
    for copy in weights[:4]:
        copy.wait()
    project_rows(y)
    across_x.wait_recv()
    relay_x.start()
    across_c.start()
    beside_c.start()
    norm_rows(s_y)
    relay_x.wait_recv()
    norm_rows(2 * (1 - y) + 1 - c)
    project_rows(1 - y)

    lane = lax.broadcasted_iota(jnp.int32, (1, 128), 1)
    left_head = lane < HD
    masks = [(lane // HD == n).astype(F32).astype(LOW) for n in range(2)]

    def mix_copy(pair):
        return send(
            mix_own.at[pair], mix_in.at[pair], sem_core_s.at[pair], sem_core_r.at[pair], sibling
        )

    def attend(pair, carry):
        lanes = pl.ds(pl.multiple_of(pair * 128, 128), 128)
        for r0, rb in blocks:
            nk = r0 + rb
            row = r0 + lax.broadcasted_iota(jnp.int32, (rb, nk), 0)
            col = lax.broadcasted_iota(jnp.int32, (rb, nk), 1)
            allowed = (col <= row) & (col < length)
            both = []
            for n in range(2):
                query = qkv[0, r0:nk, lanes] * masks[n]
                scores = jnp.where(allowed, dot_nt(query, qkv[1, :nk, lanes]), NEVER)
                expo = jnp.exp(scores - jnp.max(scores, -1, keepdims=True))
                low = (expo * (1.0 / jnp.sum(expo, -1, keepdims=True))).astype(LOW)
                chance[pair * 2 + n, r0:nk, :nk] = low
                both.append(dot(low, qkv[2, :nk, lanes]))
            mix_own[pair, r0:nk, :] = jnp.where(left_head, both[0], both[1]).astype(LOW)
        mix_copy(pair).start()
        return carry

    lax.fori_loop(0, pairs, attend, 0)

    across_c.wait_recv()
    relay_c.start()

    def turn_rows(src, dst):
        def one(b, carry):
            here = pl.ds(pl.multiple_of(b * 128, 128), 128)
            dst[:, here] = src[here, :].T
            return carry

        lax.fori_loop(0, rows // 128, one, 0)

    def place_mix(src, at):
        def one(p, carry):
            mix[:, pl.ds(pl.multiple_of(at * half + p * 128, 128), 128)] = src[p]
            return carry

        lax.fori_loop(0, pairs, one, 0)

    place_mix(mix_own, c)
    turn_rows(nrm, nrm_t)
    for p in range(pairs):
        mix_copy(p).wait_recv()
    place_mix(mix_in, 1 - c)

    weights[4].wait()

    def chunk(n, wide=WIDE):
        return pl.ds(pl.multiple_of(n * wide, wide), wide)

    def out_project(n, carry):
        mid[:, chunk(n)] = (
            dot(mix[...], wo_v[:, chunk(n)])
            + x4[:, :, chunk(n)].reshape(rows, WIDE).astype(F32)
        )
        return carry

    lax.fori_loop(0, width // WIDE, out_project, 0)

    def second_norm(b, carry):
        here = pl.ds(pl.multiple_of(b * step, step), step)
        values = mid[here, :]
        scale = lax.rsqrt(jnp.mean(values * values, -1, keepdims=True) + epsilon)
        nf[here, :] = (values * scale * gain_f[...]).astype(LOW)
        return carry

    lax.fori_loop(0, rows // step, second_norm, 0)
    turn_rows(nf, nf_t)
    for copy in weights[5:]:
        copy.wait()
    own_cot.wait()
    beside_c.wait_recv()
    relay_c.wait_recv()

    class Group:
        def __init__(self, parts, r1, r2, r3, fin, s_sem, r_sem):
            self.parts, self.r1, self.r2, self.r3, self.fin = parts, r1, r2, r3, fin
            self.s_sem, self.r_sem = s_sem, r_sem

        def copy(self, k, n, src, dst, to):
            return send(src, dst, self.s_sem.at[k, n], self.r_sem.at[k, n], to)

        def step1(self, k):
            self.hop(k, 0).start()

        def to_core(self, k):
            return self.copy(k, 5, self.fin.at[k, c], self.fin.at[k, c], sibling)

        def finish(self, k, own, new):
            for h in range(2):
                total = self.r1[own + (h,)].astype(F32) + self.r3[k, new + h].astype(F32)
                self.fin[k, c, h] = total.astype(LOW)
            self.to_core(k).start()

        def end(self, k):
            self.to_core(k).wait_recv()

        def sent(self, k):
            for n in range(self.hops):
                self.hop(k, n).wait_send()
            self.to_core(k).wait_send()

    def add(ref, at, other, of):
        ref[at] = (ref[at].astype(F32) + other[of].astype(F32)).astype(LOW)

    class XZY(Group):
        hops = 4

        def hop(self, k, n):
            r1, r2, r3 = self.r1, self.r2, self.r3
            if n == 0:
                return self.copy(k, n, self.parts.at[k, :, :, 1 - x], r1.at[k], x_dev)
            if n == 1:
                return self.copy(k, n, r1.at[k, :, 1 - z_lo], r2.at[k], near_z)
            if n == 2:
                return self.copy(k, n, r1.at[k, 1 - z_hi, z_lo], r3.at[k, pl.ds(0, 2)], far_z)
            return self.copy(k, n, r1.at[k, z_hi, z_lo], r3.at[k, pl.ds(2, 2)], y_dev)

        def step2(self, k):
            self.hop(k, 0).wait_recv()
            for lo in (1 - z_lo, z_lo):
                for hi in range(2):
                    for h in range(2):
                        add(self.r1, (k, hi, lo, h), self.parts, (k, hi, lo, x, h))
                if lo is not z_lo:
                    self.hop(k, 1).start()

        def step3(self, k):
            self.hop(k, 1).wait_recv()
            for hi in (1 - z_hi, z_hi):
                for h in range(2):
                    add(self.r1, (k, hi, z_lo, h), self.r2, (k, hi, h))
                if hi is not z_hi:
                    self.hop(k, 2).start()

        def step4(self, k):
            self.hop(k, 2).wait_recv()
            for h in range(2):
                add(self.r1, (k, z_hi, z_lo, h), self.r3, (k, h))
            self.hop(k, 3).start()

        def step5(self, k):
            self.hop(k, 3).wait_recv()
            self.finish(k, (k, z_hi, z_lo), 2)

    class ZXY(Group):
        hops = 4

        def hop(self, k, n):
            r1, r2, r3 = self.r1, self.r2, self.r3
            if n == 0:
                return self.copy(k, n, self.parts.at[k, :, 1 - z_lo], r1.at[k], near_z)
            if n == 1:
                return self.copy(k, n, r1.at[k, 1 - z_hi], r2.at[k], far_z)
            if n == 2:
                return self.copy(k, n, r1.at[k, z_hi, 1 - x], r3.at[k, pl.ds(0, 2)], x_dev)
            return self.copy(k, n, r1.at[k, z_hi, x], r3.at[k, pl.ds(2, 2)], y_dev)

        def step2(self, k):
            self.hop(k, 0).wait_recv()
            for hi in (1 - z_hi, z_hi):
                for xx in range(2):
                    for h in range(2):
                        add(self.r1, (k, hi, xx, h), self.parts, (k, hi, z_lo, xx, h))
                if hi is not z_hi:
                    self.hop(k, 1).start()

        def step3(self, k):
            self.hop(k, 1).wait_recv()
            for xx in (1 - x, x):
                for h in range(2):
                    add(self.r1, (k, z_hi, xx, h), self.r2, (k, xx, h))
                if xx is not x:
                    self.hop(k, 2).start()

        def step4(self, k):
            self.hop(k, 2).wait_recv()
            for h in range(2):
                add(self.r1, (k, z_hi, x, h), self.r3, (k, h))
            self.hop(k, 3).start()

        def step5(self, k):
            self.hop(k, 3).wait_recv()
            self.finish(k, (k, z_hi, x), 2)

    class YXZ(Group):
        hops = 5

        def hop(self, k, n):
            r1, r2, r3 = self.r1, self.r2, self.r3
            if n == 0:
                return self.copy(k, n, self.parts.at[k, :, :, :, 1 - y], r1.at[k], y_dev)
            if n == 1:
                return self.copy(k, n, r1.at[k, :, :, 1 - x], r2.at[k], x_dev)
            if n == 2:
                return self.copy(k, n, r2.at[k, :, 1 - z_lo], r3.at[k, pl.ds(0, 2)], near_z)
            if n == 3:
                return self.copy(k, n, r2.at[k, 1 - z_hi, z_lo], r3.at[k, 2], far_z)
            return self.copy(k, n, self.fin.at[k, c, y], self.fin.at[k, c, y], y_dev)

        def beside(self, k, n):
            at = self.fin.at[k, c, y] if n == 0 else self.fin.at[k, c, 1 - y]
            return self.copy(k, 5 + n, at, at, sibling)

        def step2(self, k):
            self.hop(k, 0).wait_recv()
            for xx in (1 - x, x):
                for hi in range(2):
                    for lo in range(2):
                        add(self.r1, (k, hi, lo, xx), self.parts, (k, hi, lo, xx, y))
                if xx is not x:
                    self.hop(k, 1).start()

        def step3(self, k):
            self.hop(k, 1).wait_recv()
            for lo in (1 - z_lo, z_lo):
                for hi in range(2):
                    add(self.r2, (k, hi, lo), self.r1, (k, hi, lo, x))
                if lo is not z_lo:
                    self.hop(k, 2).start()

        def step4(self, k):
            self.hop(k, 2).wait_recv()
            for hi in (1 - z_hi, z_hi):
                add(self.r2, (k, hi, z_lo), self.r3, (k, hi))
                if hi is not z_hi:
                    self.hop(k, 3).start()

        def step5(self, k):
            self.hop(k, 3).wait_recv()
            total = self.r2[k, z_hi, z_lo].astype(F32) + self.r3[k, 2].astype(F32)
            self.fin[k, c, y] = total.astype(LOW)
            self.hop(k, 4).start()
            self.beside(k, 0).start()

        def step6(self, k):
            self.hop(k, 4).wait_recv()
            self.beside(k, 1).start()

        def end(self, k):
            for n in range(2):
                self.beside(k, n).wait_recv()

        def sent(self, k):
            for n in range(self.hops):
                self.hop(k, n).wait_send()
            for n in range(2):
                self.beside(k, n).wait_send()

    class Gains:
        def hop(self, k, n):
            src = (gain_s, gain_x, gain_y, gain_z, gain_s)[n]
            dst = (gain_x, gain_y, gain_z, gain_f_z, gain_c)[n]
            to = (x_dev, y_dev, near_z, far_z, sibling)[n]
            return send(src, dst, sem_gain_s.at[n], sem_gain_r.at[n], to)

        def step1(self, k):
            self.hop(k, 0).start()

        def step2(self, k):
            self.hop(k, 0).wait()
            gain_x[...] = gain_s[...] + gain_x[...]
            self.hop(k, 1).start()

        def step3(self, k):
            self.hop(k, 1).wait()
            gain_y[...] = gain_x[...] + gain_y[...]
            self.hop(k, 2).start()

        def step4(self, k):
            self.hop(k, 2).wait()
            gain_z[...] = gain_y[...] + gain_z[...]
            self.hop(k, 3).start()

        def step5(self, k):
            self.hop(k, 3).wait()
            gain_s[...] = gain_z[...] + gain_f_z[...]
            self.hop(k, 4).start()

        def end(self, k):
            self.hop(k, 4).wait()
            top = lax.broadcasted_iota(jnp.int32, gain_s.shape, 0) == 0
            total = gain_s[...] + jnp.where(top, gain_c[...], 0.0)
            gain_c[...] = pltpu.roll(total, lax.rem(8 - i, 8) * (width // 8), 1)

        def sent(self, k):
            pass

    buffers_a = (pa, r1a, r2a, r3a, fa, sa_s, sa_r)
    buffers_d = (pd, r1d, r2d, r3d, fd, sd_s, sd_r)
    buffers_q = (pq, r1q, r2q, r3q, fq, sq_s, sq_r)
    kinds = {"x": XZY, "y": YXZ, "z": ZXY}
    chunks = [(kinds[kind](*buffers_a), n) for n, kind in enumerate(PLANS[:8])]
    chunks += [(kinds[kind](*buffers_d), n) for n, kind in enumerate(PLANS[8:11])]
    chunks += [(kinds[kind](*buffers_q), n) for n, kind in enumerate(PLANS[11:])]
    chunks += [(Gains(), 0)]
    slots = iter(ORDER)

    def first(chunk):
        group, k = chunks[chunk]
        group.step1(k)

    def turn():
        for code in next(slots):
            group, k = chunks[code // 10]
            getattr(group, f"step{code % 10}")(k)

    chunks_f = ff // WIDE
    chunks_w = width // WIDE

    def feed(n, carry):
        at = chunk(n)
        big[:, 0:WIDE] = dot(nf[...], wg_v[:, at])
        big[:, WIDE : 2 * WIDE] = dot(nf[...], wu_v[:, at])
        big[:, 2 * WIDE : 3 * WIDE] = dot_nt(cot4[...].reshape(rows, width), wd_v[at, :])

        def one(b, inner):
            here = pl.ds(pl.multiple_of(b * fine, fine), fine)
            gate = big[here, 0:WIDE]
            up = big[here, WIDE : 2 * WIDE]
            back = big[here, 2 * WIDE : 3 * WIDE]
            sigma = 0.5 * jnp.tanh(0.5 * gate) + 0.5
            silu = gate * sigma
            hid[here, at] = (silu * up).astype(LOW)
            gg[here, at] = (back * up * (sigma + silu * (1.0 - sigma))).astype(LOW)
            gu[here, at] = (back * silu).astype(LOW)
            return inner

        lax.fori_loop(0, rows // fine, one, 0, unroll=5)
        shape = pa.shape[1:]
        pa[n] = dot(nf_t[...], gg[:, at]).reshape(shape).astype(LOW)
        first(n)
        pa[n + chunks_f] = dot(nf_t[...], gu[:, at]).reshape(shape).astype(LOW)
        first(n + chunks_f)
        hid_t[at, :] = hid[:, at].T
        return carry

    for n in range(chunks_f):
        turn()
        feed(n, 0)
    turn()

    def gnf_copy(n):
        return send(
            gnf_out.at[n], gnf_in.at[n], sem_core_s.at[pairs + n], sem_core_r.at[pairs + n], sibling
        )

    def back_ffn(n, carry):
        partial = dot_nt(gg[...], wg_v[chunk(n), :]) + dot_nt(gu[...], wu_v[chunk(n), :])
        big[:, chunk(n)] = partial
        gnf_out[n] = partial.astype(LOW)
        gnf_copy(n).start()
        return carry

    lax.fori_loop(0, chunks_w, back_ffn, 0)
    turn()

    def down(n, carry):
        big[:, chunk(n + chunks_w)] = dot(hid[...], wd_v[:, chunk(n)])
        return carry

    lax.fori_loop(0, chunks_w, down, 0)
    n_core = pairs + chunks_w
    bo_copy = send(sb, rb, sem_core_s.at[n_core], sem_core_r.at[n_core], sibling)
    far = slice(width, 2 * width)

    def for_rows(core, fn):
        for yy in range(2):
            def one(b, carry, yy=yy):
                base = pl.multiple_of((2 * yy + core) * rows_here + b * step, step)
                fn(yy, b, pl.ds(base, step), pl.ds(pl.multiple_of(b * step, step), step))
                return carry

            lax.fori_loop(0, per, one, 0)

    def pack_bo(yy, b, here, there):
        sb[yy, there, :] = big[here, far].astype(LOW)

    for_rows(1 - c, pack_bo)
    bo_copy.start()

    for n in range(chunks_w):
        turn()
        at = slice(n * WIDE, (n + 1) * WIDE)
        pd[n] = (
            dot(hid_t[...], cot4[:, :, at].reshape(rows, WIDE)).reshape(pd.shape[1:]).astype(LOW)
        )
        first(8 + n)

    turn()
    bo_copy.wait_recv()

    def finish_bo(yy, b, here, there):
        bo[yy, there, :] = (mid[here, :] + big[here, far] + rb[yy, there, :].astype(F32)).astype(LOW)

    for_rows(c, finish_bo)
    bo_across = send(bo.at[1 - y], bo_in, sem_in_s.at[6], sem_in_r.at[6], y_dev)
    bo_across.start()

    turn()
    for n in range(chunks_w):
        gnf_copy(n).wait_recv()

    def middle_back(b, total):
        here = pl.ds(pl.multiple_of(b * step, step), step)
        values = mid[here, :]
        grad = big[here, 0:width] + jnp.concatenate(
            [gnf_in[n, here, :].astype(F32) for n in range(chunks_w)], -1
        )
        scale = lax.rsqrt(jnp.mean(values * values, -1, keepdims=True) + epsilon)
        unit = values * scale
        total = total + (grad * unit).reshape(step // 8, 8, width).sum(0)
        scaled = grad * gain_f[...]
        inner = jnp.mean(scaled * unit, -1, keepdims=True)
        out = cot4[b // per, pl.ds(pl.multiple_of(lax.rem(b, per) * step, step), step), :].astype(F32)
        out = out + scale * (scaled - unit * inner)
        mid[here, :] = out
        gb[here, :] = out.astype(LOW)
        return total

    total_f = lax.fori_loop(0, rows // step, middle_back, jnp.zeros((8, width), F32))

    turn()
    turn_rows(mix, mix_t)
    mine = pl.ds(pl.multiple_of(c * half, half), half)
    pq[0] = dot(mix_t[...], gb[:, mine]).reshape(pq.shape[1:]).astype(LOW)
    first(11)
    gmx[...] = dot_nt(gb[...], wo_v[mine, :]).astype(LOW)

    def attend_back(pair, carry):
        lanes = slice(pair * 128, pair * 128 + 128)

        def keep(n, at, off, value):
            where_ = slice(off * 128, off * 128 + 128)
            if n:
                value = jnp.where(left_head, big[at, where_], value)
            big[at, where_] = value

        for n in range(2):
            head = pair * 2 + n
            for r0, rb_ in blocks:
                nk = r0 + rb_
                grad = gmx[r0:nk, lanes] * masks[n]
                prob = chance[head, r0:nk, :nk].astype(F32)
                each = dot_nt(grad, qkv[2, :nk, lanes]) * prob
                low = (each - prob * jnp.sum(each, -1, keepdims=True)).astype(LOW)
                ds_s[r0:nk, :nk] = low
                keep(n, slice(r0, nk), 0, dot(low, qkv[1, :nk, lanes]))
            for k0, kb in blocks:
                at = slice(k0, k0 + kb)
                keep(n, at, 1, dot_tn(ds_s[k0:, at], qkv[0, k0:, lanes]))
                keep(n, at, 2, dot_tn(chance[head, k0:, at], gmx[k0:, lanes]))

        def one(b, inner):
            here = pl.ds(pl.multiple_of(b * 64, 64), 64)
            cosine = jnp.where(length == LONG, tab[2, here, :], tab[0, here, :])
            sine = jnp.where(length == LONG, tab[3, here, :], tab[1, here, :])
            for t in range(3):
                values = big[here, 128 * t : 128 * (t + 1)]
                if t == 0:
                    values = values * HD ** (-0.5)
                if t < 2:
                    values = values * cosine - swap_quarters(values) * sine
                gqkv[here, t * half + pair * 128 : t * half + pair * 128 + 128] = values.astype(LOW)
            return inner

        lax.fori_loop(0, rows // 64, one, 0)
        return carry

    for pair in range(pairs):
        turn()
        attend_back(pair, 0)

    for t in range(3):
        turn()
        pq[1 + t] = (
            dot(nrm_t[...], gqkv[:, t * half : (t + 1) * half]).reshape(pq.shape[1:]).astype(LOW)
        )
        first(12 + t)

    turn()

    def back_attn(n, carry):
        big[:, chunk(n)] = dot_nt(gqkv[...], wqkv_v[chunk(n), :])
        return carry

    lax.fori_loop(0, chunks_w, back_attn, 0)
    turn()

    def pack_gi(yy, b, here, there):
        sb2[yy, there, :] = big[here, 0:width].astype(LOW)

    for_rows(1 - c, pack_gi)
    gi_copy = send(sb2, rb2, sem_core_s.at[n_core + 1], sem_core_r.at[n_core + 1], sibling)
    gi_copy.start()

    def gain_back(b, total):
        here = pl.ds(pl.multiple_of(b * step, step), step)
        values = x4[b // per, pl.ds(pl.multiple_of(lax.rem(b, per) * step, step), step), :].astype(F32)
        scale = lax.rsqrt(jnp.mean(values * values, -1, keepdims=True) + epsilon)
        return total + (big[here, 0:width] * (values * scale)).reshape(step // 8, 8, width).sum(0)

    total_a = lax.fori_loop(0, rows // step, gain_back, jnp.zeros((8, width), F32))
    row = lax.broadcasted_iota(jnp.int32, (8, width), 0)
    gain_s[...] = jnp.where(
        row == 0, jnp.sum(total_a, 0, keepdims=True), jnp.sum(total_f, 0, keepdims=True)
    )
    first(15)
    turn()
    gi_copy.wait_recv()

    def finish_gi(yy, b, here, there):
        values = x4[2 * yy + c, there, :].astype(F32)
        scale = lax.rsqrt(jnp.mean(values * values, -1, keepdims=True) + epsilon)
        unit = values * scale
        scaled = (big[here, 0:width] + rb2[yy, there, :].astype(F32)) * gain_a[...]
        inner = jnp.mean(scaled * unit, -1, keepdims=True)
        gi[yy, there, :] = (mid[here, :] + scale * (scaled - unit * inner)).astype(LOW)

    for_rows(c, finish_gi)
    gi_across = send(gi.at[1 - y], gi_in, sem_in_s.at[7], sem_in_r.at[7], y_dev)
    gi_across.start()

    turn()
    for group, k in chunks:
        group.end(k)

    outs = [
        pltpu.make_async_copy(fa, fa_hbm, sem_o.at[2]),
        pltpu.make_async_copy(fd, fd_hbm, sem_o.at[3]),
        pltpu.make_async_copy(fq, fq_hbm, sem_o.at[4]),
        pltpu.make_async_copy(gain_c, gain_hbm, sem_o.at[5]),
        pltpu.make_async_copy(bo.at[y], bo_hbm.at[y], sem_o.at[6]),
        pltpu.make_async_copy(gi.at[y], gi_hbm.at[y], sem_o.at[7]),
    ]
    for copy in outs:
        copy.start()
    bo_across.wait_recv()
    gi_across.wait_recv()
    outs += [
        pltpu.make_async_copy(bo_in, bo_hbm.at[1 - y], sem_o.at[8]),
        pltpu.make_async_copy(gi_in, gi_hbm.at[1 - y], sem_o.at[9]),
    ]
    for copy in outs[6:]:
        copy.start()
    for copy in outs:
        copy.wait()

    for copy in (across_x, beside_x, across_c, beside_c, relay_x, relay_c, bo_across, gi_across):
        copy.wait_send()
    for p in range(pairs):
        mix_copy(p).wait_send()
    for n in range(chunks_w):
        gnf_copy(n).wait_send()
    bo_copy.wait_send()
    gi_copy.wait_send()
    for group, k in chunks:
        group.sent(k)


def spread(chunks_f, share, *refs):
    far, refs = refs[:6], refs[6:]
    outs, near, sem = refs[:11], refs[11:17], refs[17]
    bo_out, gi_out, da, dq, dk, dv, do, df, dg, du, dd = outs
    copies = [pltpu.make_async_copy(a, b, sem.at[n]) for n, (a, b) in enumerate(zip(far, near))]
    for copy in copies:
        copy.start()
    fa, fd, fq, bo, gi, gains = near
    for copy in copies:
        copy.wait()
    bo_out[...] = bo[...]
    gi_out[...] = gi[...]
    da[...] = gains[0, 0:share]
    df[...] = gains[1, 0:share]
    rows = fa.shape[3]
    for core in range(2):
        for h in range(2):
            at = slice(h * rows, (h + 1) * rows)
            for n in range(chunks_f):
                for b in range(WIDE // 128):
                    far = 256 * (n * (WIDE // 128) + b) + 128 * core
                    near = slice(128 * b, 128 * (b + 1))
                    dg[at, far : far + 128] = fa[n, core, h, :, near].astype(F32)
                    du[at, far : far + 128] = fa[n + chunks_f, core, h, :, near].astype(F32)
            half = fq.shape[4]
            lanes = slice(core * half, (core + 1) * half)
            for n, ref in enumerate((do, dq, dk, dv)):
                ref[at, lanes] = fq[n, core, h].astype(F32)
            deep = fd.shape[3]
            at = slice((2 * core + h) * deep, (2 * core + h + 1) * deep)
            for n in range(fd.shape[0]):
                dd[at, WIDE * n : WIDE * (n + 1)] = fd[n, core, h].astype(F32)


def item_per_chip(
    block_in, lengths, gain_attn, w_query, w_key, w_value, w_out, gain_ffn, w_gate, w_up, w_down,
    cotangent,
):
    _, rows_here, width = block_in.shape
    hidden_all = w_gate.shape[1]
    rows = rows_here * lax.axis_size("seq")
    shares = lax.axis_size("items")
    half, ff = width // 2, hidden_all // 2
    pairs = half // 128
    chunks_f, chunks_w = ff // WIDE, width // WIDE
    thin, deep = width // shares // 2, ff // shares // 2
    tables = jnp.asarray(rope_constants(rows))
    any_ = pl.BlockSpec(memory_space=pl.ANY)
    vmem = pl.BlockSpec(memory_space=pltpu.VMEM)

    def group(n, r, w):
        return [
            pltpu.VMEM((n, 2, 2, 2, 2, r, w), LOW),
            pltpu.VMEM((n, 2, 2, 2, r, w), LOW),
            pltpu.VMEM((n, 2, 2, r, w), LOW),
            pltpu.VMEM((n, 4, r, w), LOW),
            pltpu.VMEM((n, 2, 2, r, w), LOW),
        ]

    def low(*shape):
        return pltpu.VMEM(shape, LOW)

    def full(*shape):
        return pltpu.VMEM(shape, F32)

    dma = pltpu.SemaphoreType.DMA
    scratch = [
        low(4, rows_here, width), low(4, rows_here, width), full(4, rows, 128),
        low(width, 3 * half), low(width, width), low(width, ff), low(width, ff), low(ff, width),
        low(rows, width), low(width, rows), low(3, rows, half), low(2 * pairs, rows, rows),
        low(pairs, rows, 128), low(pairs, rows, 128), low(rows, width), low(width, rows),
        full(rows, width), low(rows, width), low(width, rows), low(rows, ff), low(ff, rows),
        low(rows, ff), low(rows, ff), full(rows, 2 * width),
        low(chunks_w, rows, WIDE), low(chunks_w, rows, WIDE),
        low(2, rows_here, width), low(2, rows_here, width),
        low(2, rows_here, width), low(rows_here, width),
        low(rows, width), low(rows, half), low(rows, rows), low(rows, 3 * half),
        low(2, rows_here, width), low(2, rows_here, width),
        low(2, rows_here, width), low(rows_here, width),
        full(8, width), full(8, width), full(8, width), full(8, width), full(8, width), full(8, width),
    ]
    scratch += group(2 * chunks_f, thin, WIDE) + group(chunks_w, deep, WIDE) + group(4, thin, half)
    scratch += [
        dma((5 + 3 * (ff // 128),)), dma((8,)), dma((8,)),
        dma((pairs + chunks_w + 2,)), dma((pairs + chunks_w + 2,)), dma((6,)), dma((6,)), dma((10,)),
        dma((2 * chunks_f, 8)), dma((2 * chunks_f, 8)), dma((chunks_w, 8)), dma((chunks_w, 8)),
        dma((4, 8)), dma((4, 8)),
    ]
    shape = jax.ShapeDtypeStruct
    bo, gi, fa, fd, fq, gains = pl.pallas_call(
        functools.partial(fused, (rows_here, width, hidden_all)),
        out_shape=(
            shape(block_in.shape, LOW), shape(block_in.shape, LOW),
            shape((2 * chunks_f, 2, 2, thin, WIDE), LOW), shape((chunks_w, 2, 2, deep, WIDE), LOW),
            shape((4, 2, 2, thin, half), LOW), shape((8, width), F32),
        ),
        in_specs=[pl.BlockSpec(memory_space=pltpu.SMEM), vmem, vmem] + [any_] * 10,
        out_specs=(any_,) * 6,
        scratch_shapes=scratch,
        compiler_params=pltpu.CompilerParams(
            collective_id=0, has_side_effects=True, vmem_limit_bytes=63 * 2**20
        ),
        name="block",
    )(
        lengths, gain_attn, gain_ffn, block_in, cotangent, tables,
        w_query, w_key, w_value, w_out, w_gate, w_up, w_down,
    )
    thick = (width // shares, width)
    made = (fa, fd, fq, bo, gi, gains)
    share = width // shares
    bo, gi, da, dq, dk, dv, do, df, dg, du, dd = pl.pallas_call(
        functools.partial(spread, chunks_f, share),
        out_shape=(
            shape(block_in.shape, LOW), shape(block_in.shape, LOW), shape((share,), F32),
            shape(thick, F32), shape(thick, F32), shape(thick, F32), shape(thick, F32),
            shape((share,), F32),
            shape((width // shares, hidden_all), F32), shape((width // shares, hidden_all), F32),
            shape((hidden_all // shares, width), F32),
        ),
        in_specs=[any_] * 6,
        out_specs=(vmem,) * 11,
        scratch_shapes=[pltpu.VMEM(a.shape, a.dtype) for a in made] + [dma((6,))],
        compiler_params=pltpu.CompilerParams(vmem_limit_bytes=60 * 2**20),
        name="spread",
    )(*made)
    return bo, gi, da, dq, dk, dv, do, df, dg, du, dd


def solution(mesh):
    fits = mesh.shape["seq"] == 4 and mesh.shape["items"] == 8
    return jax.shard_map(
        item_per_chip if fits else body,
        mesh=mesh,
        in_specs=(P("items", "seq", None), P("items")) + (P(),) * 9 + (P("items", "seq", None),),
        out_specs=(
            (P("items", "seq", None),) * 2
            + (P("items"),) + (P("items", None),) * 4
            + (P("items"),) + (P("items", None),) * 3
        ),
        check_vma=False,
    )
```

```python
import functools

import jax
import jax.numpy as jnp
import numpy as np
from jax import lax
from jax.experimental import pallas as pl
from jax.experimental.pallas import tpu as pltpu
from jax.sharding import PartitionSpec as P

HD = 64
SIDE_S = 16
SIDE_L = 24
LONG = 577


epsilon = 1e-05


def grid_places(lengths, rows):
    side = jnp.where(lengths == LONG, SIDE_L, SIDE_S).astype(jnp.int32)[:, None]
    place = rows[None, :] - 1
    valid = (place >= 0) & (rows[None, :] < lengths[:, None])
    place = jnp.where(valid, place, 0)
    return (place // side, place % side)


def rotary_tables(lengths, rows):
    grid_row, grid_col = grid_places(lengths, rows)
    quarter = HD // 4
    freq = 10000.0 ** (-jnp.arange(quarter, dtype=jnp.float32) / quarter)
    angle_row = grid_row[..., None].astype(jnp.float32) * freq
    angle_col = grid_col[..., None].astype(jnp.float32) * freq
    cosine = jnp.concatenate(
        [jnp.cos(angle_row), jnp.cos(angle_row), jnp.cos(angle_col), jnp.cos(angle_col)], -1
    )
    sine = jnp.concatenate(
        [jnp.sin(angle_row), jnp.sin(angle_row), jnp.sin(angle_col), jnp.sin(angle_col)], -1
    )
    return (cosine[:, :, None, :], sine[:, :, None, :])


def turn(values):
    quarter = HD // 4
    first = values[..., 0:quarter]
    second = values[..., quarter : 2 * quarter]
    third = values[..., 2 * quarter : 3 * quarter]
    fourth = values[..., 3 * quarter :]
    return jnp.concatenate([-second, first, -fourth, third], -1)


def project(left, right):
    return jnp.einsum("ird,de->ire", left, right, preferred_element_type=jnp.float32)


def back_project(grad, weight):
    return jnp.einsum("ire,de->ird", grad, weight, preferred_element_type=jnp.float32)


def weight_grad(left, right):
    return jnp.einsum("ird,ire->de", left, right, preferred_element_type=jnp.float32)


def norm_back(grad_normed, unit, scale, gain):
    scaled = grad_normed * gain
    return scale * (scaled - unit * jnp.mean(scaled * unit, -1, keepdims=True))


def body(
    block_in,
    lengths,
    gain_attn,
    w_query,
    w_key,
    w_value,
    w_out,
    gain_ffn,
    w_gate,
    w_up,
    w_down,
    cotangent,
):
    count, rows_here, width = block_in.shape
    heads = width // HD
    length_all = rows_here * lax.axis_size("seq")
    factor = HD ** (-0.5)
    query_rows = lax.axis_index("seq") * rows_here + jnp.arange(rows_here, dtype=jnp.int32)
    key_rows = jnp.arange(length_all, dtype=jnp.int32)
    cosine, sine = rotary_tables(lengths, query_rows)
    allowed = (key_rows[None, None, :] <= query_rows[None, :, None]) & (
        key_rows[None, None, :] < lengths[:, None, None]
    )

    def heads_of(array):
        return array.reshape(array.shape[0], array.shape[1], heads, HD)

    def attention_scores(query, keys_all):
        raw = (
            jnp.einsum(
                "irhe,iphe->ihrp", query, heads_of(keys_all), preferred_element_type=jnp.float32
            )
            * factor
        )
        return jnp.where(allowed[:, None], raw, -1e30)

    source = block_in.astype(jnp.float32)
    scale_attn = lax.rsqrt(jnp.mean(source * source, -1, keepdims=True) + epsilon)
    unit_attn = source * scale_attn
    normed = (unit_attn * gain_attn).astype(jnp.bfloat16)
    query_pre = heads_of(project(normed, w_query))
    keys_pre = heads_of(project(normed, w_key))
    query = (query_pre * cosine + turn(query_pre) * sine).astype(jnp.bfloat16)
    keys = (
        (keys_pre * cosine + turn(keys_pre) * sine)
        .astype(jnp.bfloat16)
        .reshape(count, rows_here, width)
    )
    values = project(normed, w_value).astype(jnp.bfloat16)
    keys_all, values_all = (
        lax.all_gather(keys, "seq", axis=1, tiled=True),
        lax.all_gather(values, "seq", axis=1, tiled=True),
    )
    scores = attention_scores(query, keys_all)
    top = jnp.max(scores, -1, keepdims=True)
    expo = jnp.exp(scores - top)
    summed = jnp.sum(expo, -1, keepdims=True)
    chance = expo / summed
    log_total = top + jnp.log(summed)
    mixed = (
        jnp.einsum(
            "ihrp,iphe->irhe",
            chance.astype(jnp.bfloat16),
            heads_of(values_all),
            preferred_element_type=jnp.float32,
        )
        .reshape(count, rows_here, width)
        .astype(jnp.bfloat16)
    )
    middle = source + project(mixed, w_out)
    scale_ffn = lax.rsqrt(jnp.mean(middle * middle, -1, keepdims=True) + epsilon)
    unit_ffn = middle * scale_ffn
    normed_ffn = (unit_ffn * gain_ffn).astype(jnp.bfloat16)
    gate = project(normed_ffn, w_gate)
    up = project(normed_ffn, w_up)
    sigma = jax.nn.sigmoid(gate)
    hidden = (gate * sigma * up).astype(jnp.bfloat16)
    block_out = (middle + project(hidden, w_down)).astype(jnp.bfloat16)
    incoming = cotangent.astype(jnp.float32)
    grad_w_down = weight_grad(hidden, cotangent)
    grad_hidden = back_project(cotangent, w_down)
    grad_gate = (grad_hidden * up * sigma * (1.0 + gate * (1.0 - sigma))).astype(jnp.bfloat16)
    grad_up = (grad_hidden * gate * sigma).astype(jnp.bfloat16)
    grad_w_gate = weight_grad(normed_ffn, grad_gate)
    grad_w_up = weight_grad(normed_ffn, grad_up)
    grad_normed_ffn = back_project(grad_gate, w_gate) + back_project(grad_up, w_up)
    grad_gain_ffn = jnp.sum(grad_normed_ffn * unit_ffn, axis=(0, 1))
    grad_middle = incoming + norm_back(grad_normed_ffn, unit_ffn, scale_ffn, gain_ffn)
    grad_branch = grad_middle.astype(jnp.bfloat16)
    grad_w_out = weight_grad(mixed, grad_branch)
    grad_mixed = heads_of(back_project(grad_branch, w_out)).astype(jnp.bfloat16)
    keys_back, values_back = (keys_all, values_all)
    chance_back = jnp.exp(attention_scores(query, keys_back) - log_total)
    grad_chance = jnp.einsum(
        "irhe,iphe->ihrp", grad_mixed, heads_of(values_back), preferred_element_type=jnp.float32
    )
    inner = jnp.sum(grad_chance * chance_back, -1, keepdims=True)
    grad_scores = (chance_back * (grad_chance - inner)).astype(jnp.bfloat16)
    grad_query = (
        jnp.einsum(
            "ihrp,iphe->irhe", grad_scores, heads_of(keys_back), preferred_element_type=jnp.float32
        )
        * factor
    )
    grad_values_sum = jnp.einsum(
        "ihrp,irhe->iphe",
        chance_back.astype(jnp.bfloat16),
        grad_mixed,
        preferred_element_type=jnp.float32,
    )
    grad_keys_sum = (
        jnp.einsum("ihrp,irhe->iphe", grad_scores, query, preferred_element_type=jnp.float32)
        * factor
    )
    grad_keys, grad_values = (
        lax.psum_scatter(
            grad_keys_sum.reshape(count, length_all, width).astype(jnp.bfloat16),
            "seq",
            scatter_dimension=1,
            tiled=True,
        ).astype(jnp.float32),
        lax.psum_scatter(
            grad_values_sum.reshape(count, length_all, width).astype(jnp.bfloat16),
            "seq",
            scatter_dimension=1,
            tiled=True,
        ).astype(jnp.float32),
    )
    grad_query_pre = (
        (grad_query * cosine - turn(grad_query * sine))
        .reshape(count, rows_here, width)
        .astype(jnp.bfloat16)
    )
    grad_keys_heads = heads_of(grad_keys)
    grad_keys_pre = (
        (grad_keys_heads * cosine - turn(grad_keys_heads * sine))
        .reshape(count, rows_here, width)
        .astype(jnp.bfloat16)
    )
    grad_values_pre = grad_values.astype(jnp.bfloat16)
    grad_w_query = weight_grad(normed, grad_query_pre)
    grad_w_key = weight_grad(normed, grad_keys_pre)
    grad_w_value = weight_grad(normed, grad_values_pre)
    grad_normed = (
        back_project(grad_query_pre, w_query)
        + back_project(grad_keys_pre, w_key)
        + back_project(grad_values_pre, w_value)
    )
    grad_gain_attn = jnp.sum(grad_normed * unit_attn, axis=(0, 1))
    grad_input = (grad_middle + norm_back(grad_normed, unit_attn, scale_attn, gain_attn)).astype(
        jnp.bfloat16
    )
    shares = (
        lax.psum_scatter(
            grad_gain_attn.astype(jnp.bfloat16), "items", scatter_dimension=0, tiled=True
        ).astype(jnp.float32),
        lax.psum_scatter(
            grad_w_query.astype(jnp.bfloat16), "items", scatter_dimension=0, tiled=True
        ).astype(jnp.float32),
        lax.psum_scatter(
            grad_w_key.astype(jnp.bfloat16), "items", scatter_dimension=0, tiled=True
        ).astype(jnp.float32),
        lax.psum_scatter(
            grad_w_value.astype(jnp.bfloat16), "items", scatter_dimension=0, tiled=True
        ).astype(jnp.float32),
        lax.psum_scatter(
            grad_w_out.astype(jnp.bfloat16), "items", scatter_dimension=0, tiled=True
        ).astype(jnp.float32),
        lax.psum_scatter(
            grad_gain_ffn.astype(jnp.bfloat16), "items", scatter_dimension=0, tiled=True
        ).astype(jnp.float32),
        lax.psum_scatter(
            grad_w_gate.astype(jnp.bfloat16), "items", scatter_dimension=0, tiled=True
        ).astype(jnp.float32),
        lax.psum_scatter(
            grad_w_up.astype(jnp.bfloat16), "items", scatter_dimension=0, tiled=True
        ).astype(jnp.float32),
        lax.psum_scatter(
            grad_w_down.astype(jnp.bfloat16), "items", scatter_dimension=0, tiled=True
        ).astype(jnp.float32),
    )
    summed = (
        lax.psum(shares[0].astype(jnp.bfloat16), "seq").astype(jnp.float32),
        lax.psum(shares[1].astype(jnp.bfloat16), "seq").astype(jnp.float32),
        lax.psum(shares[2].astype(jnp.bfloat16), "seq").astype(jnp.float32),
        lax.psum(shares[3].astype(jnp.bfloat16), "seq").astype(jnp.float32),
        lax.psum(shares[4].astype(jnp.bfloat16), "seq").astype(jnp.float32),
        lax.psum(shares[5].astype(jnp.bfloat16), "seq").astype(jnp.float32),
        lax.psum(shares[6].astype(jnp.bfloat16), "seq").astype(jnp.float32),
        lax.psum(shares[7].astype(jnp.bfloat16), "seq").astype(jnp.float32),
        lax.psum(shares[8].astype(jnp.bfloat16), "seq").astype(jnp.float32),
    )
    return (
        block_out,
        grad_input,
        summed[0],
        summed[1],
        summed[2],
        summed[3],
        summed[4],
        summed[5],
        summed[6],
        summed[7],
        summed[8],
    )


MESH = pl.DeviceIdType.MESH
SHORT = SIDE_S * SIDE_S + 1
WIDE = 256
LOW = jnp.bfloat16
F32 = jnp.float32
NEVER = -1e30

PLANS = "xzxzyyyxyxxyyxy"
ORDER = (
    (),
    (),
    (),
    (),
    (),
    (2, 42),
    (12,),
    (52, 22),
    (),
    (),
    (),
    (32,),
    (62, 72),
    (),
    (43, 3),
    (13,),
    (53, 82),
    (23,),
    (33,),
    (92,),
    (73, 44),
    (),
    (),
    (4,),
    (54, 102, 24),
    (112, 63),
    (
        14, 93, 74, 45, 55, 83, 34, 122, 103, 64, 94, 84, 132, 152, 104, 142, 65, 5, 85, 25, 113,
        133, 123, 114, 15, 143, 75, 134, 46, 56, 124, 35, 115, 95, 153, 144, 105, 125, 66, 86,
        154, 145, 135, 116, 126, 155, 146,
    ),
)


def dot(left, right):
    return lax.dot_general(left, right, (((1,), (0,)), ((), ())), preferred_element_type=F32)


def dot_nt(left, right):
    return lax.dot_general(left, right, (((1,), (1,)), ((), ())), preferred_element_type=F32)


def dot_tn(left, right):
    return lax.dot_general(left, right, (((0,), (0,)), ((), ())), preferred_element_type=F32)


def rope_constants(rows):
    quarter = HD // 4
    freq = 10000.0 ** (-np.arange(quarter) / quarter)
    tables = []
    for side, length in ((SIDE_S, SIDE_S * SIDE_S + 1), (SIDE_L, SIDE_L * SIDE_L + 1)):
        place = np.arange(rows) - 1
        place = np.where((place >= 0) & (place < length - 1), place, 0)
        row = (place // side)[:, None] * freq
        col = (place % side)[:, None] * freq
        cosine = np.concatenate([np.cos(row), np.cos(row), np.cos(col), np.cos(col)], -1)
        sine = np.concatenate([-np.sin(row), np.sin(row), -np.sin(col), np.sin(col)], -1)
        tables += [np.concatenate([cosine, cosine], -1), np.concatenate([sine, sine], -1)]
    return np.stack(tables).astype(np.float32)


def swap_quarters(values):
    lane = lax.broadcasted_iota(jnp.int32, values.shape, 1)
    first = (lane % (HD // 2)) < HD // 4
    return jnp.where(
        first, pltpu.roll(values, 2 * HD - HD // 4, 1), pltpu.roll(values, HD // 4, 1)
    )


def fused(geo, *refs):
    rows_here, width, hidden_all = geo
    (
        lens, gain_a, gain_f, x_hbm, cot_hbm, tab_hbm,
        wq, wk, wv, wo, wg, wu, wd,
        bo_hbm, gi_hbm, fa_hbm, fd_hbm, fq_hbm, gain_hbm,
        x4, cot4, tab, wqkv_v, wo_v, wg_v, wu_v, wd_v,
        nrm, nrm_t, qkv, chance, mix_own, mix_in, mix, mix_t,
        mid, nf, nf_t, hid, hid_t, gg, gu, big,
        gnf_out, gnf_in, sb, rb, bo, bo_in, gb, gmx, ds_s, gqkv, sb2, rb2, gi, gi_in,
        gain_s, gain_x, gain_y, gain_z, gain_f_z, gain_c,
        pa, r1a, r2a, r3a, fa, pd, r1d, r2d, r3d, fd, pq, r1q, r2q, r3q, fq,
        sem_w, sem_in_s, sem_in_r, sem_core_s, sem_core_r, sem_gain_s, sem_gain_r, sem_o,
        sa_s, sa_r, sd_s, sd_r, sq_s, sq_r,
    ) = refs
    s = lax.axis_index("seq")
    i = lax.axis_index("items")
    y, c = s // 2, s % 2
    z, x = i // 2, i % 2
    rows = 4 * rows_here
    half = width // 2
    ff = hidden_all // 2
    pairs = half // 128
    step = rows_here
    fine = 32
    per = rows_here // step
    blocks = [(r0, min(256, rows - r0)) for r0 in range(0, rows, 256)]

    def device(y_to, c_to, z_to, x_to):
        return (y_to * 2 + c_to, z_to * 2 + x_to)

    sibling = device(y, 1 - c, z, x)
    y_dev = device(1 - y, c, z, x)
    x_dev = device(y, c, z, 1 - x)
    z_hi, z_lo = z // 2, z % 2
    near_z = device(y, c, z + 1 - 2 * z_lo, x)
    far_z = device(y, c, z + 2 - 4 * z_hi, x)

    started = []

    def send(src, dst, s_sem, r_sem, to):
        return pltpu.make_async_remote_copy(
            src_ref=src, dst_ref=dst, send_sem=s_sem, recv_sem=r_sem,
            device_id=to, device_id_type=MESH,
        )

    def weight_copies():
        copies = [pltpu.make_async_copy(tab_hbm, tab, sem_w.at[0])]
        mine = pl.ds(pl.multiple_of(c * half, half), half)
        for t, w in enumerate((wq, wk, wv)):
            copies.append(
                pltpu.make_async_copy(
                    w.at[:, mine], wqkv_v.at[:, pl.ds(t * half, half)], sem_w.at[1 + t]
                )
            )
        copies.append(pltpu.make_async_copy(wo, wo_v, sem_w.at[4]))
        for b in range(ff // 128):
            far = pl.ds(pl.multiple_of(256 * b + 128 * c, 128), 128)
            near = pl.ds(128 * b, 128)
            copies.append(pltpu.make_async_copy(wg.at[:, far], wg_v.at[:, near], sem_w.at[5 + 3 * b]))
            copies.append(pltpu.make_async_copy(wu.at[:, far], wu_v.at[:, near], sem_w.at[6 + 3 * b]))
            copies.append(pltpu.make_async_copy(wd.at[far], wd_v.at[near], sem_w.at[7 + 3 * b]))
        return copies

    weights = weight_copies()
    own_x = pltpu.make_async_copy(x_hbm.at[y], x4.at[s], sem_o.at[0])
    own_cot = pltpu.make_async_copy(cot_hbm.at[y], cot4.at[s], sem_o.at[1])
    own_x.start()
    for copy in weights[:4]:
        copy.start()

    barrier = pltpu.get_barrier_semaphore()
    for to in (sibling, y_dev, x_dev, near_z, far_z):
        pl.semaphore_signal(barrier, inc=1, device_id=to, device_id_type=MESH)
    pl.semaphore_wait(barrier, 5)

    s_y = (1 - y) * 2 + c
    across_x = send(x_hbm.at[1 - y], x4.at[s], sem_in_s.at[0], sem_in_r.at[0], y_dev)
    beside_x = send(x_hbm.at[y], x4.at[s], sem_in_s.at[1], sem_in_r.at[1], sibling)
    across_x.start()
    beside_x.start()
    across_c = send(cot_hbm.at[1 - y], cot4.at[s], sem_in_s.at[2], sem_in_r.at[2], y_dev)
    beside_c = send(cot_hbm.at[y], cot4.at[s], sem_in_s.at[3], sem_in_r.at[3], sibling)
    own_cot.start()
    for copy in weights[4:]:
        copy.start()
    relay_x = send(x4.at[s_y], x4.at[s_y], sem_in_s.at[4], sem_in_r.at[4], sibling)
    relay_c = send(cot4.at[s_y], cot4.at[s_y], sem_in_s.at[5], sem_in_r.at[5], sibling)

    length = lens[y]

    def norm_rows(piece):
        def one(b, carry):
            here = pl.ds(pl.multiple_of(b * step, step), step)
            values = x4[piece, here, :].astype(F32)
            scale = lax.rsqrt(jnp.mean(values * values, -1, keepdims=True) + epsilon)
            there = pl.ds(pl.multiple_of(piece * rows_here + b * step, step), step)
            nrm[there, :] = (values * scale * gain_a[...]).astype(LOW)
            return carry

        lax.fori_loop(0, per, one, 0)

    def project_rows(part):
        base = pl.multiple_of(part * 2 * rows_here, 32)
        here = pl.ds(base, 2 * rows_here)
        cosine = jnp.where(length == LONG, tab[2, here, :], tab[0, here, :])
        sine = jnp.where(length == LONG, tab[3, here, :], tab[1, here, :])
        for t in range(3):
            product = dot(nrm[here, :], wqkv_v[:, t * half : (t + 1) * half])
            for p in range(pairs):
                lanes = product[:, 128 * p : 128 * (p + 1)]
                if t < 2:
                    lanes = lanes * cosine + swap_quarters(lanes) * sine
                if t == 0:
                    lanes = lanes.astype(LOW).astype(F32) * HD ** (-0.5)
                qkv[t, here, 128 * p : 128 * (p + 1)] = lanes.astype(LOW)

    own_x.wait()
    norm_rows(s)
    beside_x.wait_recv()
    norm_rows(2 * y + 1 - c)
    for copy in weights[:4]:
        copy.wait()
    project_rows(y)
    across_x.wait_recv()
    relay_x.start()
    across_c.start()
    beside_c.start()
    norm_rows(s_y)
    relay_x.wait_recv()
    norm_rows(2 * (1 - y) + 1 - c)
    project_rows(1 - y)

    lane = lax.broadcasted_iota(jnp.int32, (1, 128), 1)
    left_head = lane < HD
    masks = [(lane // HD == n).astype(F32).astype(LOW) for n in range(2)]

    def mix_copy(pair):
        return send(
            mix_own.at[pair], mix_in.at[pair], sem_core_s.at[pair], sem_core_r.at[pair], sibling
        )

    tiles = blocks
    key = lax.broadcasted_iota(jnp.int32, (1, rows), 1)
    bias = jnp.where(key < length, 0.0, NEVER)

    def stacked(first, second):
        return jnp.concatenate([first, second], 0)

    def attend(pair, carry):
        lanes = pl.ds(pl.multiple_of(pair * 128, 128), 128)
        parts = []
        for k0, kb in tiles:
            query = qkv[0, k0:, lanes]
            part = dot_nt(stacked(query * masks[0], query * masks[1]), qkv[1, k0 : k0 + kb, lanes])
            parts.append(part + bias[:, k0 : k0 + kb] if k0 + kb > SHORT else part)
        for n in range(2):
            for r0, rb in blocks:
                scores = []
                for (k0, kb), part in zip(tiles, parts):
                    if k0 <= r0:
                        base = n * (rows - k0) + r0 - k0
                        here = part[base : base + rb]
                        if k0 == r0:
                            row = lax.broadcasted_iota(jnp.int32, here.shape, 0)
                            col = lax.broadcasted_iota(jnp.int32, here.shape, 1)
                            here = jnp.where(col <= row, here, NEVER)
                        scores.append((k0, kb, here))
                top = functools.reduce(jnp.maximum, [jnp.max(p, -1, keepdims=True) for _, _, p in scores])
                expo = [(k0, kb, jnp.exp(p - top)) for k0, kb, p in scores]
                inverse = 1.0 / sum(jnp.sum(p, -1, keepdims=True) for _, _, p in expo)
                for k0, kb, p in expo:
                    chance[pair * 2 + n, r0 : r0 + rb, k0 : k0 + kb] = (p * inverse).astype(LOW)
        outs = []
        for k0, kb in tiles:
            at = slice(k0, k0 + kb)
            low = stacked(chance[pair * 2, k0:, at], chance[pair * 2 + 1, k0:, at])
            outs.append(dot(low, qkv[2, at, lanes]))
        for r0, rb in blocks:
            both = []
            for n in range(2):
                at = [n * (rows - k0) + r0 - k0 for k0, _ in tiles if k0 <= r0]
                both.append(sum(out[b : b + rb] for b, out in zip(at, outs)))
            mix_own[pair, r0 : r0 + rb, :] = jnp.where(left_head, both[0], both[1]).astype(LOW)
        mix_copy(pair).start()
        return carry

    lax.fori_loop(0, pairs, attend, 0)

    across_c.wait_recv()
    relay_c.start()

    def turn_rows(src, dst):
        def one(b, carry):
            here = pl.ds(pl.multiple_of(b * 128, 128), 128)
            dst[:, here] = src[here, :].T
            return carry

        lax.fori_loop(0, rows // 128, one, 0)

    def place_mix(src, at):
        def one(p, carry):
            mix[:, pl.ds(pl.multiple_of(at * half + p * 128, 128), 128)] = src[p]
            return carry

        lax.fori_loop(0, pairs, one, 0)

    place_mix(mix_own, c)
    turn_rows(nrm, nrm_t)
    for p in range(pairs):
        mix_copy(p).wait_recv()
    place_mix(mix_in, 1 - c)

    weights[4].wait()

    def chunk(n, wide=WIDE):
        return pl.ds(pl.multiple_of(n * wide, wide), wide)

    def out_project(n, carry):
        mid[:, chunk(n)] = (
            dot(mix[...], wo_v[:, chunk(n)])
            + x4[:, :, chunk(n)].reshape(rows, WIDE).astype(F32)
        )
        return carry

    lax.fori_loop(0, width // WIDE, out_project, 0)

    def second_norm(b, carry):
        here = pl.ds(pl.multiple_of(b * step, step), step)
        values = mid[here, :]
        scale = lax.rsqrt(jnp.mean(values * values, -1, keepdims=True) + epsilon)
        nf[here, :] = (values * scale * gain_f[...]).astype(LOW)
        return carry

    lax.fori_loop(0, rows // step, second_norm, 0)
    turn_rows(nf, nf_t)
    for copy in weights[5:]:
        copy.wait()
    own_cot.wait()
    beside_c.wait_recv()
    relay_c.wait_recv()

    class Group:
        def __init__(self, parts, r1, r2, r3, fin, s_sem, r_sem):
            self.parts, self.r1, self.r2, self.r3, self.fin = parts, r1, r2, r3, fin
            self.s_sem, self.r_sem = s_sem, r_sem

        def copy(self, k, n, src, dst, to):
            return send(src, dst, self.s_sem.at[k, n], self.r_sem.at[k, n], to)

        def step1(self, k):
            self.hop(k, 0).start()

        def to_core(self, k):
            return self.copy(k, 5, self.fin.at[k, c], self.fin.at[k, c], sibling)

        def finish(self, k, own, new):
            for h in range(2):
                total = self.r1[own + (h,)].astype(F32) + self.r3[k, new + h].astype(F32)
                self.fin[k, c, h] = total.astype(LOW)
            self.to_core(k).start()

        def end(self, k):
            self.to_core(k).wait_recv()

        def sent(self, k):
            for n in range(self.hops):
                self.hop(k, n).wait_send()
            self.to_core(k).wait_send()

    def add(ref, at, other, of):
        ref[at] = (ref[at].astype(F32) + other[of].astype(F32)).astype(LOW)

    class XZY(Group):
        hops = 4

        def hop(self, k, n):
            r1, r2, r3 = self.r1, self.r2, self.r3
            if n == 0:
                return self.copy(k, n, self.parts.at[k, :, :, 1 - x], r1.at[k], x_dev)
            if n == 1:
                return self.copy(k, n, r1.at[k, :, 1 - z_lo], r2.at[k], near_z)
            if n == 2:
                return self.copy(k, n, r1.at[k, 1 - z_hi, z_lo], r3.at[k, pl.ds(0, 2)], far_z)
            return self.copy(k, n, r1.at[k, z_hi, z_lo], r3.at[k, pl.ds(2, 2)], y_dev)

        def step2(self, k):
            self.hop(k, 0).wait_recv()
            for lo in (1 - z_lo, z_lo):
                for hi in range(2):
                    for h in range(2):
                        add(self.r1, (k, hi, lo, h), self.parts, (k, hi, lo, x, h))
                if lo is not z_lo:
                    self.hop(k, 1).start()

        def step3(self, k):
            self.hop(k, 1).wait_recv()
            for hi in (1 - z_hi, z_hi):
                for h in range(2):
                    add(self.r1, (k, hi, z_lo, h), self.r2, (k, hi, h))
                if hi is not z_hi:
                    self.hop(k, 2).start()

        def step4(self, k):
            self.hop(k, 2).wait_recv()
            for h in range(2):
                add(self.r1, (k, z_hi, z_lo, h), self.r3, (k, h))
            self.hop(k, 3).start()

        def step5(self, k):
            self.hop(k, 3).wait_recv()
            self.finish(k, (k, z_hi, z_lo), 2)

    class ZXY(Group):
        hops = 4

        def hop(self, k, n):
            r1, r2, r3 = self.r1, self.r2, self.r3
            if n == 0:
                return self.copy(k, n, self.parts.at[k, :, 1 - z_lo], r1.at[k], near_z)
            if n == 1:
                return self.copy(k, n, r1.at[k, 1 - z_hi], r2.at[k], far_z)
            if n == 2:
                return self.copy(k, n, r1.at[k, z_hi, 1 - x], r3.at[k, pl.ds(0, 2)], x_dev)
            return self.copy(k, n, r1.at[k, z_hi, x], r3.at[k, pl.ds(2, 2)], y_dev)

        def step2(self, k):
            self.hop(k, 0).wait_recv()
            for hi in (1 - z_hi, z_hi):
                for xx in range(2):
                    for h in range(2):
                        add(self.r1, (k, hi, xx, h), self.parts, (k, hi, z_lo, xx, h))
                if hi is not z_hi:
                    self.hop(k, 1).start()

        def step3(self, k):
            self.hop(k, 1).wait_recv()
            for xx in (1 - x, x):
                for h in range(2):
                    add(self.r1, (k, z_hi, xx, h), self.r2, (k, xx, h))
                if xx is not x:
                    self.hop(k, 2).start()

        def step4(self, k):
            self.hop(k, 2).wait_recv()
            for h in range(2):
                add(self.r1, (k, z_hi, x, h), self.r3, (k, h))
            self.hop(k, 3).start()

        def step5(self, k):
            self.hop(k, 3).wait_recv()
            self.finish(k, (k, z_hi, x), 2)

    class YXZ(Group):
        hops = 5

        def hop(self, k, n):
            r1, r2, r3 = self.r1, self.r2, self.r3
            if n == 0:
                return self.copy(k, n, self.parts.at[k, :, :, :, 1 - y], r1.at[k], y_dev)
            if n == 1:
                return self.copy(k, n, r1.at[k, :, :, 1 - x], r2.at[k], x_dev)
            if n == 2:
                return self.copy(k, n, r2.at[k, :, 1 - z_lo], r3.at[k, pl.ds(0, 2)], near_z)
            if n == 3:
                return self.copy(k, n, r2.at[k, 1 - z_hi, z_lo], r3.at[k, 2], far_z)
            return self.copy(k, n, self.fin.at[k, c, y], self.fin.at[k, c, y], y_dev)

        def beside(self, k, n):
            at = self.fin.at[k, c, y] if n == 0 else self.fin.at[k, c, 1 - y]
            return self.copy(k, 5 + n, at, at, sibling)

        def step2(self, k):
            self.hop(k, 0).wait_recv()
            for xx in (1 - x, x):
                for hi in range(2):
                    for lo in range(2):
                        add(self.r1, (k, hi, lo, xx), self.parts, (k, hi, lo, xx, y))
                if xx is not x:
                    self.hop(k, 1).start()

        def step3(self, k):
            self.hop(k, 1).wait_recv()
            for lo in (1 - z_lo, z_lo):
                for hi in range(2):
                    add(self.r2, (k, hi, lo), self.r1, (k, hi, lo, x))
                if lo is not z_lo:
                    self.hop(k, 2).start()

        def step4(self, k):
            self.hop(k, 2).wait_recv()
            for hi in (1 - z_hi, z_hi):
                add(self.r2, (k, hi, z_lo), self.r3, (k, hi))
                if hi is not z_hi:
                    self.hop(k, 3).start()

        def step5(self, k):
            self.hop(k, 3).wait_recv()
            total = self.r2[k, z_hi, z_lo].astype(F32) + self.r3[k, 2].astype(F32)
            self.fin[k, c, y] = total.astype(LOW)
            self.hop(k, 4).start()
            self.beside(k, 0).start()

        def step6(self, k):
            self.hop(k, 4).wait_recv()
            self.beside(k, 1).start()

        def end(self, k):
            for n in range(2):
                self.beside(k, n).wait_recv()

        def sent(self, k):
            for n in range(self.hops):
                self.hop(k, n).wait_send()
            for n in range(2):
                self.beside(k, n).wait_send()

    class Gains:
        def hop(self, k, n):
            src = (gain_s, gain_x, gain_y, gain_z, gain_s)[n]
            dst = (gain_x, gain_y, gain_z, gain_f_z, gain_c)[n]
            to = (x_dev, y_dev, near_z, far_z, sibling)[n]
            return send(src, dst, sem_gain_s.at[n], sem_gain_r.at[n], to)

        def step1(self, k):
            self.hop(k, 0).start()

        def step2(self, k):
            self.hop(k, 0).wait()
            gain_x[...] = gain_s[...] + gain_x[...]
            self.hop(k, 1).start()

        def step3(self, k):
            self.hop(k, 1).wait()
            gain_y[...] = gain_x[...] + gain_y[...]
            self.hop(k, 2).start()

        def step4(self, k):
            self.hop(k, 2).wait()
            gain_z[...] = gain_y[...] + gain_z[...]
            self.hop(k, 3).start()

        def step5(self, k):
            self.hop(k, 3).wait()
            gain_s[...] = gain_z[...] + gain_f_z[...]
            self.hop(k, 4).start()

        def end(self, k):
            self.hop(k, 4).wait()
            top = lax.broadcasted_iota(jnp.int32, gain_s.shape, 0) == 0
            total = gain_s[...] + jnp.where(top, gain_c[...], 0.0)
            gain_c[...] = pltpu.roll(total, lax.rem(8 - i, 8) * (width // 8), 1)

        def sent(self, k):
            pass

    buffers_a = (pa, r1a, r2a, r3a, fa, sa_s, sa_r)
    buffers_d = (pd, r1d, r2d, r3d, fd, sd_s, sd_r)
    buffers_q = (pq, r1q, r2q, r3q, fq, sq_s, sq_r)
    kinds = {"x": XZY, "y": YXZ, "z": ZXY}
    chunks = [(kinds[kind](*buffers_a), n) for n, kind in enumerate(PLANS[:8])]
    chunks += [(kinds[kind](*buffers_d), n) for n, kind in enumerate(PLANS[8:11])]
    chunks += [(kinds[kind](*buffers_q), n) for n, kind in enumerate(PLANS[11:])]
    chunks += [(Gains(), 0)]
    slots = iter(ORDER)

    def first(chunk):
        group, k = chunks[chunk]
        group.step1(k)

    def turn():
        for code in next(slots):
            group, k = chunks[code // 10]
            getattr(group, f"step{code % 10}")(k)

    chunks_f = ff // WIDE
    chunks_w = width // WIDE

    def feed(n, carry):
        at = chunk(n)
        big[:, 0:WIDE] = dot(nf[...], wg_v[:, at])
        big[:, WIDE : 2 * WIDE] = dot(nf[...], wu_v[:, at])
        big[:, 2 * WIDE : 3 * WIDE] = dot_nt(cot4[...].reshape(rows, width), wd_v[at, :])

        def one(b, inner):
            here = pl.ds(pl.multiple_of(b * fine, fine), fine)
            gate = big[here, 0:WIDE]
            up = big[here, WIDE : 2 * WIDE]
            back = big[here, 2 * WIDE : 3 * WIDE]
            sigma = 0.5 * jnp.tanh(0.5 * gate) + 0.5
            silu = gate * sigma
            hid[here, at] = (silu * up).astype(LOW)
            gg[here, at] = (back * up * (sigma + silu * (1.0 - sigma))).astype(LOW)
            gu[here, at] = (back * silu).astype(LOW)
            return inner

        lax.fori_loop(0, rows // fine, one, 0, unroll=5)
        shape = pa.shape[1:]
        pa[n] = dot(nf_t[...], gg[:, at]).reshape(shape).astype(LOW)
        first(n)
        pa[n + chunks_f] = dot(nf_t[...], gu[:, at]).reshape(shape).astype(LOW)
        first(n + chunks_f)
        hid_t[at, :] = hid[:, at].T
        return carry

    for n in range(chunks_f):
        turn()
        feed(n, 0)
    turn()

    def gnf_copy(n):
        return send(
            gnf_out.at[n], gnf_in.at[n], sem_core_s.at[pairs + n], sem_core_r.at[pairs + n], sibling
        )

    def back_ffn(n, carry):
        partial = dot_nt(gg[...], wg_v[chunk(n), :]) + dot_nt(gu[...], wu_v[chunk(n), :])
        big[:, chunk(n)] = partial
        gnf_out[n] = partial.astype(LOW)
        gnf_copy(n).start()
        return carry

    for n in range(chunks_w):
        back_ffn(n, 0)
        turn()

    def down(n, carry):
        big[:, chunk(n + chunks_w)] = dot(hid[...], wd_v[:, chunk(n)])
        return carry

    lax.fori_loop(0, chunks_w, down, 0)
    n_core = pairs + chunks_w
    bo_copy = send(sb, rb, sem_core_s.at[n_core], sem_core_r.at[n_core], sibling)
    far = slice(width, 2 * width)

    def for_rows(core, fn):
        for yy in range(2):
            def one(b, carry, yy=yy):
                base = pl.multiple_of((2 * yy + core) * rows_here + b * step, step)
                fn(yy, b, pl.ds(base, step), pl.ds(pl.multiple_of(b * step, step), step))
                return carry

            lax.fori_loop(0, per, one, 0)

    def pack_bo(yy, b, here, there):
        sb[yy, there, :] = big[here, far].astype(LOW)

    for_rows(1 - c, pack_bo)
    bo_copy.start()

    for n in range(chunks_w):
        turn()
        at = slice(n * WIDE, (n + 1) * WIDE)
        pd[n] = (
            dot(hid_t[...], cot4[:, :, at].reshape(rows, WIDE)).reshape(pd.shape[1:]).astype(LOW)
        )
        first(8 + n)

    turn()
    bo_copy.wait_recv()

    def finish_bo(yy, b, here, there):
        bo[yy, there, :] = (mid[here, :] + big[here, far] + rb[yy, there, :].astype(F32)).astype(LOW)

    for_rows(c, finish_bo)
    bo_across = send(bo.at[1 - y], bo_in, sem_in_s.at[6], sem_in_r.at[6], y_dev)
    bo_across.start()

    turn()
    for n in range(chunks_w):
        gnf_copy(n).wait_recv()

    def middle_back(b, total):
        here = pl.ds(pl.multiple_of(b * step, step), step)
        values = mid[here, :]
        grad = big[here, 0:width] + jnp.concatenate(
            [gnf_in[n, here, :].astype(F32) for n in range(chunks_w)], -1
        )
        scale = lax.rsqrt(jnp.mean(values * values, -1, keepdims=True) + epsilon)
        unit = values * scale
        total = total + (grad * unit).reshape(step // 8, 8, width).sum(0)
        scaled = grad * gain_f[...]
        inner = jnp.mean(scaled * unit, -1, keepdims=True)
        out = cot4[b // per, pl.ds(pl.multiple_of(lax.rem(b, per) * step, step), step), :].astype(F32)
        out = out + scale * (scaled - unit * inner)
        mid[here, :] = out
        gb[here, :] = out.astype(LOW)
        return total

    total_f = lax.fori_loop(0, rows // step, middle_back, jnp.zeros((8, width), F32))

    turn()
    turn_rows(mix, mix_t)
    mine = pl.ds(pl.multiple_of(c * half, half), half)
    pq[0] = dot(mix_t[...], gb[:, mine]).reshape(pq.shape[1:]).astype(LOW)
    first(11)
    gmx[...] = dot_nt(gb[...], wo_v[mine, :]).astype(LOW)

    def query_back(pair):
        lanes = slice(pair * 128, pair * 128 + 128)
        grads = []
        for k0, kb in tiles:
            grad = gmx[k0:, lanes]
            grads.append(
                dot_nt(stacked(grad * masks[0], grad * masks[1]), qkv[2, k0 : k0 + kb, lanes])
            )
        for n in range(2):
            for r0, rb in blocks:
                both = []
                for (k0, kb), grad in zip(tiles, grads):
                    if k0 <= r0:
                        base = n * (rows - k0) + r0 - k0
                        prob = chance[pair * 2 + n, r0 : r0 + rb, k0 : k0 + kb].astype(F32)
                        both.append((slice(k0, k0 + kb), prob, grad[base : base + rb] * prob))
                inner = sum(jnp.sum(each, -1, keepdims=True) for _, _, each in both)
                for at, prob, each in both:
                    ds_s[n, r0 : r0 + rb, at] = (each - prob * inner).astype(LOW)
        outs = []
        for k0, kb in tiles:
            at = slice(k0, k0 + kb)
            outs.append(dot(stacked(ds_s[0, k0:, at], ds_s[1, k0:, at]), qkv[1, at, lanes]))
        for r0, rb in blocks:
            both = []
            for n in range(2):
                at = [n * (rows - k0) + r0 - k0 for k0, _ in tiles if k0 <= r0]
                both.append(sum(out[b : b + rb] for b, out in zip(at, outs)))
            big[r0 : r0 + rb, 0:128] = jnp.where(left_head, both[0], both[1])

    def keys_back(pair):
        lanes = slice(pair * 128, pair * 128 + 128)

        def beside(first, second):
            return jnp.concatenate([first, second], 1)

        for k0, kb in tiles:
            at = slice(k0, k0 + kb)
            out = dot_tn(beside(ds_s[0, k0:, at], ds_s[1, k0:, at]), qkv[0, k0:, lanes])
            big[at, 128:256] = jnp.where(left_head, out[:kb], out[kb:])
            low = beside(chance[pair * 2, k0:, at], chance[pair * 2 + 1, k0:, at])
            out = dot_tn(low, gmx[k0:, lanes])
            big[at, 256:384] = jnp.where(left_head, out[:kb], out[kb:])

        def one(b, inner):
            here = pl.ds(pl.multiple_of(b * 64, 64), 64)
            cosine = jnp.where(length == LONG, tab[2, here, :], tab[0, here, :])
            sine = jnp.where(length == LONG, tab[3, here, :], tab[1, here, :])
            for t in range(3):
                values = big[here, 128 * t : 128 * (t + 1)]
                if t == 0:
                    values = values * HD ** (-0.5)
                if t < 2:
                    values = values * cosine - swap_quarters(values) * sine
                gqkv[here, t * half + pair * 128 : t * half + pair * 128 + 128] = values.astype(LOW)
            return inner

        lax.fori_loop(0, rows // 64, one, 0, unroll=5)

    for pair in range(pairs):
        turn()
        query_back(pair)
        turn()
        keys_back(pair)

    for t in range(3):
        turn()
        pq[1 + t] = (
            dot(nrm_t[...], gqkv[:, t * half : (t + 1) * half]).reshape(pq.shape[1:]).astype(LOW)
        )
        first(12 + t)

    turn()

    def back_attn(n, carry):
        big[:, chunk(n)] = dot_nt(gqkv[...], wqkv_v[chunk(n), :])
        return carry

    lax.fori_loop(0, chunks_w, back_attn, 0)
    turn()

    def pack_gi(yy, b, here, there):
        sb2[yy, there, :] = big[here, 0:width].astype(LOW)

    for_rows(1 - c, pack_gi)
    gi_copy = send(sb2, rb2, sem_core_s.at[n_core + 1], sem_core_r.at[n_core + 1], sibling)
    gi_copy.start()

    def gain_back(b, total):
        here = pl.ds(pl.multiple_of(b * step, step), step)
        values = x4[b // per, pl.ds(pl.multiple_of(lax.rem(b, per) * step, step), step), :].astype(F32)
        scale = lax.rsqrt(jnp.mean(values * values, -1, keepdims=True) + epsilon)
        return total + (big[here, 0:width] * (values * scale)).reshape(step // 8, 8, width).sum(0)

    total_a = lax.fori_loop(0, rows // step, gain_back, jnp.zeros((8, width), F32))
    row = lax.broadcasted_iota(jnp.int32, (8, width), 0)
    gain_s[...] = jnp.where(
        row == 0, jnp.sum(total_a, 0, keepdims=True), jnp.sum(total_f, 0, keepdims=True)
    )
    first(15)
    turn()
    gi_copy.wait_recv()

    def finish_gi(yy, b, here, there):
        values = x4[2 * yy + c, there, :].astype(F32)
        scale = lax.rsqrt(jnp.mean(values * values, -1, keepdims=True) + epsilon)
        unit = values * scale
        scaled = (big[here, 0:width] + rb2[yy, there, :].astype(F32)) * gain_a[...]
        inner = jnp.mean(scaled * unit, -1, keepdims=True)
        gi[yy, there, :] = (mid[here, :] + scale * (scaled - unit * inner)).astype(LOW)

    for_rows(c, finish_gi)
    gi_across = send(gi.at[1 - y], gi_in, sem_in_s.at[7], sem_in_r.at[7], y_dev)
    gi_across.start()

    turn()
    for group, k in chunks:
        group.end(k)

    outs = [
        pltpu.make_async_copy(fa, fa_hbm, sem_o.at[2]),
        pltpu.make_async_copy(fd, fd_hbm, sem_o.at[3]),
        pltpu.make_async_copy(fq, fq_hbm, sem_o.at[4]),
        pltpu.make_async_copy(gain_c, gain_hbm, sem_o.at[5]),
        pltpu.make_async_copy(bo.at[y], bo_hbm.at[y], sem_o.at[6]),
        pltpu.make_async_copy(gi.at[y], gi_hbm.at[y], sem_o.at[7]),
    ]
    for copy in outs:
        copy.start()
    bo_across.wait_recv()
    gi_across.wait_recv()
    outs += [
        pltpu.make_async_copy(bo_in, bo_hbm.at[1 - y], sem_o.at[8]),
        pltpu.make_async_copy(gi_in, gi_hbm.at[1 - y], sem_o.at[9]),
    ]
    for copy in outs[6:]:
        copy.start()
    for copy in outs:
        copy.wait()

    for copy in (across_x, beside_x, across_c, beside_c, relay_x, relay_c, bo_across, gi_across):
        copy.wait_send()
    for p in range(pairs):
        mix_copy(p).wait_send()
    for n in range(chunks_w):
        gnf_copy(n).wait_send()
    bo_copy.wait_send()
    gi_copy.wait_send()
    for group, k in chunks:
        group.sent(k)


def spread(chunks_f, share, *refs):
    fa_far, fd_far, fq_far, bo, gi, gains_far = refs[:6]
    outs, (fa, fd, fq, gains), stage, sem_in, sem_out = refs[6:17], refs[17:21], refs[21:28], *refs[28:]
    bo_out, gi_out, da, df = outs[0], outs[1], outs[2], outs[7]
    ends = outs[3:7] + outs[8:]
    dq, dk, dv, do, dg, du, dd = stage
    near = [
        pltpu.make_async_copy(a, b, sem_in.at[n])
        for n, (a, b) in enumerate(
            [(fa_far.at[:chunks_f], fa.at[:chunks_f]), (fa_far.at[chunks_f:], fa.at[chunks_f:])]
            + [(fd_far, fd), (fq_far, fq), (gains_far, gains), (bo, bo_out), (gi, gi_out)]
        )
    ]
    for copy in near:
        copy.start()
    done = [pltpu.make_async_copy(a, b, sem_out.at[n]) for n, (a, b) in enumerate(zip(stage, ends))]
    rows, half, deep = fa.shape[3], fq.shape[4], fd.shape[3]
    halves = [(core, h, slice(h * rows, (h + 1) * rows)) for core in range(2) for h in range(2)]

    for first, ref, copy in ((0, dg, 0), (chunks_f, du, 1)):
        near[copy].wait()
        for core, h, at in halves:
            for n in range(chunks_f):
                for b in range(WIDE // 128):
                    far = 256 * (n * (WIDE // 128) + b) + 128 * core
                    ref[at, far : far + 128] = fa[
                        n + first, core, h, :, 128 * b : 128 * (b + 1)
                    ].astype(F32)
        done[4 + copy].start()
    near[2].wait()
    for core, h, _ in halves:
        at = slice((2 * core + h) * deep, (2 * core + h + 1) * deep)
        for n in range(fd.shape[0]):
            dd[at, WIDE * n : WIDE * (n + 1)] = fd[n, core, h].astype(F32)
    done[6].start()
    near[3].wait()
    for n, (ref, end) in enumerate(((do, 3), (dq, 0), (dk, 1), (dv, 2))):
        for core, h, at in halves:
            ref[at, core * half : (core + 1) * half] = fq[n, core, h].astype(F32)
        done[end].start()
    near[4].wait()
    da[...] = gains[0, 0:share]
    df[...] = gains[1, 0:share]
    near[5].wait()
    near[6].wait()
    for copy in done:
        copy.wait()


def item_per_chip(
    block_in, lengths, gain_attn, w_query, w_key, w_value, w_out, gain_ffn, w_gate, w_up, w_down,
    cotangent,
):
    _, rows_here, width = block_in.shape
    hidden_all = w_gate.shape[1]
    rows = rows_here * lax.axis_size("seq")
    shares = lax.axis_size("items")
    half, ff = width // 2, hidden_all // 2
    pairs = half // 128
    chunks_f, chunks_w = ff // WIDE, width // WIDE
    thin, deep = width // shares // 2, ff // shares // 2
    tables = jnp.asarray(rope_constants(rows))
    any_ = pl.BlockSpec(memory_space=pl.ANY)
    vmem = pl.BlockSpec(memory_space=pltpu.VMEM)

    def group(n, r, w):
        return [
            pltpu.VMEM((n, 2, 2, 2, 2, r, w), LOW),
            pltpu.VMEM((n, 2, 2, 2, r, w), LOW),
            pltpu.VMEM((n, 2, 2, r, w), LOW),
            pltpu.VMEM((n, 4, r, w), LOW),
            pltpu.VMEM((n, 2, 2, r, w), LOW),
        ]

    def low(*shape):
        return pltpu.VMEM(shape, LOW)

    def full(*shape):
        return pltpu.VMEM(shape, F32)

    dma = pltpu.SemaphoreType.DMA
    scratch = [
        low(4, rows_here, width), low(4, rows_here, width), full(4, rows, 128),
        low(width, 3 * half), low(width, width), low(width, ff), low(width, ff), low(ff, width),
        low(rows, width), low(width, rows), low(3, rows, half), low(2 * pairs, rows, rows),
        low(pairs, rows, 128), low(pairs, rows, 128), low(rows, width), low(width, rows),
        full(rows, width), low(rows, width), low(width, rows), low(rows, ff), low(ff, rows),
        low(rows, ff), low(rows, ff), full(rows, 2 * width),
        low(chunks_w, rows, WIDE), low(chunks_w, rows, WIDE),
        low(2, rows_here, width), low(2, rows_here, width),
        low(2, rows_here, width), low(rows_here, width),
        low(rows, width), low(rows, half), low(2, rows, rows), low(rows, 3 * half),
        low(2, rows_here, width), low(2, rows_here, width),
        low(2, rows_here, width), low(rows_here, width),
        full(8, width), full(8, width), full(8, width), full(8, width), full(8, width), full(8, width),
    ]
    scratch += group(2 * chunks_f, thin, WIDE) + group(chunks_w, deep, WIDE) + group(4, thin, half)
    scratch += [
        dma((5 + 3 * (ff // 128),)), dma((8,)), dma((8,)),
        dma((pairs + chunks_w + 2,)), dma((pairs + chunks_w + 2,)), dma((6,)), dma((6,)), dma((10,)),
        dma((2 * chunks_f, 8)), dma((2 * chunks_f, 8)), dma((chunks_w, 8)), dma((chunks_w, 8)),
        dma((4, 8)), dma((4, 8)),
    ]
    shape = jax.ShapeDtypeStruct
    bo, gi, fa, fd, fq, gains = pl.pallas_call(
        functools.partial(fused, (rows_here, width, hidden_all)),
        out_shape=(
            shape(block_in.shape, LOW), shape(block_in.shape, LOW),
            shape((2 * chunks_f, 2, 2, thin, WIDE), LOW), shape((chunks_w, 2, 2, deep, WIDE), LOW),
            shape((4, 2, 2, thin, half), LOW), shape((8, width), F32),
        ),
        in_specs=[pl.BlockSpec(memory_space=pltpu.SMEM), vmem, vmem] + [any_] * 10,
        out_specs=(any_,) * 6,
        scratch_shapes=scratch,
        compiler_params=pltpu.CompilerParams(
            collective_id=0, has_side_effects=True, vmem_limit_bytes=63 * 2**20
        ),
        name="block",
    )(
        lengths, gain_attn, gain_ffn, block_in, cotangent, tables,
        w_query, w_key, w_value, w_out, w_gate, w_up, w_down,
    )
    thick = (width // shares, width)
    made = (fa, fd, fq, bo, gi, gains)
    share = width // shares
    bo, gi, da, dq, dk, dv, do, df, dg, du, dd = pl.pallas_call(
        functools.partial(spread, chunks_f, share),
        out_shape=(
            shape(block_in.shape, LOW), shape(block_in.shape, LOW), shape((share,), F32),
            shape(thick, F32), shape(thick, F32), shape(thick, F32), shape(thick, F32),
            shape((share,), F32),
            shape((width // shares, hidden_all), F32), shape((width // shares, hidden_all), F32),
            shape((hidden_all // shares, width), F32),
        ),
        in_specs=[any_] * 6,
        out_specs=(vmem,) * 3 + (any_,) * 4 + (vmem,) + (any_,) * 3,
        scratch_shapes=[pltpu.VMEM(a.shape, a.dtype) for a in (fa, fd, fq, gains)]
        + [pltpu.VMEM(thick, F32)] * 4
        + [pltpu.VMEM((width // shares, hidden_all), F32)] * 2
        + [pltpu.VMEM((hidden_all // shares, width), F32), dma((7,)), dma((7,))],
        compiler_params=pltpu.CompilerParams(vmem_limit_bytes=60 * 2**20),
        name="spread",
    )(*made)
    return bo, gi, da, dq, dk, dv, do, df, dg, du, dd


def solution(mesh):
    fits = mesh.shape["seq"] == 4 and mesh.shape["items"] == 8
    return jax.shard_map(
        item_per_chip if fits else body,
        mesh=mesh,
        in_specs=(P("items", "seq", None), P("items")) + (P(),) * 9 + (P("items", "seq", None),),
        out_specs=(
            (P("items", "seq", None),) * 2
            + (P("items"),) + (P("items", None),) * 4
            + (P("items"),) + (P("items", None),) * 3
        ),
        check_vma=False,
    )
```

```python
import functools

import jax
import jax.numpy as jnp
import numpy as np
from jax import lax
from jax.experimental import pallas as pl
from jax.experimental.pallas import tpu as pltpu
from jax.sharding import PartitionSpec as P

HD = 64
SIDE_S = 16
SIDE_L = 24
LONG = 577


epsilon = 1e-05


def grid_places(lengths, rows):
    side = jnp.where(lengths == LONG, SIDE_L, SIDE_S).astype(jnp.int32)[:, None]
    place = rows[None, :] - 1
    valid = (place >= 0) & (rows[None, :] < lengths[:, None])
    place = jnp.where(valid, place, 0)
    return (place // side, place % side)


def rotary_tables(lengths, rows):
    grid_row, grid_col = grid_places(lengths, rows)
    quarter = HD // 4
    freq = 10000.0 ** (-jnp.arange(quarter, dtype=jnp.float32) / quarter)
    angle_row = grid_row[..., None].astype(jnp.float32) * freq
    angle_col = grid_col[..., None].astype(jnp.float32) * freq
    cosine = jnp.concatenate(
        [jnp.cos(angle_row), jnp.cos(angle_row), jnp.cos(angle_col), jnp.cos(angle_col)], -1
    )
    sine = jnp.concatenate(
        [jnp.sin(angle_row), jnp.sin(angle_row), jnp.sin(angle_col), jnp.sin(angle_col)], -1
    )
    return (cosine[:, :, None, :], sine[:, :, None, :])


def turn(values):
    quarter = HD // 4
    first = values[..., 0:quarter]
    second = values[..., quarter : 2 * quarter]
    third = values[..., 2 * quarter : 3 * quarter]
    fourth = values[..., 3 * quarter :]
    return jnp.concatenate([-second, first, -fourth, third], -1)


def project(left, right):
    return jnp.einsum("ird,de->ire", left, right, preferred_element_type=jnp.float32)


def back_project(grad, weight):
    return jnp.einsum("ire,de->ird", grad, weight, preferred_element_type=jnp.float32)


def weight_grad(left, right):
    return jnp.einsum("ird,ire->de", left, right, preferred_element_type=jnp.float32)


def norm_back(grad_normed, unit, scale, gain):
    scaled = grad_normed * gain
    return scale * (scaled - unit * jnp.mean(scaled * unit, -1, keepdims=True))


def body(
    block_in,
    lengths,
    gain_attn,
    w_query,
    w_key,
    w_value,
    w_out,
    gain_ffn,
    w_gate,
    w_up,
    w_down,
    cotangent,
):
    count, rows_here, width = block_in.shape
    heads = width // HD
    length_all = rows_here * lax.axis_size("seq")
    factor = HD ** (-0.5)
    query_rows = lax.axis_index("seq") * rows_here + jnp.arange(rows_here, dtype=jnp.int32)
    key_rows = jnp.arange(length_all, dtype=jnp.int32)
    cosine, sine = rotary_tables(lengths, query_rows)
    allowed = (key_rows[None, None, :] <= query_rows[None, :, None]) & (
        key_rows[None, None, :] < lengths[:, None, None]
    )

    def heads_of(array):
        return array.reshape(array.shape[0], array.shape[1], heads, HD)

    def attention_scores(query, keys_all):
        raw = (
            jnp.einsum(
                "irhe,iphe->ihrp", query, heads_of(keys_all), preferred_element_type=jnp.float32
            )
            * factor
        )
        return jnp.where(allowed[:, None], raw, -1e30)

    source = block_in.astype(jnp.float32)
    scale_attn = lax.rsqrt(jnp.mean(source * source, -1, keepdims=True) + epsilon)
    unit_attn = source * scale_attn
    normed = (unit_attn * gain_attn).astype(jnp.bfloat16)
    query_pre = heads_of(project(normed, w_query))
    keys_pre = heads_of(project(normed, w_key))
    query = (query_pre * cosine + turn(query_pre) * sine).astype(jnp.bfloat16)
    keys = (
        (keys_pre * cosine + turn(keys_pre) * sine)
        .astype(jnp.bfloat16)
        .reshape(count, rows_here, width)
    )
    values = project(normed, w_value).astype(jnp.bfloat16)
    keys_all, values_all = (
        lax.all_gather(keys, "seq", axis=1, tiled=True),
        lax.all_gather(values, "seq", axis=1, tiled=True),
    )
    scores = attention_scores(query, keys_all)
    top = jnp.max(scores, -1, keepdims=True)
    expo = jnp.exp(scores - top)
    summed = jnp.sum(expo, -1, keepdims=True)
    chance = expo / summed
    log_total = top + jnp.log(summed)
    mixed = (
        jnp.einsum(
            "ihrp,iphe->irhe",
            chance.astype(jnp.bfloat16),
            heads_of(values_all),
            preferred_element_type=jnp.float32,
        )
        .reshape(count, rows_here, width)
        .astype(jnp.bfloat16)
    )
    middle = source + project(mixed, w_out)
    scale_ffn = lax.rsqrt(jnp.mean(middle * middle, -1, keepdims=True) + epsilon)
    unit_ffn = middle * scale_ffn
    normed_ffn = (unit_ffn * gain_ffn).astype(jnp.bfloat16)
    gate = project(normed_ffn, w_gate)
    up = project(normed_ffn, w_up)
    sigma = jax.nn.sigmoid(gate)
    hidden = (gate * sigma * up).astype(jnp.bfloat16)
    block_out = (middle + project(hidden, w_down)).astype(jnp.bfloat16)
    incoming = cotangent.astype(jnp.float32)
    grad_w_down = weight_grad(hidden, cotangent)
    grad_hidden = back_project(cotangent, w_down)
    grad_gate = (grad_hidden * up * sigma * (1.0 + gate * (1.0 - sigma))).astype(jnp.bfloat16)
    grad_up = (grad_hidden * gate * sigma).astype(jnp.bfloat16)
    grad_w_gate = weight_grad(normed_ffn, grad_gate)
    grad_w_up = weight_grad(normed_ffn, grad_up)
    grad_normed_ffn = back_project(grad_gate, w_gate) + back_project(grad_up, w_up)
    grad_gain_ffn = jnp.sum(grad_normed_ffn * unit_ffn, axis=(0, 1))
    grad_middle = incoming + norm_back(grad_normed_ffn, unit_ffn, scale_ffn, gain_ffn)
    grad_branch = grad_middle.astype(jnp.bfloat16)
    grad_w_out = weight_grad(mixed, grad_branch)
    grad_mixed = heads_of(back_project(grad_branch, w_out)).astype(jnp.bfloat16)
    keys_back, values_back = (keys_all, values_all)
    chance_back = jnp.exp(attention_scores(query, keys_back) - log_total)
    grad_chance = jnp.einsum(
        "irhe,iphe->ihrp", grad_mixed, heads_of(values_back), preferred_element_type=jnp.float32
    )
    inner = jnp.sum(grad_chance * chance_back, -1, keepdims=True)
    grad_scores = (chance_back * (grad_chance - inner)).astype(jnp.bfloat16)
    grad_query = (
        jnp.einsum(
            "ihrp,iphe->irhe", grad_scores, heads_of(keys_back), preferred_element_type=jnp.float32
        )
        * factor
    )
    grad_values_sum = jnp.einsum(
        "ihrp,irhe->iphe",
        chance_back.astype(jnp.bfloat16),
        grad_mixed,
        preferred_element_type=jnp.float32,
    )
    grad_keys_sum = (
        jnp.einsum("ihrp,irhe->iphe", grad_scores, query, preferred_element_type=jnp.float32)
        * factor
    )
    grad_keys, grad_values = (
        lax.psum_scatter(
            grad_keys_sum.reshape(count, length_all, width).astype(jnp.bfloat16),
            "seq",
            scatter_dimension=1,
            tiled=True,
        ).astype(jnp.float32),
        lax.psum_scatter(
            grad_values_sum.reshape(count, length_all, width).astype(jnp.bfloat16),
            "seq",
            scatter_dimension=1,
            tiled=True,
        ).astype(jnp.float32),
    )
    grad_query_pre = (
        (grad_query * cosine - turn(grad_query * sine))
        .reshape(count, rows_here, width)
        .astype(jnp.bfloat16)
    )
    grad_keys_heads = heads_of(grad_keys)
    grad_keys_pre = (
        (grad_keys_heads * cosine - turn(grad_keys_heads * sine))
        .reshape(count, rows_here, width)
        .astype(jnp.bfloat16)
    )
    grad_values_pre = grad_values.astype(jnp.bfloat16)
    grad_w_query = weight_grad(normed, grad_query_pre)
    grad_w_key = weight_grad(normed, grad_keys_pre)
    grad_w_value = weight_grad(normed, grad_values_pre)
    grad_normed = (
        back_project(grad_query_pre, w_query)
        + back_project(grad_keys_pre, w_key)
        + back_project(grad_values_pre, w_value)
    )
    grad_gain_attn = jnp.sum(grad_normed * unit_attn, axis=(0, 1))
    grad_input = (grad_middle + norm_back(grad_normed, unit_attn, scale_attn, gain_attn)).astype(
        jnp.bfloat16
    )
    shares = (
        lax.psum_scatter(
            grad_gain_attn.astype(jnp.bfloat16), "items", scatter_dimension=0, tiled=True
        ).astype(jnp.float32),
        lax.psum_scatter(
            grad_w_query.astype(jnp.bfloat16), "items", scatter_dimension=0, tiled=True
        ).astype(jnp.float32),
        lax.psum_scatter(
            grad_w_key.astype(jnp.bfloat16), "items", scatter_dimension=0, tiled=True
        ).astype(jnp.float32),
        lax.psum_scatter(
            grad_w_value.astype(jnp.bfloat16), "items", scatter_dimension=0, tiled=True
        ).astype(jnp.float32),
        lax.psum_scatter(
            grad_w_out.astype(jnp.bfloat16), "items", scatter_dimension=0, tiled=True
        ).astype(jnp.float32),
        lax.psum_scatter(
            grad_gain_ffn.astype(jnp.bfloat16), "items", scatter_dimension=0, tiled=True
        ).astype(jnp.float32),
        lax.psum_scatter(
            grad_w_gate.astype(jnp.bfloat16), "items", scatter_dimension=0, tiled=True
        ).astype(jnp.float32),
        lax.psum_scatter(
            grad_w_up.astype(jnp.bfloat16), "items", scatter_dimension=0, tiled=True
        ).astype(jnp.float32),
        lax.psum_scatter(
            grad_w_down.astype(jnp.bfloat16), "items", scatter_dimension=0, tiled=True
        ).astype(jnp.float32),
    )
    summed = (
        lax.psum(shares[0].astype(jnp.bfloat16), "seq").astype(jnp.float32),
        lax.psum(shares[1].astype(jnp.bfloat16), "seq").astype(jnp.float32),
        lax.psum(shares[2].astype(jnp.bfloat16), "seq").astype(jnp.float32),
        lax.psum(shares[3].astype(jnp.bfloat16), "seq").astype(jnp.float32),
        lax.psum(shares[4].astype(jnp.bfloat16), "seq").astype(jnp.float32),
        lax.psum(shares[5].astype(jnp.bfloat16), "seq").astype(jnp.float32),
        lax.psum(shares[6].astype(jnp.bfloat16), "seq").astype(jnp.float32),
        lax.psum(shares[7].astype(jnp.bfloat16), "seq").astype(jnp.float32),
        lax.psum(shares[8].astype(jnp.bfloat16), "seq").astype(jnp.float32),
    )
    return (
        block_out,
        grad_input,
        summed[0],
        summed[1],
        summed[2],
        summed[3],
        summed[4],
        summed[5],
        summed[6],
        summed[7],
        summed[8],
    )


MESH = pl.DeviceIdType.MESH
SHORT = SIDE_S * SIDE_S + 1
WIDE = 256
LOW = jnp.bfloat16
F32 = jnp.float32
NEVER = -1e30

PLANS = "xyzyzxyyzxxyyxy"
ORDER = (
    (),
    (),
    (),
    (),
    (),
    (2, 42),
    (12,),
    (),
    (52, 22),
    (62,),
    (),
    (13,),
    (3,),
    (43,),
    (32,),
    (63, 53),
    (72,),
    (23,),
    (92,),
    (),
    (),
    (),
    (82,),
    (),
    (14, 102, 4, 44, 64, 33, 112, 54),
    (),
    (
        73, 24, 93, 122, 83, 15, 132, 103, 65, 34, 74, 113, 142, 152, 5, 45, 94, 55, 123, 84, 133,
        104, 35, 75, 143, 114, 25, 16, 66, 124, 153, 95, 134, 85, 144, 105, 115, 36, 76, 125, 154,
        135, 145, 116, 126, 155, 146,
    ),
)


def dot(left, right):
    return lax.dot_general(left, right, (((1,), (0,)), ((), ())), preferred_element_type=F32)


def dot_nt(left, right):
    return lax.dot_general(left, right, (((1,), (1,)), ((), ())), preferred_element_type=F32)


def dot_tn(left, right):
    return lax.dot_general(left, right, (((0,), (0,)), ((), ())), preferred_element_type=F32)


def rope_constants(rows):
    quarter = HD // 4
    freq = 10000.0 ** (-np.arange(quarter) / quarter)
    tables = []
    for side, length in ((SIDE_S, SIDE_S * SIDE_S + 1), (SIDE_L, SIDE_L * SIDE_L + 1)):
        place = np.arange(rows) - 1
        place = np.where((place >= 0) & (place < length - 1), place, 0)
        row = (place // side)[:, None] * freq
        col = (place % side)[:, None] * freq
        cosine = np.concatenate([np.cos(row), np.cos(row), np.cos(col), np.cos(col)], -1)
        sine = np.concatenate([-np.sin(row), np.sin(row), -np.sin(col), np.sin(col)], -1)
        tables += [np.concatenate([cosine, cosine], -1), np.concatenate([sine, sine], -1)]
    return np.stack(tables).astype(np.float32)


def swap_quarters(values):
    lane = lax.broadcasted_iota(jnp.int32, values.shape, 1)
    first = (lane % (HD // 2)) < HD // 4
    return jnp.where(
        first, pltpu.roll(values, 2 * HD - HD // 4, 1), pltpu.roll(values, HD // 4, 1)
    )


def fused(geo, *refs):
    rows_here, width, hidden_all = geo
    (
        lens, gain_a, gain_f, x_hbm, cot_hbm, tab_hbm,
        wq, wk, wv, wo, wg, wu, wd,
        bo_hbm, gi_hbm, fa_hbm, fd_hbm, fq_hbm, gain_hbm,
        x4, cot4, tab, wqkv_v, wo_v, wg_v, wu_v, wd_v,
        nrm, nrm_t, qkv, chance, mix_own, mix_in, mix, mix_t,
        mid, nf, nf_t, hid, hid_t, gg, gu, big,
        gnf_out, gnf_in, sb, rb, bo, bo_in, gb, gmx, ds_s, gqkv, sb2, rb2, gi, gi_in,
        gain_s, gain_x, gain_y, gain_z, gain_f_z, gain_c,
        pa, r1a, r2a, r3a, fa, pd, r1d, r2d, r3d, fd, pq, r1q, r2q, r3q, fq,
        sem_w, sem_in_s, sem_in_r, sem_core_s, sem_core_r, sem_gain_s, sem_gain_r, sem_o,
        sa_s, sa_r, sd_s, sd_r, sq_s, sq_r,
    ) = refs
    s = lax.axis_index("seq")
    i = lax.axis_index("items")
    y, c = s // 2, s % 2
    z, x = i // 2, i % 2
    rows = 4 * rows_here
    half = width // 2
    ff = hidden_all // 2
    pairs = half // 128
    step = rows_here
    fine = 32
    per = rows_here // step
    blocks = [(r0, min(256, rows - r0)) for r0 in range(0, rows, 256)]

    def device(y_to, c_to, z_to, x_to):
        return (y_to * 2 + c_to, z_to * 2 + x_to)

    sibling = device(y, 1 - c, z, x)
    y_dev = device(1 - y, c, z, x)
    x_dev = device(y, c, z, 1 - x)
    z_hi, z_lo = z // 2, z % 2
    near_z = device(y, c, z + 1 - 2 * z_lo, x)
    far_z = device(y, c, z + 2 - 4 * z_hi, x)

    started = []

    def send(src, dst, s_sem, r_sem, to):
        return pltpu.make_async_remote_copy(
            src_ref=src, dst_ref=dst, send_sem=s_sem, recv_sem=r_sem,
            device_id=to, device_id_type=MESH,
        )

    def weight_copies():
        copies = [pltpu.make_async_copy(tab_hbm, tab, sem_w.at[0])]
        mine = pl.ds(pl.multiple_of(c * half, half), half)
        for t, w in enumerate((wq, wk, wv)):
            copies.append(
                pltpu.make_async_copy(
                    w.at[:, mine], wqkv_v.at[:, pl.ds(t * half, half)], sem_w.at[1 + t]
                )
            )
        copies.append(pltpu.make_async_copy(wo, wo_v, sem_w.at[4]))
        for b in range(ff // 128):
            far = pl.ds(pl.multiple_of(256 * b + 128 * c, 128), 128)
            near = pl.ds(128 * b, 128)
            copies.append(pltpu.make_async_copy(wg.at[:, far], wg_v.at[:, near], sem_w.at[5 + 3 * b]))
            copies.append(pltpu.make_async_copy(wu.at[:, far], wu_v.at[:, near], sem_w.at[6 + 3 * b]))
            copies.append(pltpu.make_async_copy(wd.at[far], wd_v.at[near], sem_w.at[7 + 3 * b]))
        return copies

    weights = weight_copies()
    own_x = pltpu.make_async_copy(x_hbm.at[y], x4.at[s], sem_o.at[0])
    own_cot = pltpu.make_async_copy(cot_hbm.at[y], cot4.at[s], sem_o.at[1])
    own_x.start()
    for copy in weights[:4]:
        copy.start()

    barrier = pltpu.get_barrier_semaphore()
    for to in (sibling, y_dev, x_dev, near_z, far_z):
        pl.semaphore_signal(barrier, inc=1, device_id=to, device_id_type=MESH)
    pl.semaphore_wait(barrier, 5)

    s_y = (1 - y) * 2 + c
    across_x = send(x_hbm.at[1 - y], x4.at[s], sem_in_s.at[0], sem_in_r.at[0], y_dev)
    beside_x = send(x_hbm.at[y], x4.at[s], sem_in_s.at[1], sem_in_r.at[1], sibling)
    across_x.start()
    beside_x.start()
    across_c = send(cot_hbm.at[1 - y], cot4.at[s], sem_in_s.at[2], sem_in_r.at[2], y_dev)
    beside_c = send(cot_hbm.at[y], cot4.at[s], sem_in_s.at[3], sem_in_r.at[3], sibling)
    own_cot.start()
    for copy in weights[4:]:
        copy.start()
    relay_x = send(x4.at[s_y], x4.at[s_y], sem_in_s.at[4], sem_in_r.at[4], sibling)
    relay_c = send(cot4.at[s_y], cot4.at[s_y], sem_in_s.at[5], sem_in_r.at[5], sibling)

    length = lens[y]

    def norm_rows(piece):
        def one(b, carry):
            here = pl.ds(pl.multiple_of(b * step, step), step)
            values = x4[piece, here, :].astype(F32)
            scale = lax.rsqrt(jnp.mean(values * values, -1, keepdims=True) + epsilon)
            there = pl.ds(pl.multiple_of(piece * rows_here + b * step, step), step)
            nrm[there, :] = (values * scale * gain_a[...]).astype(LOW)
            return carry

        lax.fori_loop(0, per, one, 0)

    def project_rows(part):
        base = pl.multiple_of(part * 2 * rows_here, 32)
        here = pl.ds(base, 2 * rows_here)
        cosine = jnp.where(length == LONG, tab[2, here, :], tab[0, here, :])
        sine = jnp.where(length == LONG, tab[3, here, :], tab[1, here, :])
        for t in range(3):
            product = dot(nrm[here, :], wqkv_v[:, t * half : (t + 1) * half])
            for p in range(pairs):
                lanes = product[:, 128 * p : 128 * (p + 1)]
                if t < 2:
                    lanes = lanes * cosine + swap_quarters(lanes) * sine
                if t == 0:
                    lanes = lanes.astype(LOW).astype(F32) * HD ** (-0.5)
                qkv[t, here, 128 * p : 128 * (p + 1)] = lanes.astype(LOW)

    own_x.wait()
    norm_rows(s)
    beside_x.wait_recv()
    norm_rows(2 * y + 1 - c)
    for copy in weights[:4]:
        copy.wait()
    project_rows(y)
    across_x.wait_recv()
    relay_x.start()
    across_c.start()
    beside_c.start()
    norm_rows(s_y)
    relay_x.wait_recv()
    norm_rows(2 * (1 - y) + 1 - c)
    project_rows(1 - y)

    lane = lax.broadcasted_iota(jnp.int32, (1, 128), 1)
    left_head = lane < HD
    masks = [(lane // HD == n).astype(F32).astype(LOW) for n in range(2)]

    def mix_copy(pair):
        return send(
            mix_own.at[pair], mix_in.at[pair], sem_core_s.at[pair], sem_core_r.at[pair], sibling
        )

    tiles = blocks
    key = lax.broadcasted_iota(jnp.int32, (1, rows), 1)
    bias = jnp.where(key < length, 0.0, NEVER)

    def stacked(first, second):
        return jnp.concatenate([first, second], 0)

    def attend(pair, carry):
        lanes = pl.ds(pl.multiple_of(pair * 128, 128), 128)
        parts = []
        for k0, kb in tiles:
            query = qkv[0, k0:, lanes]
            part = dot_nt(stacked(query * masks[0], query * masks[1]), qkv[1, k0 : k0 + kb, lanes])
            parts.append(part + bias[:, k0 : k0 + kb] if k0 + kb > SHORT else part)
        for n in range(2):
            for r0, rb in blocks:
                scores = []
                for (k0, kb), part in zip(tiles, parts):
                    if k0 <= r0:
                        base = n * (rows - k0) + r0 - k0
                        here = part[base : base + rb]
                        if k0 == r0:
                            row = lax.broadcasted_iota(jnp.int32, here.shape, 0)
                            col = lax.broadcasted_iota(jnp.int32, here.shape, 1)
                            here = jnp.where(col <= row, here, NEVER)
                        scores.append((k0, kb, here))
                top = functools.reduce(jnp.maximum, [jnp.max(p, -1, keepdims=True) for _, _, p in scores])
                expo = [(k0, kb, jnp.exp(p - top)) for k0, kb, p in scores]
                inverse = 1.0 / sum(jnp.sum(p, -1, keepdims=True) for _, _, p in expo)
                for k0, kb, p in expo:
                    chance[pair * 2 + n, r0 : r0 + rb, k0 : k0 + kb] = (p * inverse).astype(LOW)
        outs = []
        for k0, kb in tiles:
            at = slice(k0, k0 + kb)
            low = stacked(chance[pair * 2, k0:, at], chance[pair * 2 + 1, k0:, at])
            outs.append(dot(low, qkv[2, at, lanes]))
        for r0, rb in blocks:
            both = []
            for n in range(2):
                at = [n * (rows - k0) + r0 - k0 for k0, _ in tiles if k0 <= r0]
                both.append(sum(out[b : b + rb] for b, out in zip(at, outs)))
            mix_own[pair, r0 : r0 + rb, :] = jnp.where(left_head, both[0], both[1]).astype(LOW)
        mix_copy(pair).start()
        return carry

    lax.fori_loop(0, pairs, attend, 0)

    across_c.wait_recv()
    relay_c.start()

    def turn_rows(src, dst):
        def one(b, carry):
            here = pl.ds(pl.multiple_of(b * 128, 128), 128)
            dst[:, here] = src[here, :].T
            return carry

        lax.fori_loop(0, rows // 128, one, 0)

    def place_mix(src, at):
        def one(p, carry):
            mix[:, pl.ds(pl.multiple_of(at * half + p * 128, 128), 128)] = src[p]
            return carry

        lax.fori_loop(0, pairs, one, 0)

    place_mix(mix_own, c)
    turn_rows(nrm, nrm_t)
    for p in range(pairs):
        mix_copy(p).wait_recv()
    place_mix(mix_in, 1 - c)

    weights[4].wait()

    def chunk(n, wide=WIDE):
        return pl.ds(pl.multiple_of(n * wide, wide), wide)

    def out_project(n, carry):
        mid[:, chunk(n)] = (
            dot(mix[...], wo_v[:, chunk(n)])
            + x4[:, :, chunk(n)].reshape(rows, WIDE).astype(F32)
        )
        return carry

    lax.fori_loop(0, width // WIDE, out_project, 0)

    def second_norm(b, carry):
        here = pl.ds(pl.multiple_of(b * step, step), step)
        values = mid[here, :]
        scale = lax.rsqrt(jnp.mean(values * values, -1, keepdims=True) + epsilon)
        nf[here, :] = (values * scale * gain_f[...]).astype(LOW)
        return carry

    lax.fori_loop(0, rows // step, second_norm, 0)
    turn_rows(nf, nf_t)
    for copy in weights[5:]:
        copy.wait()
    own_cot.wait()
    beside_c.wait_recv()
    relay_c.wait_recv()

    class Group:
        def __init__(self, parts, r1, r2, r3, fin, s_sem, r_sem):
            self.parts, self.r1, self.r2, self.r3, self.fin = parts, r1, r2, r3, fin
            self.s_sem, self.r_sem = s_sem, r_sem

        def copy(self, k, n, src, dst, to):
            return send(src, dst, self.s_sem.at[k, n], self.r_sem.at[k, n], to)

        def step1(self, k):
            self.hop(k, 0).start()

        def to_core(self, k):
            return self.copy(k, 5, self.fin.at[k, c], self.fin.at[k, c], sibling)

        def finish(self, k, own, new):
            for h in range(2):
                total = self.r1[own + (h,)].astype(F32) + self.r3[k, new + h].astype(F32)
                self.fin[k, c, h] = total.astype(LOW)
            self.to_core(k).start()

        def end(self, k):
            self.to_core(k).wait_recv()

        def sent(self, k):
            for n in range(self.hops):
                self.hop(k, n).wait_send()
            self.to_core(k).wait_send()

    def add(ref, at, other, of):
        ref[at] = (ref[at].astype(F32) + other[of].astype(F32)).astype(LOW)

    class XZY(Group):
        hops = 4

        def hop(self, k, n):
            r1, r2, r3 = self.r1, self.r2, self.r3
            if n == 0:
                return self.copy(k, n, self.parts.at[k, :, :, 1 - x], r1.at[k], x_dev)
            if n == 1:
                return self.copy(k, n, r1.at[k, :, 1 - z_lo], r2.at[k], near_z)
            if n == 2:
                return self.copy(k, n, r1.at[k, 1 - z_hi, z_lo], r3.at[k, pl.ds(0, 2)], far_z)
            return self.copy(k, n, r1.at[k, z_hi, z_lo], r3.at[k, pl.ds(2, 2)], y_dev)

        def step2(self, k):
            self.hop(k, 0).wait_recv()
            for lo in (1 - z_lo, z_lo):
                for hi in range(2):
                    for h in range(2):
                        add(self.r1, (k, hi, lo, h), self.parts, (k, hi, lo, x, h))
                if lo is not z_lo:
                    self.hop(k, 1).start()

        def step3(self, k):
            self.hop(k, 1).wait_recv()
            for hi in (1 - z_hi, z_hi):
                for h in range(2):
                    add(self.r1, (k, hi, z_lo, h), self.r2, (k, hi, h))
                if hi is not z_hi:
                    self.hop(k, 2).start()

        def step4(self, k):
            self.hop(k, 2).wait_recv()
            for h in range(2):
                add(self.r1, (k, z_hi, z_lo, h), self.r3, (k, h))
            self.hop(k, 3).start()

        def step5(self, k):
            self.hop(k, 3).wait_recv()
            self.finish(k, (k, z_hi, z_lo), 2)

    class ZXY(Group):
        hops = 4

        def hop(self, k, n):
            r1, r2, r3 = self.r1, self.r2, self.r3
            if n == 0:
                return self.copy(k, n, self.parts.at[k, :, 1 - z_lo], r1.at[k], near_z)
            if n == 1:
                return self.copy(k, n, r1.at[k, 1 - z_hi], r2.at[k], far_z)
            if n == 2:
                return self.copy(k, n, r1.at[k, z_hi, 1 - x], r3.at[k, pl.ds(0, 2)], x_dev)
            return self.copy(k, n, r1.at[k, z_hi, x], r3.at[k, pl.ds(2, 2)], y_dev)

        def step2(self, k):
            self.hop(k, 0).wait_recv()
            for hi in (1 - z_hi, z_hi):
                for xx in range(2):
                    for h in range(2):
                        add(self.r1, (k, hi, xx, h), self.parts, (k, hi, z_lo, xx, h))
                if hi is not z_hi:
                    self.hop(k, 1).start()

        def step3(self, k):
            self.hop(k, 1).wait_recv()
            for xx in (1 - x, x):
                for h in range(2):
                    add(self.r1, (k, z_hi, xx, h), self.r2, (k, xx, h))
                if xx is not x:
                    self.hop(k, 2).start()

        def step4(self, k):
            self.hop(k, 2).wait_recv()
            for h in range(2):
                add(self.r1, (k, z_hi, x, h), self.r3, (k, h))
            self.hop(k, 3).start()

        def step5(self, k):
            self.hop(k, 3).wait_recv()
            self.finish(k, (k, z_hi, x), 2)

    class YXZ(Group):
        hops = 5

        def hop(self, k, n):
            r1, r2, r3 = self.r1, self.r2, self.r3
            if n == 0:
                return self.copy(k, n, self.parts.at[k, :, :, :, 1 - y], r1.at[k], y_dev)
            if n == 1:
                return self.copy(k, n, r1.at[k, :, :, 1 - x], r2.at[k], x_dev)
            if n == 2:
                return self.copy(k, n, r2.at[k, :, 1 - z_lo], r3.at[k, pl.ds(0, 2)], near_z)
            if n == 3:
                return self.copy(k, n, r2.at[k, 1 - z_hi, z_lo], r3.at[k, 2], far_z)
            return self.copy(k, n, self.fin.at[k, c, y], self.fin.at[k, c, y], y_dev)

        def beside(self, k, n):
            at = self.fin.at[k, c, y] if n == 0 else self.fin.at[k, c, 1 - y]
            return self.copy(k, 5 + n, at, at, sibling)

        def step2(self, k):
            self.hop(k, 0).wait_recv()
            for xx in (1 - x, x):
                for hi in range(2):
                    for lo in range(2):
                        add(self.r1, (k, hi, lo, xx), self.parts, (k, hi, lo, xx, y))
                if xx is not x:
                    self.hop(k, 1).start()

        def step3(self, k):
            self.hop(k, 1).wait_recv()
            for lo in (1 - z_lo, z_lo):
                for hi in range(2):
                    add(self.r2, (k, hi, lo), self.r1, (k, hi, lo, x))
                if lo is not z_lo:
                    self.hop(k, 2).start()

        def step4(self, k):
            self.hop(k, 2).wait_recv()
            for hi in (1 - z_hi, z_hi):
                add(self.r2, (k, hi, z_lo), self.r3, (k, hi))
                if hi is not z_hi:
                    self.hop(k, 3).start()

        def step5(self, k):
            self.hop(k, 3).wait_recv()
            total = self.r2[k, z_hi, z_lo].astype(F32) + self.r3[k, 2].astype(F32)
            self.fin[k, c, y] = total.astype(LOW)
            self.hop(k, 4).start()
            self.beside(k, 0).start()

        def step6(self, k):
            self.hop(k, 4).wait_recv()
            self.beside(k, 1).start()

        def end(self, k):
            for n in range(2):
                self.beside(k, n).wait_recv()

        def sent(self, k):
            for n in range(self.hops):
                self.hop(k, n).wait_send()
            for n in range(2):
                self.beside(k, n).wait_send()

    class Gains:
        def hop(self, k, n):
            src = (gain_s, gain_x, gain_y, gain_z, gain_s)[n]
            dst = (gain_x, gain_y, gain_z, gain_f_z, gain_c)[n]
            to = (x_dev, y_dev, near_z, far_z, sibling)[n]
            return send(src, dst, sem_gain_s.at[n], sem_gain_r.at[n], to)

        def step1(self, k):
            self.hop(k, 0).start()

        def step2(self, k):
            self.hop(k, 0).wait()
            gain_x[...] = gain_s[...] + gain_x[...]
            self.hop(k, 1).start()

        def step3(self, k):
            self.hop(k, 1).wait()
            gain_y[...] = gain_x[...] + gain_y[...]
            self.hop(k, 2).start()

        def step4(self, k):
            self.hop(k, 2).wait()
            gain_z[...] = gain_y[...] + gain_z[...]
            self.hop(k, 3).start()

        def step5(self, k):
            self.hop(k, 3).wait()
            gain_s[...] = gain_z[...] + gain_f_z[...]
            self.hop(k, 4).start()

        def end(self, k):
            self.hop(k, 4).wait()
            top = lax.broadcasted_iota(jnp.int32, gain_s.shape, 0) == 0
            total = gain_s[...] + jnp.where(top, gain_c[...], 0.0)
            gain_c[...] = pltpu.roll(total, lax.rem(8 - i, 8) * (width // 8), 1)

        def sent(self, k):
            pass

    buffers_a = (pa, r1a, r2a, r3a, fa, sa_s, sa_r)
    buffers_d = (pd, r1d, r2d, r3d, fd, sd_s, sd_r)
    buffers_q = (pq, r1q, r2q, r3q, fq, sq_s, sq_r)
    kinds = {"x": XZY, "y": YXZ, "z": ZXY}
    chunks = [(kinds[kind](*buffers_a), n) for n, kind in enumerate(PLANS[:8])]
    chunks += [(kinds[kind](*buffers_d), n) for n, kind in enumerate(PLANS[8:11])]
    chunks += [(kinds[kind](*buffers_q), n) for n, kind in enumerate(PLANS[11:])]
    chunks += [(Gains(), 0)]
    slots = iter(ORDER)

    def first(chunk):
        group, k = chunks[chunk]
        group.step1(k)

    def turn():
        for code in next(slots):
            group, k = chunks[code // 10]
            getattr(group, f"step{code % 10}")(k)

    chunks_f = ff // WIDE
    chunks_w = width // WIDE

    def feed(n, carry):
        at = chunk(n)
        big[:, 0:WIDE] = dot(nf[...], wg_v[:, at])
        big[:, WIDE : 2 * WIDE] = dot(nf[...], wu_v[:, at])
        big[:, 2 * WIDE : 3 * WIDE] = dot_nt(cot4[...].reshape(rows, width), wd_v[at, :])

        def one(b, inner):
            here = pl.ds(pl.multiple_of(b * fine, fine), fine)
            gate = big[here, 0:WIDE]
            up = big[here, WIDE : 2 * WIDE]
            back = big[here, 2 * WIDE : 3 * WIDE]
            sigma = 0.5 * jnp.tanh(0.5 * gate) + 0.5
            silu = gate * sigma
            hid[here, at] = (silu * up).astype(LOW)
            gg[here, at] = (back * up * (sigma + silu * (1.0 - sigma))).astype(LOW)
            gu[here, at] = (back * silu).astype(LOW)
            return inner

        lax.fori_loop(0, rows // fine, one, 0, unroll=5)
        shape = pa.shape[1:]
        pa[n] = dot(nf_t[...], gg[:, at]).reshape(shape).astype(LOW)
        first(n)
        pa[n + chunks_f] = dot(nf_t[...], gu[:, at]).reshape(shape).astype(LOW)
        first(n + chunks_f)
        hid_t[at, :] = hid[:, at].T
        return carry

    for n in range(chunks_f):
        turn()
        feed(n, 0)
    turn()

    def gnf_copy(n):
        return send(
            gnf_out.at[n], gnf_in.at[n], sem_core_s.at[pairs + n], sem_core_r.at[pairs + n], sibling
        )

    def back_ffn(n, carry):
        partial = dot_nt(gg[...], wg_v[chunk(n), :]) + dot_nt(gu[...], wu_v[chunk(n), :])
        big[:, chunk(n)] = partial
        gnf_out[n] = partial.astype(LOW)
        gnf_copy(n).start()
        return carry

    for n in range(chunks_w):
        back_ffn(n, 0)
        turn()

    def down(n, carry):
        big[:, chunk(n + chunks_w)] = dot(hid[...], wd_v[:, chunk(n)])
        return carry

    lax.fori_loop(0, chunks_w, down, 0)
    n_core = pairs + chunks_w
    bo_copy = send(sb, rb, sem_core_s.at[n_core], sem_core_r.at[n_core], sibling)
    far = slice(width, 2 * width)

    def for_rows(core, fn):
        for yy in range(2):
            def one(b, carry, yy=yy):
                base = pl.multiple_of((2 * yy + core) * rows_here + b * step, step)
                fn(yy, b, pl.ds(base, step), pl.ds(pl.multiple_of(b * step, step), step))
                return carry

            lax.fori_loop(0, per, one, 0)

    def pack_bo(yy, b, here, there):
        sb[yy, there, :] = big[here, far].astype(LOW)

    for_rows(1 - c, pack_bo)
    bo_copy.start()

    for n in range(chunks_w):
        turn()
        at = slice(n * WIDE, (n + 1) * WIDE)
        pd[n] = (
            dot(hid_t[...], cot4[:, :, at].reshape(rows, WIDE)).reshape(pd.shape[1:]).astype(LOW)
        )
        first(8 + n)

    turn()
    bo_copy.wait_recv()

    def finish_bo(yy, b, here, there):
        bo[yy, there, :] = (mid[here, :] + big[here, far] + rb[yy, there, :].astype(F32)).astype(LOW)

    for_rows(c, finish_bo)
    bo_across = send(bo.at[1 - y], bo_in, sem_in_s.at[6], sem_in_r.at[6], y_dev)
    bo_across.start()

    turn()
    for n in range(chunks_w):
        gnf_copy(n).wait_recv()

    def middle_back(b, total):
        here = pl.ds(pl.multiple_of(b * step, step), step)
        values = mid[here, :]
        grad = big[here, 0:width] + jnp.concatenate(
            [gnf_in[n, here, :].astype(F32) for n in range(chunks_w)], -1
        )
        scale = lax.rsqrt(jnp.mean(values * values, -1, keepdims=True) + epsilon)
        unit = values * scale
        total = total + (grad * unit).reshape(step // 8, 8, width).sum(0)
        scaled = grad * gain_f[...]
        inner = jnp.mean(scaled * unit, -1, keepdims=True)
        out = cot4[b // per, pl.ds(pl.multiple_of(lax.rem(b, per) * step, step), step), :].astype(F32)
        out = out + scale * (scaled - unit * inner)
        mid[here, :] = out
        gb[here, :] = out.astype(LOW)
        return total

    total_f = lax.fori_loop(0, rows // step, middle_back, jnp.zeros((8, width), F32))

    turn()
    turn_rows(mix, mix_t)
    mine = pl.ds(pl.multiple_of(c * half, half), half)
    pq[0] = dot(mix_t[...], gb[:, mine]).reshape(pq.shape[1:]).astype(LOW)
    first(11)
    gmx[...] = dot_nt(gb[...], wo_v[mine, :]).astype(LOW)

    def query_back(pair):
        lanes = slice(pair * 128, pair * 128 + 128)
        grads = []
        for k0, kb in tiles:
            grad = gmx[k0:, lanes]
            grads.append(
                dot_nt(stacked(grad * masks[0], grad * masks[1]), qkv[2, k0 : k0 + kb, lanes])
            )
        for n in range(2):
            for r0, rb in blocks:
                both = []
                for (k0, kb), grad in zip(tiles, grads):
                    if k0 <= r0:
                        base = n * (rows - k0) + r0 - k0
                        prob = chance[pair * 2 + n, r0 : r0 + rb, k0 : k0 + kb].astype(F32)
                        both.append((slice(k0, k0 + kb), prob, grad[base : base + rb] * prob))
                inner = sum(jnp.sum(each, -1, keepdims=True) for _, _, each in both)
                for at, prob, each in both:
                    ds_s[n, r0 : r0 + rb, at] = (each - prob * inner).astype(LOW)
        outs = []
        for k0, kb in tiles:
            at = slice(k0, k0 + kb)
            outs.append(dot(stacked(ds_s[0, k0:, at], ds_s[1, k0:, at]), qkv[1, at, lanes]))
        for r0, rb in blocks:
            both = []
            for n in range(2):
                at = [n * (rows - k0) + r0 - k0 for k0, _ in tiles if k0 <= r0]
                both.append(sum(out[b : b + rb] for b, out in zip(at, outs)))
            big[r0 : r0 + rb, 0:128] = jnp.where(left_head, both[0], both[1])

    def keys_back(pair):
        lanes = slice(pair * 128, pair * 128 + 128)

        def beside(first, second):
            return jnp.concatenate([first, second], 1)

        for k0, kb in tiles:
            at = slice(k0, k0 + kb)
            out = dot_tn(beside(ds_s[0, k0:, at], ds_s[1, k0:, at]), qkv[0, k0:, lanes])
            big[at, 128:256] = jnp.where(left_head, out[:kb], out[kb:])
            low = beside(chance[pair * 2, k0:, at], chance[pair * 2 + 1, k0:, at])
            out = dot_tn(low, gmx[k0:, lanes])
            big[at, 256:384] = jnp.where(left_head, out[:kb], out[kb:])

        def one(b, inner):
            here = pl.ds(pl.multiple_of(b * 64, 64), 64)
            cosine = jnp.where(length == LONG, tab[2, here, :], tab[0, here, :])
            sine = jnp.where(length == LONG, tab[3, here, :], tab[1, here, :])
            for t in range(3):
                values = big[here, 128 * t : 128 * (t + 1)]
                if t == 0:
                    values = values * HD ** (-0.5)
                if t < 2:
                    values = values * cosine - swap_quarters(values) * sine
                gqkv[here, t * half + pair * 128 : t * half + pair * 128 + 128] = values.astype(LOW)
            return inner

        lax.fori_loop(0, rows // 64, one, 0, unroll=5)

    for pair in range(pairs):
        turn()
        query_back(pair)
        turn()
        keys_back(pair)

    for t in range(3):
        turn()
        pq[1 + t] = (
            dot(nrm_t[...], gqkv[:, t * half : (t + 1) * half]).reshape(pq.shape[1:]).astype(LOW)
        )
        first(12 + t)

    turn()

    def back_attn(n, carry):
        big[:, chunk(n)] = dot_nt(gqkv[...], wqkv_v[chunk(n), :])
        return carry

    lax.fori_loop(0, chunks_w, back_attn, 0)
    turn()

    def pack_gi(yy, b, here, there):
        sb2[yy, there, :] = big[here, 0:width].astype(LOW)

    for_rows(1 - c, pack_gi)
    gi_copy = send(sb2, rb2, sem_core_s.at[n_core + 1], sem_core_r.at[n_core + 1], sibling)
    gi_copy.start()

    def gain_back(b, total):
        here = pl.ds(pl.multiple_of(b * step, step), step)
        values = x4[b // per, pl.ds(pl.multiple_of(lax.rem(b, per) * step, step), step), :].astype(F32)
        scale = lax.rsqrt(jnp.mean(values * values, -1, keepdims=True) + epsilon)
        return total + (big[here, 0:width] * (values * scale)).reshape(step // 8, 8, width).sum(0)

    total_a = lax.fori_loop(0, rows // step, gain_back, jnp.zeros((8, width), F32))
    row = lax.broadcasted_iota(jnp.int32, (8, width), 0)
    gain_s[...] = jnp.where(
        row == 0, jnp.sum(total_a, 0, keepdims=True), jnp.sum(total_f, 0, keepdims=True)
    )
    first(15)
    turn()
    gi_copy.wait_recv()

    def finish_gi(yy, b, here, there):
        values = x4[2 * yy + c, there, :].astype(F32)
        scale = lax.rsqrt(jnp.mean(values * values, -1, keepdims=True) + epsilon)
        unit = values * scale
        scaled = (big[here, 0:width] + rb2[yy, there, :].astype(F32)) * gain_a[...]
        inner = jnp.mean(scaled * unit, -1, keepdims=True)
        gi[yy, there, :] = (mid[here, :] + scale * (scaled - unit * inner)).astype(LOW)

    for_rows(c, finish_gi)
    gi_across = send(gi.at[1 - y], gi_in, sem_in_s.at[7], sem_in_r.at[7], y_dev)
    gi_across.start()

    turn()
    for group, k in chunks:
        group.end(k)

    outs = [
        pltpu.make_async_copy(fa, fa_hbm, sem_o.at[2]),
        pltpu.make_async_copy(fd, fd_hbm, sem_o.at[3]),
        pltpu.make_async_copy(fq, fq_hbm, sem_o.at[4]),
        pltpu.make_async_copy(gain_c, gain_hbm, sem_o.at[5]),
        pltpu.make_async_copy(bo.at[y], bo_hbm.at[y], sem_o.at[6]),
        pltpu.make_async_copy(gi.at[y], gi_hbm.at[y], sem_o.at[7]),
    ]
    for copy in outs:
        copy.start()
    bo_across.wait_recv()
    gi_across.wait_recv()
    outs += [
        pltpu.make_async_copy(bo_in, bo_hbm.at[1 - y], sem_o.at[8]),
        pltpu.make_async_copy(gi_in, gi_hbm.at[1 - y], sem_o.at[9]),
    ]
    for copy in outs[6:]:
        copy.start()
    for copy in outs:
        copy.wait()

    for copy in (across_x, beside_x, across_c, beside_c, relay_x, relay_c, bo_across, gi_across):
        copy.wait_send()
    for p in range(pairs):
        mix_copy(p).wait_send()
    for n in range(chunks_w):
        gnf_copy(n).wait_send()
    bo_copy.wait_send()
    gi_copy.wait_send()
    for group, k in chunks:
        group.sent(k)


def spread(chunks_f, share, *refs):
    fa_far, fd_far, fq_far, bo, gi, gains_far = refs[:6]
    outs, (fa, fd, fq, gains), stage, sem_in, sem_out = refs[6:17], refs[17:21], refs[21:28], *refs[28:]
    bo_out, gi_out, da, df = outs[0], outs[1], outs[2], outs[7]
    ends = outs[3:7] + outs[8:]
    dq, dk, dv, do, dg, du, dd = stage
    near = [
        pltpu.make_async_copy(a, b, sem_in.at[n])
        for n, (a, b) in enumerate(
            [(fa_far.at[:chunks_f], fa.at[:chunks_f]), (fa_far.at[chunks_f:], fa.at[chunks_f:])]
            + [(fd_far, fd), (fq_far, fq), (gains_far, gains), (bo, bo_out), (gi, gi_out)]
        )
    ]
    for copy in near:
        copy.start()
    done = [pltpu.make_async_copy(a, b, sem_out.at[n]) for n, (a, b) in enumerate(zip(stage, ends))]
    rows, half, deep = fa.shape[3], fq.shape[4], fd.shape[3]
    halves = [(core, h, slice(h * rows, (h + 1) * rows)) for core in range(2) for h in range(2)]

    for first, ref, copy in ((0, dg, 0), (chunks_f, du, 1)):
        near[copy].wait()
        for core, h, at in halves:
            for n in range(chunks_f):
                for b in range(WIDE // 128):
                    far = 256 * (n * (WIDE // 128) + b) + 128 * core
                    ref[at, far : far + 128] = fa[
                        n + first, core, h, :, 128 * b : 128 * (b + 1)
                    ].astype(F32)
        done[4 + copy].start()
    near[2].wait()
    for core, h, _ in halves:
        at = slice((2 * core + h) * deep, (2 * core + h + 1) * deep)
        for n in range(fd.shape[0]):
            dd[at, WIDE * n : WIDE * (n + 1)] = fd[n, core, h].astype(F32)
    done[6].start()
    near[3].wait()
    for n, (ref, end) in enumerate(((do, 3), (dq, 0), (dk, 1), (dv, 2))):
        for core, h, at in halves:
            ref[at, core * half : (core + 1) * half] = fq[n, core, h].astype(F32)
        done[end].start()
    near[4].wait()
    da[...] = gains[0, 0:share]
    df[...] = gains[1, 0:share]
    near[5].wait()
    near[6].wait()
    for copy in done:
        copy.wait()


def item_per_chip(
    block_in, lengths, gain_attn, w_query, w_key, w_value, w_out, gain_ffn, w_gate, w_up, w_down,
    cotangent,
):
    _, rows_here, width = block_in.shape
    hidden_all = w_gate.shape[1]
    rows = rows_here * lax.axis_size("seq")
    shares = lax.axis_size("items")
    half, ff = width // 2, hidden_all // 2
    pairs = half // 128
    chunks_f, chunks_w = ff // WIDE, width // WIDE
    thin, deep = width // shares // 2, ff // shares // 2
    tables = jnp.asarray(rope_constants(rows))
    any_ = pl.BlockSpec(memory_space=pl.ANY)
    vmem = pl.BlockSpec(memory_space=pltpu.VMEM)

    def group(n, r, w):
        return [
            pltpu.VMEM((n, 2, 2, 2, 2, r, w), LOW),
            pltpu.VMEM((n, 2, 2, 2, r, w), LOW),
            pltpu.VMEM((n, 2, 2, r, w), LOW),
            pltpu.VMEM((n, 4, r, w), LOW),
            pltpu.VMEM((n, 2, 2, r, w), LOW),
        ]

    def low(*shape):
        return pltpu.VMEM(shape, LOW)

    def full(*shape):
        return pltpu.VMEM(shape, F32)

    dma = pltpu.SemaphoreType.DMA
    scratch = [
        low(4, rows_here, width), low(4, rows_here, width), full(4, rows, 128),
        low(width, 3 * half), low(width, width), low(width, ff), low(width, ff), low(ff, width),
        low(rows, width), low(width, rows), low(3, rows, half), low(2 * pairs, rows, rows),
        low(pairs, rows, 128), low(pairs, rows, 128), low(rows, width), low(width, rows),
        full(rows, width), low(rows, width), low(width, rows), low(rows, ff), low(ff, rows),
        low(rows, ff), low(rows, ff), full(rows, 2 * width),
        low(chunks_w, rows, WIDE), low(chunks_w, rows, WIDE),
        low(2, rows_here, width), low(2, rows_here, width),
        low(2, rows_here, width), low(rows_here, width),
        low(rows, width), low(rows, half), low(2, rows, rows), low(rows, 3 * half),
        low(2, rows_here, width), low(2, rows_here, width),
        low(2, rows_here, width), low(rows_here, width),
        full(8, width), full(8, width), full(8, width), full(8, width), full(8, width), full(8, width),
    ]
    scratch += group(2 * chunks_f, thin, WIDE) + group(chunks_w, deep, WIDE) + group(4, thin, half)
    scratch += [
        dma((5 + 3 * (ff // 128),)), dma((8,)), dma((8,)),
        dma((pairs + chunks_w + 2,)), dma((pairs + chunks_w + 2,)), dma((6,)), dma((6,)), dma((10,)),
        dma((2 * chunks_f, 8)), dma((2 * chunks_f, 8)), dma((chunks_w, 8)), dma((chunks_w, 8)),
        dma((4, 8)), dma((4, 8)),
    ]
    shape = jax.ShapeDtypeStruct
    bo, gi, fa, fd, fq, gains = pl.pallas_call(
        functools.partial(fused, (rows_here, width, hidden_all)),
        out_shape=(
            shape(block_in.shape, LOW), shape(block_in.shape, LOW),
            shape((2 * chunks_f, 2, 2, thin, WIDE), LOW), shape((chunks_w, 2, 2, deep, WIDE), LOW),
            shape((4, 2, 2, thin, half), LOW), shape((8, width), F32),
        ),
        in_specs=[pl.BlockSpec(memory_space=pltpu.SMEM), vmem, vmem] + [any_] * 10,
        out_specs=(any_,) * 6,
        scratch_shapes=scratch,
        compiler_params=pltpu.CompilerParams(
            collective_id=0, has_side_effects=True, vmem_limit_bytes=63 * 2**20
        ),
        name="block",
    )(
        lengths, gain_attn, gain_ffn, block_in, cotangent, tables,
        w_query, w_key, w_value, w_out, w_gate, w_up, w_down,
    )
    thick = (width // shares, width)
    made = (fa, fd, fq, bo, gi, gains)
    share = width // shares
    bo, gi, da, dq, dk, dv, do, df, dg, du, dd = pl.pallas_call(
        functools.partial(spread, chunks_f, share),
        out_shape=(
            shape(block_in.shape, LOW), shape(block_in.shape, LOW), shape((share,), F32),
            shape(thick, F32), shape(thick, F32), shape(thick, F32), shape(thick, F32),
            shape((share,), F32),
            shape((width // shares, hidden_all), F32), shape((width // shares, hidden_all), F32),
            shape((hidden_all // shares, width), F32),
        ),
        in_specs=[any_] * 6,
        out_specs=(vmem,) * 3 + (any_,) * 4 + (vmem,) + (any_,) * 3,
        scratch_shapes=[pltpu.VMEM(a.shape, a.dtype) for a in (fa, fd, fq, gains)]
        + [pltpu.VMEM(thick, F32)] * 4
        + [pltpu.VMEM((width // shares, hidden_all), F32)] * 2
        + [pltpu.VMEM((hidden_all // shares, width), F32), dma((7,)), dma((7,))],
        compiler_params=pltpu.CompilerParams(vmem_limit_bytes=60 * 2**20),
        name="spread",
    )(*made)
    return bo, gi, da, dq, dk, dv, do, df, dg, du, dd


def solution(mesh):
    fits = mesh.shape["seq"] == 4 and mesh.shape["items"] == 8
    return jax.shard_map(
        item_per_chip if fits else body,
        mesh=mesh,
        in_specs=(P("items", "seq", None), P("items")) + (P(),) * 9 + (P("items", "seq", None),),
        out_specs=(
            (P("items", "seq", None),) * 2
            + (P("items"),) + (P("items", None),) * 4
            + (P("items"),) + (P("items", None),) * 3
        ),
        check_vma=False,
    )
```

```python
import functools

import jax
import jax.numpy as jnp
import numpy as np
from jax import lax
from jax.experimental import pallas as pl
from jax.experimental.pallas import tpu as pltpu
from jax.sharding import PartitionSpec as P

HD = 64
SIDE_S = 16
SIDE_L = 24
LONG = 577


epsilon = 1e-05


def grid_places(lengths, rows):
    side = jnp.where(lengths == LONG, SIDE_L, SIDE_S).astype(jnp.int32)[:, None]
    place = rows[None, :] - 1
    valid = (place >= 0) & (rows[None, :] < lengths[:, None])
    place = jnp.where(valid, place, 0)
    return (place // side, place % side)


def rotary_tables(lengths, rows):
    grid_row, grid_col = grid_places(lengths, rows)
    quarter = HD // 4
    freq = 10000.0 ** (-jnp.arange(quarter, dtype=jnp.float32) / quarter)
    angle_row = grid_row[..., None].astype(jnp.float32) * freq
    angle_col = grid_col[..., None].astype(jnp.float32) * freq
    cosine = jnp.concatenate(
        [jnp.cos(angle_row), jnp.cos(angle_row), jnp.cos(angle_col), jnp.cos(angle_col)], -1
    )
    sine = jnp.concatenate(
        [jnp.sin(angle_row), jnp.sin(angle_row), jnp.sin(angle_col), jnp.sin(angle_col)], -1
    )
    return (cosine[:, :, None, :], sine[:, :, None, :])


def turn(values):
    quarter = HD // 4
    first = values[..., 0:quarter]
    second = values[..., quarter : 2 * quarter]
    third = values[..., 2 * quarter : 3 * quarter]
    fourth = values[..., 3 * quarter :]
    return jnp.concatenate([-second, first, -fourth, third], -1)


def project(left, right):
    return jnp.einsum("ird,de->ire", left, right, preferred_element_type=jnp.float32)


def back_project(grad, weight):
    return jnp.einsum("ire,de->ird", grad, weight, preferred_element_type=jnp.float32)


def weight_grad(left, right):
    return jnp.einsum("ird,ire->de", left, right, preferred_element_type=jnp.float32)


def norm_back(grad_normed, unit, scale, gain):
    scaled = grad_normed * gain
    return scale * (scaled - unit * jnp.mean(scaled * unit, -1, keepdims=True))


def body(
    block_in,
    lengths,
    gain_attn,
    w_query,
    w_key,
    w_value,
    w_out,
    gain_ffn,
    w_gate,
    w_up,
    w_down,
    cotangent,
):
    count, rows_here, width = block_in.shape
    heads = width // HD
    length_all = rows_here * lax.axis_size("seq")
    factor = HD ** (-0.5)
    query_rows = lax.axis_index("seq") * rows_here + jnp.arange(rows_here, dtype=jnp.int32)
    key_rows = jnp.arange(length_all, dtype=jnp.int32)
    cosine, sine = rotary_tables(lengths, query_rows)
    allowed = (key_rows[None, None, :] <= query_rows[None, :, None]) & (
        key_rows[None, None, :] < lengths[:, None, None]
    )

    def heads_of(array):
        return array.reshape(array.shape[0], array.shape[1], heads, HD)

    def attention_scores(query, keys_all):
        raw = (
            jnp.einsum(
                "irhe,iphe->ihrp", query, heads_of(keys_all), preferred_element_type=jnp.float32
            )
            * factor
        )
        return jnp.where(allowed[:, None], raw, -1e30)

    source = block_in.astype(jnp.float32)
    scale_attn = lax.rsqrt(jnp.mean(source * source, -1, keepdims=True) + epsilon)
    unit_attn = source * scale_attn
    normed = (unit_attn * gain_attn).astype(jnp.bfloat16)
    query_pre = heads_of(project(normed, w_query))
    keys_pre = heads_of(project(normed, w_key))
    query = (query_pre * cosine + turn(query_pre) * sine).astype(jnp.bfloat16)
    keys = (
        (keys_pre * cosine + turn(keys_pre) * sine)
        .astype(jnp.bfloat16)
        .reshape(count, rows_here, width)
    )
    values = project(normed, w_value).astype(jnp.bfloat16)
    keys_all, values_all = (
        lax.all_gather(keys, "seq", axis=1, tiled=True),
        lax.all_gather(values, "seq", axis=1, tiled=True),
    )
    scores = attention_scores(query, keys_all)
    top = jnp.max(scores, -1, keepdims=True)
    expo = jnp.exp(scores - top)
    summed = jnp.sum(expo, -1, keepdims=True)
    chance = expo / summed
    log_total = top + jnp.log(summed)
    mixed = (
        jnp.einsum(
            "ihrp,iphe->irhe",
            chance.astype(jnp.bfloat16),
            heads_of(values_all),
            preferred_element_type=jnp.float32,
        )
        .reshape(count, rows_here, width)
        .astype(jnp.bfloat16)
    )
    middle = source + project(mixed, w_out)
    scale_ffn = lax.rsqrt(jnp.mean(middle * middle, -1, keepdims=True) + epsilon)
    unit_ffn = middle * scale_ffn
    normed_ffn = (unit_ffn * gain_ffn).astype(jnp.bfloat16)
    gate = project(normed_ffn, w_gate)
    up = project(normed_ffn, w_up)
    sigma = jax.nn.sigmoid(gate)
    hidden = (gate * sigma * up).astype(jnp.bfloat16)
    block_out = (middle + project(hidden, w_down)).astype(jnp.bfloat16)
    incoming = cotangent.astype(jnp.float32)
    grad_w_down = weight_grad(hidden, cotangent)
    grad_hidden = back_project(cotangent, w_down)
    grad_gate = (grad_hidden * up * sigma * (1.0 + gate * (1.0 - sigma))).astype(jnp.bfloat16)
    grad_up = (grad_hidden * gate * sigma).astype(jnp.bfloat16)
    grad_w_gate = weight_grad(normed_ffn, grad_gate)
    grad_w_up = weight_grad(normed_ffn, grad_up)
    grad_normed_ffn = back_project(grad_gate, w_gate) + back_project(grad_up, w_up)
    grad_gain_ffn = jnp.sum(grad_normed_ffn * unit_ffn, axis=(0, 1))
    grad_middle = incoming + norm_back(grad_normed_ffn, unit_ffn, scale_ffn, gain_ffn)
    grad_branch = grad_middle.astype(jnp.bfloat16)
    grad_w_out = weight_grad(mixed, grad_branch)
    grad_mixed = heads_of(back_project(grad_branch, w_out)).astype(jnp.bfloat16)
    keys_back, values_back = (keys_all, values_all)
    chance_back = jnp.exp(attention_scores(query, keys_back) - log_total)
    grad_chance = jnp.einsum(
        "irhe,iphe->ihrp", grad_mixed, heads_of(values_back), preferred_element_type=jnp.float32
    )
    inner = jnp.sum(grad_chance * chance_back, -1, keepdims=True)
    grad_scores = (chance_back * (grad_chance - inner)).astype(jnp.bfloat16)
    grad_query = (
        jnp.einsum(
            "ihrp,iphe->irhe", grad_scores, heads_of(keys_back), preferred_element_type=jnp.float32
        )
        * factor
    )
    grad_values_sum = jnp.einsum(
        "ihrp,irhe->iphe",
        chance_back.astype(jnp.bfloat16),
        grad_mixed,
        preferred_element_type=jnp.float32,
    )
    grad_keys_sum = (
        jnp.einsum("ihrp,irhe->iphe", grad_scores, query, preferred_element_type=jnp.float32)
        * factor
    )
    grad_keys, grad_values = (
        lax.psum_scatter(
            grad_keys_sum.reshape(count, length_all, width).astype(jnp.bfloat16),
            "seq",
            scatter_dimension=1,
            tiled=True,
        ).astype(jnp.float32),
        lax.psum_scatter(
            grad_values_sum.reshape(count, length_all, width).astype(jnp.bfloat16),
            "seq",
            scatter_dimension=1,
            tiled=True,
        ).astype(jnp.float32),
    )
    grad_query_pre = (
        (grad_query * cosine - turn(grad_query * sine))
        .reshape(count, rows_here, width)
        .astype(jnp.bfloat16)
    )
    grad_keys_heads = heads_of(grad_keys)
    grad_keys_pre = (
        (grad_keys_heads * cosine - turn(grad_keys_heads * sine))
        .reshape(count, rows_here, width)
        .astype(jnp.bfloat16)
    )
    grad_values_pre = grad_values.astype(jnp.bfloat16)
    grad_w_query = weight_grad(normed, grad_query_pre)
    grad_w_key = weight_grad(normed, grad_keys_pre)
    grad_w_value = weight_grad(normed, grad_values_pre)
    grad_normed = (
        back_project(grad_query_pre, w_query)
        + back_project(grad_keys_pre, w_key)
        + back_project(grad_values_pre, w_value)
    )
    grad_gain_attn = jnp.sum(grad_normed * unit_attn, axis=(0, 1))
    grad_input = (grad_middle + norm_back(grad_normed, unit_attn, scale_attn, gain_attn)).astype(
        jnp.bfloat16
    )
    shares = (
        lax.psum_scatter(
            grad_gain_attn.astype(jnp.bfloat16), "items", scatter_dimension=0, tiled=True
        ).astype(jnp.float32),
        lax.psum_scatter(
            grad_w_query.astype(jnp.bfloat16), "items", scatter_dimension=0, tiled=True
        ).astype(jnp.float32),
        lax.psum_scatter(
            grad_w_key.astype(jnp.bfloat16), "items", scatter_dimension=0, tiled=True
        ).astype(jnp.float32),
        lax.psum_scatter(
            grad_w_value.astype(jnp.bfloat16), "items", scatter_dimension=0, tiled=True
        ).astype(jnp.float32),
        lax.psum_scatter(
            grad_w_out.astype(jnp.bfloat16), "items", scatter_dimension=0, tiled=True
        ).astype(jnp.float32),
        lax.psum_scatter(
            grad_gain_ffn.astype(jnp.bfloat16), "items", scatter_dimension=0, tiled=True
        ).astype(jnp.float32),
        lax.psum_scatter(
            grad_w_gate.astype(jnp.bfloat16), "items", scatter_dimension=0, tiled=True
        ).astype(jnp.float32),
        lax.psum_scatter(
            grad_w_up.astype(jnp.bfloat16), "items", scatter_dimension=0, tiled=True
        ).astype(jnp.float32),
        lax.psum_scatter(
            grad_w_down.astype(jnp.bfloat16), "items", scatter_dimension=0, tiled=True
        ).astype(jnp.float32),
    )
    summed = (
        lax.psum(shares[0].astype(jnp.bfloat16), "seq").astype(jnp.float32),
        lax.psum(shares[1].astype(jnp.bfloat16), "seq").astype(jnp.float32),
        lax.psum(shares[2].astype(jnp.bfloat16), "seq").astype(jnp.float32),
        lax.psum(shares[3].astype(jnp.bfloat16), "seq").astype(jnp.float32),
        lax.psum(shares[4].astype(jnp.bfloat16), "seq").astype(jnp.float32),
        lax.psum(shares[5].astype(jnp.bfloat16), "seq").astype(jnp.float32),
        lax.psum(shares[6].astype(jnp.bfloat16), "seq").astype(jnp.float32),
        lax.psum(shares[7].astype(jnp.bfloat16), "seq").astype(jnp.float32),
        lax.psum(shares[8].astype(jnp.bfloat16), "seq").astype(jnp.float32),
    )
    return (
        block_out,
        grad_input,
        summed[0],
        summed[1],
        summed[2],
        summed[3],
        summed[4],
        summed[5],
        summed[6],
        summed[7],
        summed[8],
    )


MESH = pl.DeviceIdType.MESH
SHORT = SIDE_S * SIDE_S + 1
WIDE = 256
LOW = jnp.bfloat16
F32 = jnp.float32
NEVER = -1e30

PLANS = "xyzyzxyyzxxyyxy"
ORDER = (
    (),
    (),
    (),
    (),
    (),
    (2, 42),
    (12,),
    (),
    (52, 22),
    (62,),
    (),
    (13,),
    (3,),
    (43,),
    (32,),
    (63, 53),
    (72,),
    (23,),
    (92,),
    (),
    (),
    (),
    (82,),
    (),
    (14, 102, 4, 44, 64, 33, 112, 54),
    (),
    (
        73, 24, 93, 122, 83, 15, 132, 103, 65, 34, 74, 113, 142, 152, 5, 45, 94, 55, 123, 84, 133,
        104, 35, 75, 143, 114, 25, 16, 66, 124, 153, 95, 134, 85, 144, 105, 115, 36, 76, 125, 154,
        135, 145, 116, 126, 155, 146,
    ),
)


def dot(left, right):
    return lax.dot_general(left, right, (((1,), (0,)), ((), ())), preferred_element_type=F32)


def dot_nt(left, right):
    return lax.dot_general(left, right, (((1,), (1,)), ((), ())), preferred_element_type=F32)


def dot_tn(left, right):
    return lax.dot_general(left, right, (((0,), (0,)), ((), ())), preferred_element_type=F32)


def rope_constants(rows):
    quarter = HD // 4
    freq = 10000.0 ** (-np.arange(quarter) / quarter)
    tables = []
    for side, length in ((SIDE_S, SIDE_S * SIDE_S + 1), (SIDE_L, SIDE_L * SIDE_L + 1)):
        place = np.arange(rows) - 1
        place = np.where((place >= 0) & (place < length - 1), place, 0)
        row = (place // side)[:, None] * freq
        col = (place % side)[:, None] * freq
        cosine = np.concatenate([np.cos(row), np.cos(row), np.cos(col), np.cos(col)], -1)
        sine = np.concatenate([-np.sin(row), np.sin(row), -np.sin(col), np.sin(col)], -1)
        tables += [np.concatenate([cosine, cosine], -1), np.concatenate([sine, sine], -1)]
    return np.stack(tables).astype(np.float32)


def swap_quarters(values):
    lane = lax.broadcasted_iota(jnp.int32, values.shape, 1)
    first = (lane % (HD // 2)) < HD // 4
    return jnp.where(
        first, pltpu.roll(values, 2 * HD - HD // 4, 1), pltpu.roll(values, HD // 4, 1)
    )


def fused(geo, *refs):
    rows_here, width, hidden_all = geo
    (
        lens, gain_a, gain_f, x_hbm, cot_hbm, tab_hbm,
        wq, wk, wv, wo, wg, wu, wd,
        bo_hbm, gi_hbm, fa_hbm, fd_hbm, fq_hbm, gain_hbm,
        x4, cot4, tab, wqkv_v, wo_v, wg_v, wu_v, wd_v,
        nrm, nrm_t, qkv, chance, mix_own, mix_in, mix, mix_t,
        mid, nf, nf_t, hid, hid_t, gg, gu, big,
        gnf_out, gnf_in, sb, rb, bo, bo_in, gb, gmx, ds_s, gqkv, sb2, rb2, gi, gi_in,
        gain_s, gain_x, gain_y, gain_z, gain_f_z, gain_c,
        pa, r1a, r2a, r3a, fa, pd, r1d, r2d, r3d, fd, pq, r1q, r2q, r3q, fq,
        sem_w, sem_in_s, sem_in_r, sem_core_s, sem_core_r, sem_gain_s, sem_gain_r, sem_o,
        sa_s, sa_r, sd_s, sd_r, sq_s, sq_r,
    ) = refs
    s = lax.axis_index("seq")
    i = lax.axis_index("items")
    y, c = s // 2, s % 2
    z, x = i // 2, i % 2
    rows = 4 * rows_here
    half = width // 2
    ff = hidden_all // 2
    pairs = half // 128
    step = rows_here
    fine = 32
    per = rows_here // step
    blocks = [(r0, min(256, rows - r0)) for r0 in range(0, rows, 256)]

    def device(y_to, c_to, z_to, x_to):
        return (y_to * 2 + c_to, z_to * 2 + x_to)

    sibling = device(y, 1 - c, z, x)
    y_dev = device(1 - y, c, z, x)
    x_dev = device(y, c, z, 1 - x)
    z_hi, z_lo = z // 2, z % 2
    near_z = device(y, c, z + 1 - 2 * z_lo, x)
    far_z = device(y, c, z + 2 - 4 * z_hi, x)

    started = []

    def send(src, dst, s_sem, r_sem, to):
        return pltpu.make_async_remote_copy(
            src_ref=src, dst_ref=dst, send_sem=s_sem, recv_sem=r_sem,
            device_id=to, device_id_type=MESH,
        )

    def weight_copies():
        copies = [pltpu.make_async_copy(tab_hbm, tab, sem_w.at[0])]
        mine = pl.ds(pl.multiple_of(c * half, half), half)
        for t, w in enumerate((wq, wk, wv)):
            copies.append(
                pltpu.make_async_copy(
                    w.at[:, mine], wqkv_v.at[:, pl.ds(t * half, half)], sem_w.at[1 + t]
                )
            )
        copies.append(pltpu.make_async_copy(wo, wo_v, sem_w.at[4]))
        for b in range(ff // 128):
            far = pl.ds(pl.multiple_of(256 * b + 128 * c, 128), 128)
            near = pl.ds(128 * b, 128)
            copies.append(pltpu.make_async_copy(wg.at[:, far], wg_v.at[:, near], sem_w.at[5 + 3 * b]))
            copies.append(pltpu.make_async_copy(wu.at[:, far], wu_v.at[:, near], sem_w.at[6 + 3 * b]))
            copies.append(pltpu.make_async_copy(wd.at[far], wd_v.at[near], sem_w.at[7 + 3 * b]))
        return copies

    weights = weight_copies()
    own_x = pltpu.make_async_copy(x_hbm.at[y], x4.at[s], sem_o.at[0])
    own_cot = pltpu.make_async_copy(cot_hbm.at[y], cot4.at[s], sem_o.at[1])
    own_x.start()
    for copy in weights[:4]:
        copy.start()

    barrier = pltpu.get_barrier_semaphore()
    for to in (sibling, y_dev, x_dev, near_z, far_z):
        pl.semaphore_signal(barrier, inc=1, device_id=to, device_id_type=MESH)
    pl.semaphore_wait(barrier, 5)

    s_y = (1 - y) * 2 + c
    across_x = send(x_hbm.at[1 - y], x4.at[s], sem_in_s.at[0], sem_in_r.at[0], y_dev)
    beside_x = send(x_hbm.at[y], x4.at[s], sem_in_s.at[1], sem_in_r.at[1], sibling)
    across_x.start()
    beside_x.start()
    across_c = send(cot_hbm.at[1 - y], cot4.at[s], sem_in_s.at[2], sem_in_r.at[2], y_dev)
    beside_c = send(cot_hbm.at[y], cot4.at[s], sem_in_s.at[3], sem_in_r.at[3], sibling)
    own_cot.start()
    for copy in weights[4:]:
        copy.start()
    relay_x = send(x4.at[s_y], x4.at[s_y], sem_in_s.at[4], sem_in_r.at[4], sibling)
    relay_c = send(cot4.at[s_y], cot4.at[s_y], sem_in_s.at[5], sem_in_r.at[5], sibling)

    length = lens[y]

    def norm_rows(piece):
        def one(b, carry):
            here = pl.ds(pl.multiple_of(b * step, step), step)
            values = x4[piece, here, :].astype(F32)
            scale = lax.rsqrt(jnp.mean(values * values, -1, keepdims=True) + epsilon)
            there = pl.ds(pl.multiple_of(piece * rows_here + b * step, step), step)
            nrm[there, :] = (values * scale * gain_a[...]).astype(LOW)
            return carry

        lax.fori_loop(0, per, one, 0)

    def project_rows(part):
        base = pl.multiple_of(part * 2 * rows_here, 32)
        here = pl.ds(base, 2 * rows_here)
        cosine = jnp.where(length == LONG, tab[2, here, :], tab[0, here, :])
        sine = jnp.where(length == LONG, tab[3, here, :], tab[1, here, :])
        for t in range(3):
            product = dot(nrm[here, :], wqkv_v[:, t * half : (t + 1) * half])
            for p in range(pairs):
                lanes = product[:, 128 * p : 128 * (p + 1)]
                if t < 2:
                    lanes = lanes * cosine + swap_quarters(lanes) * sine
                if t == 0:
                    lanes = lanes.astype(LOW).astype(F32) * HD ** (-0.5)
                qkv[t, here, 128 * p : 128 * (p + 1)] = lanes.astype(LOW)

    own_x.wait()
    norm_rows(s)
    beside_x.wait_recv()
    norm_rows(2 * y + 1 - c)
    for copy in weights[:4]:
        copy.wait()
    project_rows(y)
    across_x.wait_recv()
    relay_x.start()
    across_c.start()
    beside_c.start()
    norm_rows(s_y)
    relay_x.wait_recv()
    norm_rows(2 * (1 - y) + 1 - c)
    project_rows(1 - y)

    lane = lax.broadcasted_iota(jnp.int32, (1, 128), 1)
    left_head = lane < HD
    masks = [(lane // HD == n).astype(F32).astype(LOW) for n in range(2)]

    def mix_copy(pair):
        return send(
            mix_own.at[pair], mix_in.at[pair], sem_core_s.at[pair], sem_core_r.at[pair], sibling
        )

    tiles = blocks
    key = lax.broadcasted_iota(jnp.int32, (1, rows), 1)
    bias = jnp.where(key < length, 0.0, NEVER)

    def stacked(first, second):
        return jnp.concatenate([first, second], 0)

    def attend(pair, carry):
        lanes = pl.ds(pl.multiple_of(pair * 128, 128), 128)
        parts = []
        for k0, kb in tiles:
            query = qkv[0, k0:, lanes]
            part = dot_nt(stacked(query * masks[0], query * masks[1]), qkv[1, k0 : k0 + kb, lanes])
            parts.append(part + bias[:, k0 : k0 + kb] if k0 + kb > SHORT else part)
        for n in range(2):
            for r0, rb in blocks:
                scores = []
                for (k0, kb), part in zip(tiles, parts):
                    if k0 <= r0:
                        base = n * (rows - k0) + r0 - k0
                        here = part[base : base + rb]
                        if k0 == r0:
                            row = lax.broadcasted_iota(jnp.int32, here.shape, 0)
                            col = lax.broadcasted_iota(jnp.int32, here.shape, 1)
                            here = jnp.where(col <= row, here, NEVER)
                        scores.append((k0, kb, here))
                top = functools.reduce(jnp.maximum, [jnp.max(p, -1, keepdims=True) for _, _, p in scores])
                expo = [(k0, kb, jnp.exp(p - top)) for k0, kb, p in scores]
                inverse = 1.0 / sum(jnp.sum(p, -1, keepdims=True) for _, _, p in expo)
                for k0, kb, p in expo:
                    chance[pair * 2 + n, r0 : r0 + rb, k0 : k0 + kb] = (p * inverse).astype(LOW)
        outs = []
        for k0, kb in tiles:
            at = slice(k0, k0 + kb)
            low = stacked(chance[pair * 2, k0:, at], chance[pair * 2 + 1, k0:, at])
            outs.append(dot(low, qkv[2, at, lanes]))
        for r0, rb in blocks:
            both = []
            for n in range(2):
                at = [n * (rows - k0) + r0 - k0 for k0, _ in tiles if k0 <= r0]
                both.append(sum(out[b : b + rb] for b, out in zip(at, outs)))
            mix_own[pair, r0 : r0 + rb, :] = jnp.where(left_head, both[0], both[1]).astype(LOW)
        mix_copy(pair).start()
        return carry

    lax.fori_loop(0, pairs, attend, 0)

    across_c.wait_recv()
    relay_c.start()

    def turn_rows(src, dst):
        def one(b, carry):
            here = pl.ds(pl.multiple_of(b * 128, 128), 128)
            dst[:, here] = src[here, :].T
            return carry

        lax.fori_loop(0, rows // 128, one, 0)

    def place_mix(src, at):
        def one(p, carry):
            mix[:, pl.ds(pl.multiple_of(at * half + p * 128, 128), 128)] = src[p]
            return carry

        lax.fori_loop(0, pairs, one, 0)

    place_mix(mix_own, c)
    turn_rows(nrm, nrm_t)
    for p in range(pairs):
        mix_copy(p).wait_recv()
    place_mix(mix_in, 1 - c)

    weights[4].wait()

    def chunk(n, wide=WIDE):
        return pl.ds(pl.multiple_of(n * wide, wide), wide)

    def out_project(n, carry):
        mid[:, chunk(n)] = (
            dot(mix[...], wo_v[:, chunk(n)])
            + x4[:, :, chunk(n)].reshape(rows, WIDE).astype(F32)
        )
        return carry

    lax.fori_loop(0, width // WIDE, out_project, 0)

    def second_norm(b, carry):
        here = pl.ds(pl.multiple_of(b * step, step), step)
        values = mid[here, :]
        scale = lax.rsqrt(jnp.mean(values * values, -1, keepdims=True) + epsilon)
        nf[here, :] = (values * scale * gain_f[...]).astype(LOW)
        return carry

    lax.fori_loop(0, rows // step, second_norm, 0)
    turn_rows(nf, nf_t)
    for copy in weights[5:]:
        copy.wait()
    own_cot.wait()
    beside_c.wait_recv()
    relay_c.wait_recv()

    class Group:
        def __init__(self, parts, r1, r2, r3, fin, s_sem, r_sem):
            self.parts, self.r1, self.r2, self.r3, self.fin = parts, r1, r2, r3, fin
            self.s_sem, self.r_sem = s_sem, r_sem

        def copy(self, k, n, src, dst, to):
            return send(src, dst, self.s_sem.at[k, n], self.r_sem.at[k, n], to)

        def step1(self, k):
            self.hop(k, 0).start()

        def to_core(self, k):
            return self.copy(k, 5, self.fin.at[k, c], self.fin.at[k, c], sibling)

        def finish(self, k, own, new):
            for h in range(2):
                total = self.r1[own + (h,)].astype(F32) + self.r3[k, new + h].astype(F32)
                self.fin[k, c, h] = total.astype(LOW)
            self.to_core(k).start()

        def end(self, k):
            self.to_core(k).wait_recv()

        def sent(self, k):
            for n in range(self.hops):
                self.hop(k, n).wait_send()
            self.to_core(k).wait_send()

    def add(ref, at, other, of):
        ref[at] = (ref[at].astype(F32) + other[of].astype(F32)).astype(LOW)

    class XZY(Group):
        hops = 4

        def hop(self, k, n):
            r1, r2, r3 = self.r1, self.r2, self.r3
            if n == 0:
                return self.copy(k, n, self.parts.at[k, :, :, 1 - x], r1.at[k], x_dev)
            if n == 1:
                return self.copy(k, n, r1.at[k, :, 1 - z_lo], r2.at[k], near_z)
            if n == 2:
                return self.copy(k, n, r1.at[k, 1 - z_hi, z_lo], r3.at[k, pl.ds(0, 2)], far_z)
            return self.copy(k, n, r1.at[k, z_hi, z_lo], r3.at[k, pl.ds(2, 2)], y_dev)

        def step2(self, k):
            self.hop(k, 0).wait_recv()
            for lo in (1 - z_lo, z_lo):
                for hi in range(2):
                    for h in range(2):
                        add(self.r1, (k, hi, lo, h), self.parts, (k, hi, lo, x, h))
                if lo is not z_lo:
                    self.hop(k, 1).start()

        def step3(self, k):
            self.hop(k, 1).wait_recv()
            for hi in (1 - z_hi, z_hi):
                for h in range(2):
                    add(self.r1, (k, hi, z_lo, h), self.r2, (k, hi, h))
                if hi is not z_hi:
                    self.hop(k, 2).start()

        def step4(self, k):
            self.hop(k, 2).wait_recv()
            for h in range(2):
                add(self.r1, (k, z_hi, z_lo, h), self.r3, (k, h))
            self.hop(k, 3).start()

        def step5(self, k):
            self.hop(k, 3).wait_recv()
            self.finish(k, (k, z_hi, z_lo), 2)

    class ZXY(Group):
        hops = 4

        def hop(self, k, n):
            r1, r2, r3 = self.r1, self.r2, self.r3
            if n == 0:
                return self.copy(k, n, self.parts.at[k, :, 1 - z_lo], r1.at[k], near_z)
            if n == 1:
                return self.copy(k, n, r1.at[k, 1 - z_hi], r2.at[k], far_z)
            if n == 2:
                return self.copy(k, n, r1.at[k, z_hi, 1 - x], r3.at[k, pl.ds(0, 2)], x_dev)
            return self.copy(k, n, r1.at[k, z_hi, x], r3.at[k, pl.ds(2, 2)], y_dev)

        def step2(self, k):
            self.hop(k, 0).wait_recv()
            for hi in (1 - z_hi, z_hi):
                for xx in range(2):
                    for h in range(2):
                        add(self.r1, (k, hi, xx, h), self.parts, (k, hi, z_lo, xx, h))
                if hi is not z_hi:
                    self.hop(k, 1).start()

        def step3(self, k):
            self.hop(k, 1).wait_recv()
            for xx in (1 - x, x):
                for h in range(2):
                    add(self.r1, (k, z_hi, xx, h), self.r2, (k, xx, h))
                if xx is not x:
                    self.hop(k, 2).start()

        def step4(self, k):
            self.hop(k, 2).wait_recv()
            for h in range(2):
                add(self.r1, (k, z_hi, x, h), self.r3, (k, h))
            self.hop(k, 3).start()

        def step5(self, k):
            self.hop(k, 3).wait_recv()
            self.finish(k, (k, z_hi, x), 2)

    class YXZ(Group):
        hops = 5

        def hop(self, k, n):
            r1, r2, r3 = self.r1, self.r2, self.r3
            if n == 0:
                return self.copy(k, n, self.parts.at[k, :, :, :, 1 - y], r1.at[k], y_dev)
            if n == 1:
                return self.copy(k, n, r1.at[k, :, :, 1 - x], r2.at[k], x_dev)
            if n == 2:
                return self.copy(k, n, r2.at[k, :, 1 - z_lo], r3.at[k, pl.ds(0, 2)], near_z)
            if n == 3:
                return self.copy(k, n, r2.at[k, 1 - z_hi, z_lo], r3.at[k, 2], far_z)
            return self.copy(k, n, self.fin.at[k, c, y], self.fin.at[k, c, y], y_dev)

        def beside(self, k, n):
            at = self.fin.at[k, c, y] if n == 0 else self.fin.at[k, c, 1 - y]
            return self.copy(k, 5 + n, at, at, sibling)

        def step2(self, k):
            self.hop(k, 0).wait_recv()
            for xx in (1 - x, x):
                for hi in range(2):
                    for lo in range(2):
                        add(self.r1, (k, hi, lo, xx), self.parts, (k, hi, lo, xx, y))
                if xx is not x:
                    self.hop(k, 1).start()

        def step3(self, k):
            self.hop(k, 1).wait_recv()
            for lo in (1 - z_lo, z_lo):
                for hi in range(2):
                    add(self.r2, (k, hi, lo), self.r1, (k, hi, lo, x))
                if lo is not z_lo:
                    self.hop(k, 2).start()

        def step4(self, k):
            self.hop(k, 2).wait_recv()
            for hi in (1 - z_hi, z_hi):
                add(self.r2, (k, hi, z_lo), self.r3, (k, hi))
                if hi is not z_hi:
                    self.hop(k, 3).start()

        def step5(self, k):
            self.hop(k, 3).wait_recv()
            total = self.r2[k, z_hi, z_lo].astype(F32) + self.r3[k, 2].astype(F32)
            self.fin[k, c, y] = total.astype(LOW)
            self.hop(k, 4).start()
            self.beside(k, 0).start()

        def step6(self, k):
            self.hop(k, 4).wait_recv()
            self.beside(k, 1).start()

        def end(self, k):
            for n in range(2):
                self.beside(k, n).wait_recv()

        def sent(self, k):
            for n in range(self.hops):
                self.hop(k, n).wait_send()
            for n in range(2):
                self.beside(k, n).wait_send()

    class Gains:
        def hop(self, k, n):
            src = (gain_s, gain_x, gain_y, gain_z, gain_s)[n]
            dst = (gain_x, gain_y, gain_z, gain_f_z, gain_c)[n]
            to = (x_dev, y_dev, near_z, far_z, sibling)[n]
            return send(src, dst, sem_gain_s.at[n], sem_gain_r.at[n], to)

        def step1(self, k):
            self.hop(k, 0).start()

        def step2(self, k):
            self.hop(k, 0).wait()
            gain_x[...] = gain_s[...] + gain_x[...]
            self.hop(k, 1).start()

        def step3(self, k):
            self.hop(k, 1).wait()
            gain_y[...] = gain_x[...] + gain_y[...]
            self.hop(k, 2).start()

        def step4(self, k):
            self.hop(k, 2).wait()
            gain_z[...] = gain_y[...] + gain_z[...]
            self.hop(k, 3).start()

        def step5(self, k):
            self.hop(k, 3).wait()
            gain_s[...] = gain_z[...] + gain_f_z[...]
            self.hop(k, 4).start()

        def end(self, k):
            self.hop(k, 4).wait()
            top = lax.broadcasted_iota(jnp.int32, gain_s.shape, 0) == 0
            total = gain_s[...] + jnp.where(top, gain_c[...], 0.0)
            gain_c[...] = pltpu.roll(total, lax.rem(8 - i, 8) * (width // 8), 1)

        def sent(self, k):
            pass

    buffers_a = (pa, r1a, r2a, r3a, fa, sa_s, sa_r)
    buffers_d = (pd, r1d, r2d, r3d, fd, sd_s, sd_r)
    buffers_q = (pq, r1q, r2q, r3q, fq, sq_s, sq_r)
    kinds = {"x": XZY, "y": YXZ, "z": ZXY}
    chunks = [(kinds[kind](*buffers_a), n) for n, kind in enumerate(PLANS[:8])]
    chunks += [(kinds[kind](*buffers_d), n) for n, kind in enumerate(PLANS[8:11])]
    chunks += [(kinds[kind](*buffers_q), n) for n, kind in enumerate(PLANS[11:])]
    chunks += [(Gains(), 0)]
    slots = iter(ORDER)

    def first(chunk):
        group, k = chunks[chunk]
        group.step1(k)

    def turn():
        for code in next(slots):
            group, k = chunks[code // 10]
            getattr(group, f"step{code % 10}")(k)

    chunks_f = ff // WIDE
    chunks_w = width // WIDE

    def feed(n, carry):
        at = chunk(n)
        big[:, 0:WIDE] = dot(nf[...], wg_v[:, at])
        big[:, WIDE : 2 * WIDE] = dot(nf[...], wu_v[:, at])
        big[:, 2 * WIDE : 3 * WIDE] = dot_nt(cot4[...].reshape(rows, width), wd_v[at, :])

        def one(b, inner):
            here = pl.ds(pl.multiple_of(b * fine, fine), fine)
            gate = big[here, 0:WIDE]
            up = big[here, WIDE : 2 * WIDE]
            back = big[here, 2 * WIDE : 3 * WIDE]
            sigma = 0.5 * jnp.tanh(0.5 * gate) + 0.5
            silu = gate * sigma
            hid[here, at] = (silu * up).astype(LOW)
            gg[here, at] = (back * up * (sigma + silu * (1.0 - sigma))).astype(LOW)
            gu[here, at] = (back * silu).astype(LOW)
            return inner

        lax.fori_loop(0, rows // fine, one, 0, unroll=5)
        shape = pa.shape[1:]
        pa[n] = dot(nf_t[...], gg[:, at]).reshape(shape).astype(LOW)
        first(n)
        pa[n + chunks_f] = dot(nf_t[...], gu[:, at]).reshape(shape).astype(LOW)
        first(n + chunks_f)
        hid_t[at, :] = hid[:, at].T
        return carry

    for n in range(chunks_f):
        turn()
        feed(n, 0)
    turn()

    def gnf_copy(n):
        return send(
            gnf_out.at[n], gnf_in.at[n], sem_core_s.at[pairs + n], sem_core_r.at[pairs + n], sibling
        )

    def back_ffn(n, carry):
        partial = dot_nt(gg[...], wg_v[chunk(n), :]) + dot_nt(gu[...], wu_v[chunk(n), :])
        big[:, chunk(n)] = partial
        gnf_out[n] = partial.astype(LOW)
        gnf_copy(n).start()
        return carry

    for n in range(chunks_w):
        back_ffn(n, 0)
        turn()

    def down(n, carry):
        big[:, chunk(n + chunks_w)] = dot(hid[...], wd_v[:, chunk(n)])
        return carry

    lax.fori_loop(0, chunks_w, down, 0)
    n_core = pairs + chunks_w
    bo_copy = send(sb, rb, sem_core_s.at[n_core], sem_core_r.at[n_core], sibling)
    far = slice(width, 2 * width)

    def for_rows(core, fn):
        for yy in range(2):
            def one(b, carry, yy=yy):
                base = pl.multiple_of((2 * yy + core) * rows_here + b * step, step)
                fn(yy, b, pl.ds(base, step), pl.ds(pl.multiple_of(b * step, step), step))
                return carry

            lax.fori_loop(0, per, one, 0)

    def pack_bo(yy, b, here, there):
        sb[yy, there, :] = big[here, far].astype(LOW)

    for_rows(1 - c, pack_bo)
    bo_copy.start()

    for n in range(chunks_w):
        turn()
        at = slice(n * WIDE, (n + 1) * WIDE)
        pd[n] = (
            dot(hid_t[...], cot4[:, :, at].reshape(rows, WIDE)).reshape(pd.shape[1:]).astype(LOW)
        )
        first(8 + n)

    turn()
    bo_copy.wait_recv()

    def finish_bo(yy, b, here, there):
        bo[yy, there, :] = (mid[here, :] + big[here, far] + rb[yy, there, :].astype(F32)).astype(LOW)

    for_rows(c, finish_bo)
    bo_across = send(bo.at[1 - y], bo_in, sem_in_s.at[6], sem_in_r.at[6], y_dev)
    bo_across.start()

    turn()
    for n in range(chunks_w):
        gnf_copy(n).wait_recv()

    def middle_back(b, total):
        here = pl.ds(pl.multiple_of(b * step, step), step)
        values = mid[here, :]
        grad = big[here, 0:width] + jnp.concatenate(
            [gnf_in[n, here, :].astype(F32) for n in range(chunks_w)], -1
        )
        scale = lax.rsqrt(jnp.mean(values * values, -1, keepdims=True) + epsilon)
        unit = values * scale
        total = total + (grad * unit).reshape(step // 8, 8, width).sum(0)
        scaled = grad * gain_f[...]
        inner = jnp.mean(scaled * unit, -1, keepdims=True)
        out = cot4[b // per, pl.ds(pl.multiple_of(lax.rem(b, per) * step, step), step), :].astype(F32)
        out = out + scale * (scaled - unit * inner)
        mid[here, :] = out
        gb[here, :] = out.astype(LOW)
        return total

    total_f = lax.fori_loop(0, rows // step, middle_back, jnp.zeros((8, width), F32))

    turn()
    turn_rows(mix, mix_t)
    mine = pl.ds(pl.multiple_of(c * half, half), half)
    pq[0] = dot(mix_t[...], gb[:, mine]).reshape(pq.shape[1:]).astype(LOW)
    first(11)
    gmx[...] = dot_nt(gb[...], wo_v[mine, :]).astype(LOW)

    def query_back(pair):
        lanes = slice(pair * 128, pair * 128 + 128)
        grads = []
        for k0, kb in tiles:
            grad = gmx[k0:, lanes]
            grads.append(
                dot_nt(stacked(grad * masks[0], grad * masks[1]), qkv[2, k0 : k0 + kb, lanes])
            )
        for n in range(2):
            for r0, rb in blocks:
                both = []
                for (k0, kb), grad in zip(tiles, grads):
                    if k0 <= r0:
                        base = n * (rows - k0) + r0 - k0
                        prob = chance[pair * 2 + n, r0 : r0 + rb, k0 : k0 + kb].astype(F32)
                        both.append((slice(k0, k0 + kb), prob, grad[base : base + rb] * prob))
                inner = sum(jnp.sum(each, -1, keepdims=True) for _, _, each in both)
                for at, prob, each in both:
                    ds_s[n, r0 : r0 + rb, at] = (each - prob * inner).astype(LOW)
        outs = []
        for k0, kb in tiles:
            at = slice(k0, k0 + kb)
            outs.append(dot(stacked(ds_s[0, k0:, at], ds_s[1, k0:, at]), qkv[1, at, lanes]))
        for r0, rb in blocks:
            both = []
            for n in range(2):
                at = [n * (rows - k0) + r0 - k0 for k0, _ in tiles if k0 <= r0]
                both.append(sum(out[b : b + rb] for b, out in zip(at, outs)))
            big[r0 : r0 + rb, 0:128] = jnp.where(left_head, both[0], both[1])

    def keys_back(pair):
        lanes = slice(pair * 128, pair * 128 + 128)

        def beside(first, second):
            return jnp.concatenate([first, second], 1)

        for k0, kb in tiles:
            at = slice(k0, k0 + kb)
            out = dot_tn(beside(ds_s[0, k0:, at], ds_s[1, k0:, at]), qkv[0, k0:, lanes])
            big[at, 128:256] = jnp.where(left_head, out[:kb], out[kb:])
            low = beside(chance[pair * 2, k0:, at], chance[pair * 2 + 1, k0:, at])
            out = dot_tn(low, gmx[k0:, lanes])
            big[at, 256:384] = jnp.where(left_head, out[:kb], out[kb:])

        def one(b, inner):
            here = pl.ds(pl.multiple_of(b * 64, 64), 64)
            cosine = jnp.where(length == LONG, tab[2, here, :], tab[0, here, :])
            sine = jnp.where(length == LONG, tab[3, here, :], tab[1, here, :])
            for t in range(3):
                values = big[here, 128 * t : 128 * (t + 1)]
                if t == 0:
                    values = values * HD ** (-0.5)
                if t < 2:
                    values = values * cosine - swap_quarters(values) * sine
                gqkv[here, t * half + pair * 128 : t * half + pair * 128 + 128] = values.astype(LOW)
            return inner

        lax.fori_loop(0, rows // 64, one, 0, unroll=5)

    for pair in range(pairs):
        turn()
        query_back(pair)
        turn()
        keys_back(pair)

    for t in range(3):
        turn()
        pq[1 + t] = (
            dot(nrm_t[...], gqkv[:, t * half : (t + 1) * half]).reshape(pq.shape[1:]).astype(LOW)
        )
        first(12 + t)

    turn()

    def back_attn(n, carry):
        big[:, chunk(n)] = dot_nt(gqkv[...], wqkv_v[chunk(n), :])
        return carry

    lax.fori_loop(0, chunks_w, back_attn, 0)
    turn()

    def pack_gi(yy, b, here, there):
        sb2[yy, there, :] = big[here, 0:width].astype(LOW)

    for_rows(1 - c, pack_gi)
    gi_copy = send(sb2, rb2, sem_core_s.at[n_core + 1], sem_core_r.at[n_core + 1], sibling)
    gi_copy.start()

    def gain_back(b, total):
        here = pl.ds(pl.multiple_of(b * step, step), step)
        values = x4[b // per, pl.ds(pl.multiple_of(lax.rem(b, per) * step, step), step), :].astype(F32)
        scale = lax.rsqrt(jnp.mean(values * values, -1, keepdims=True) + epsilon)
        return total + (big[here, 0:width] * (values * scale)).reshape(step // 8, 8, width).sum(0)

    total_a = lax.fori_loop(0, rows // step, gain_back, jnp.zeros((8, width), F32))
    row = lax.broadcasted_iota(jnp.int32, (8, width), 0)
    gain_s[...] = jnp.where(
        row == 0, jnp.sum(total_a, 0, keepdims=True), jnp.sum(total_f, 0, keepdims=True)
    )
    first(15)
    turn()
    gi_copy.wait_recv()

    def finish_gi(yy, b, here, there):
        values = x4[2 * yy + c, there, :].astype(F32)
        scale = lax.rsqrt(jnp.mean(values * values, -1, keepdims=True) + epsilon)
        unit = values * scale
        scaled = (big[here, 0:width] + rb2[yy, there, :].astype(F32)) * gain_a[...]
        inner = jnp.mean(scaled * unit, -1, keepdims=True)
        gi[yy, there, :] = (mid[here, :] + scale * (scaled - unit * inner)).astype(LOW)

    for_rows(c, finish_gi)
    gi_across = send(gi.at[1 - y], gi_in, sem_in_s.at[7], sem_in_r.at[7], y_dev)
    gi_across.start()

    outs = [
        pltpu.make_async_copy(bo.at[y], bo_hbm.at[y], sem_o.at[6]),
        pltpu.make_async_copy(gi.at[y], gi_hbm.at[y], sem_o.at[7]),
        pltpu.make_async_copy(bo_in, bo_hbm.at[1 - y], sem_o.at[8]),
        pltpu.make_async_copy(gi_in, gi_hbm.at[1 - y], sem_o.at[9]),
        pltpu.make_async_copy(fa, fa_hbm, sem_o.at[2]),
        pltpu.make_async_copy(fd, fd_hbm, sem_o.at[3]),
        pltpu.make_async_copy(fq, fq_hbm, sem_o.at[4]),
        pltpu.make_async_copy(gain_c, gain_hbm, sem_o.at[5]),
    ]
    outs[0].start()
    outs[1].start()
    turn()
    bo_across.wait_recv()
    outs[2].start()
    gi_across.wait_recv()
    outs[3].start()
    for n, part in enumerate((chunks[:8], chunks[8:11], chunks[11:15], chunks[15:])):
        for group, k in part:
            group.end(k)
        outs[4 + n].start()
    for copy in outs:
        copy.wait()

    for copy in (across_x, beside_x, across_c, beside_c, relay_x, relay_c, bo_across, gi_across):
        copy.wait_send()
    for p in range(pairs):
        mix_copy(p).wait_send()
    for n in range(chunks_w):
        gnf_copy(n).wait_send()
    bo_copy.wait_send()
    gi_copy.wait_send()
    for group, k in chunks:
        group.sent(k)


def spread(chunks_f, share, *refs):
    fa_far, fd_far, fq_far, bo, gi, gains_far = refs[:6]
    outs, (fa, fd, fq, gains), stage, sem_in, sem_out = refs[6:17], refs[17:21], refs[21:28], *refs[28:]
    bo_out, gi_out, da, df = outs[0], outs[1], outs[2], outs[7]
    ends = outs[3:7] + outs[8:]
    dq, dk, dv, do, dg, du, dd = stage
    near = [
        pltpu.make_async_copy(a, b, sem_in.at[n])
        for n, (a, b) in enumerate(
            [(fa_far.at[:chunks_f], fa.at[:chunks_f]), (fa_far.at[chunks_f:], fa.at[chunks_f:])]
            + [(fd_far, fd), (fq_far, fq), (gains_far, gains), (bo, bo_out), (gi, gi_out)]
        )
    ]
    for copy in near:
        copy.start()
    done = [pltpu.make_async_copy(a, b, sem_out.at[n]) for n, (a, b) in enumerate(zip(stage, ends))]
    rows, half, deep = fa.shape[3], fq.shape[4], fd.shape[3]
    halves = [(core, h, slice(h * rows, (h + 1) * rows)) for core in range(2) for h in range(2)]

    for first, ref, copy in ((0, dg, 0), (chunks_f, du, 1)):
        near[copy].wait()
        for core, h, at in halves:
            for n in range(chunks_f):
                for b in range(WIDE // 128):
                    far = 256 * (n * (WIDE // 128) + b) + 128 * core
                    ref[at, far : far + 128] = fa[
                        n + first, core, h, :, 128 * b : 128 * (b + 1)
                    ].astype(F32)
        done[4 + copy].start()
    near[2].wait()
    for core, h, _ in halves:
        at = slice((2 * core + h) * deep, (2 * core + h + 1) * deep)
        for n in range(fd.shape[0]):
            dd[at, WIDE * n : WIDE * (n + 1)] = fd[n, core, h].astype(F32)
    done[6].start()
    near[3].wait()
    for n, (ref, end) in enumerate(((do, 3), (dq, 0), (dk, 1), (dv, 2))):
        for core, h, at in halves:
            ref[at, core * half : (core + 1) * half] = fq[n, core, h].astype(F32)
        done[end].start()
    near[4].wait()
    da[...] = gains[0, 0:share]
    df[...] = gains[1, 0:share]
    near[5].wait()
    near[6].wait()
    for copy in done:
        copy.wait()


def item_per_chip(
    block_in, lengths, gain_attn, w_query, w_key, w_value, w_out, gain_ffn, w_gate, w_up, w_down,
    cotangent,
):
    _, rows_here, width = block_in.shape
    hidden_all = w_gate.shape[1]
    rows = rows_here * lax.axis_size("seq")
    shares = lax.axis_size("items")
    half, ff = width // 2, hidden_all // 2
    pairs = half // 128
    chunks_f, chunks_w = ff // WIDE, width // WIDE
    thin, deep = width // shares // 2, ff // shares // 2
    tables = jnp.asarray(rope_constants(rows))
    any_ = pl.BlockSpec(memory_space=pl.ANY)
    vmem = pl.BlockSpec(memory_space=pltpu.VMEM)

    def group(n, r, w):
        return [
            pltpu.VMEM((n, 2, 2, 2, 2, r, w), LOW),
            pltpu.VMEM((n, 2, 2, 2, r, w), LOW),
            pltpu.VMEM((n, 2, 2, r, w), LOW),
            pltpu.VMEM((n, 4, r, w), LOW),
            pltpu.VMEM((n, 2, 2, r, w), LOW),
        ]

    def low(*shape):
        return pltpu.VMEM(shape, LOW)

    def full(*shape):
        return pltpu.VMEM(shape, F32)

    dma = pltpu.SemaphoreType.DMA
    scratch = [
        low(4, rows_here, width), low(4, rows_here, width), full(4, rows, 128),
        low(width, 3 * half), low(width, width), low(width, ff), low(width, ff), low(ff, width),
        low(rows, width), low(width, rows), low(3, rows, half), low(2 * pairs, rows, rows),
        low(pairs, rows, 128), low(pairs, rows, 128), low(rows, width), low(width, rows),
        full(rows, width), low(rows, width), low(width, rows), low(rows, ff), low(ff, rows),
        low(rows, ff), low(rows, ff), full(rows, 2 * width),
        low(chunks_w, rows, WIDE), low(chunks_w, rows, WIDE),
        low(2, rows_here, width), low(2, rows_here, width),
        low(2, rows_here, width), low(rows_here, width),
        low(rows, width), low(rows, half), low(2, rows, rows), low(rows, 3 * half),
        low(2, rows_here, width), low(2, rows_here, width),
        low(2, rows_here, width), low(rows_here, width),
        full(8, width), full(8, width), full(8, width), full(8, width), full(8, width), full(8, width),
    ]
    scratch += group(2 * chunks_f, thin, WIDE) + group(chunks_w, deep, WIDE) + group(4, thin, half)
    scratch += [
        dma((5 + 3 * (ff // 128),)), dma((8,)), dma((8,)),
        dma((pairs + chunks_w + 2,)), dma((pairs + chunks_w + 2,)), dma((6,)), dma((6,)), dma((10,)),
        dma((2 * chunks_f, 8)), dma((2 * chunks_f, 8)), dma((chunks_w, 8)), dma((chunks_w, 8)),
        dma((4, 8)), dma((4, 8)),
    ]
    shape = jax.ShapeDtypeStruct
    bo, gi, fa, fd, fq, gains = pl.pallas_call(
        functools.partial(fused, (rows_here, width, hidden_all)),
        out_shape=(
            shape(block_in.shape, LOW), shape(block_in.shape, LOW),
            shape((2 * chunks_f, 2, 2, thin, WIDE), LOW), shape((chunks_w, 2, 2, deep, WIDE), LOW),
            shape((4, 2, 2, thin, half), LOW), shape((8, width), F32),
        ),
        in_specs=[pl.BlockSpec(memory_space=pltpu.SMEM), vmem, vmem] + [any_] * 10,
        out_specs=(any_,) * 6,
        scratch_shapes=scratch,
        compiler_params=pltpu.CompilerParams(
            collective_id=0, has_side_effects=True, vmem_limit_bytes=63 * 2**20
        ),
        name="block",
    )(
        lengths, gain_attn, gain_ffn, block_in, cotangent, tables,
        w_query, w_key, w_value, w_out, w_gate, w_up, w_down,
    )
    thick = (width // shares, width)
    made = (fa, fd, fq, bo, gi, gains)
    share = width // shares
    bo, gi, da, dq, dk, dv, do, df, dg, du, dd = pl.pallas_call(
        functools.partial(spread, chunks_f, share),
        out_shape=(
            shape(block_in.shape, LOW), shape(block_in.shape, LOW), shape((share,), F32),
            shape(thick, F32), shape(thick, F32), shape(thick, F32), shape(thick, F32),
            shape((share,), F32),
            shape((width // shares, hidden_all), F32), shape((width // shares, hidden_all), F32),
            shape((hidden_all // shares, width), F32),
        ),
        in_specs=[any_] * 6,
        out_specs=(vmem,) * 3 + (any_,) * 4 + (vmem,) + (any_,) * 3,
        scratch_shapes=[pltpu.VMEM(a.shape, a.dtype) for a in (fa, fd, fq, gains)]
        + [pltpu.VMEM(thick, F32)] * 4
        + [pltpu.VMEM((width // shares, hidden_all), F32)] * 2
        + [pltpu.VMEM((hidden_all // shares, width), F32), dma((7,)), dma((7,))],
        compiler_params=pltpu.CompilerParams(vmem_limit_bytes=60 * 2**20),
        name="spread",
    )(*made)
    return bo, gi, da, dq, dk, dv, do, df, dg, du, dd


def solution(mesh):
    fits = mesh.shape["seq"] == 4 and mesh.shape["items"] == 8
    return jax.shard_map(
        item_per_chip if fits else body,
        mesh=mesh,
        in_specs=(P("items", "seq", None), P("items")) + (P(),) * 9 + (P("items", "seq", None),),
        out_specs=(
            (P("items", "seq", None),) * 2
            + (P("items"),) + (P("items", None),) * 4
            + (P("items"),) + (P("items", None),) * 3
        ),
        check_vma=False,
    )
```

```python
import functools

import jax
import jax.numpy as jnp
import numpy as np
from jax import lax
from jax.experimental import pallas as pl
from jax.experimental.pallas import tpu as pltpu
from jax.sharding import PartitionSpec as P

HD = 64
SIDE_S = 16
SIDE_L = 24
LONG = 577


epsilon = 1e-05


def grid_places(lengths, rows):
    side = jnp.where(lengths == LONG, SIDE_L, SIDE_S).astype(jnp.int32)[:, None]
    place = rows[None, :] - 1
    valid = (place >= 0) & (rows[None, :] < lengths[:, None])
    place = jnp.where(valid, place, 0)
    return (place // side, place % side)


def rotary_tables(lengths, rows):
    grid_row, grid_col = grid_places(lengths, rows)
    quarter = HD // 4
    freq = 10000.0 ** (-jnp.arange(quarter, dtype=jnp.float32) / quarter)
    angle_row = grid_row[..., None].astype(jnp.float32) * freq
    angle_col = grid_col[..., None].astype(jnp.float32) * freq
    cosine = jnp.concatenate(
        [jnp.cos(angle_row), jnp.cos(angle_row), jnp.cos(angle_col), jnp.cos(angle_col)], -1
    )
    sine = jnp.concatenate(
        [jnp.sin(angle_row), jnp.sin(angle_row), jnp.sin(angle_col), jnp.sin(angle_col)], -1
    )
    return (cosine[:, :, None, :], sine[:, :, None, :])


def turn(values):
    quarter = HD // 4
    first = values[..., 0:quarter]
    second = values[..., quarter : 2 * quarter]
    third = values[..., 2 * quarter : 3 * quarter]
    fourth = values[..., 3 * quarter :]
    return jnp.concatenate([-second, first, -fourth, third], -1)


def project(left, right):
    return jnp.einsum("ird,de->ire", left, right, preferred_element_type=jnp.float32)


def back_project(grad, weight):
    return jnp.einsum("ire,de->ird", grad, weight, preferred_element_type=jnp.float32)


def weight_grad(left, right):
    return jnp.einsum("ird,ire->de", left, right, preferred_element_type=jnp.float32)


def norm_back(grad_normed, unit, scale, gain):
    scaled = grad_normed * gain
    return scale * (scaled - unit * jnp.mean(scaled * unit, -1, keepdims=True))


def body(
    block_in,
    lengths,
    gain_attn,
    w_query,
    w_key,
    w_value,
    w_out,
    gain_ffn,
    w_gate,
    w_up,
    w_down,
    cotangent,
):
    count, rows_here, width = block_in.shape
    heads = width // HD
    length_all = rows_here * lax.axis_size("seq")
    factor = HD ** (-0.5)
    query_rows = lax.axis_index("seq") * rows_here + jnp.arange(rows_here, dtype=jnp.int32)
    key_rows = jnp.arange(length_all, dtype=jnp.int32)
    cosine, sine = rotary_tables(lengths, query_rows)
    allowed = (key_rows[None, None, :] <= query_rows[None, :, None]) & (
        key_rows[None, None, :] < lengths[:, None, None]
    )

    def heads_of(array):
        return array.reshape(array.shape[0], array.shape[1], heads, HD)

    def attention_scores(query, keys_all):
        raw = (
            jnp.einsum(
                "irhe,iphe->ihrp", query, heads_of(keys_all), preferred_element_type=jnp.float32
            )
            * factor
        )
        return jnp.where(allowed[:, None], raw, -1e30)

    source = block_in.astype(jnp.float32)
    scale_attn = lax.rsqrt(jnp.mean(source * source, -1, keepdims=True) + epsilon)
    unit_attn = source * scale_attn
    normed = (unit_attn * gain_attn).astype(jnp.bfloat16)
    query_pre = heads_of(project(normed, w_query))
    keys_pre = heads_of(project(normed, w_key))
    query = (query_pre * cosine + turn(query_pre) * sine).astype(jnp.bfloat16)
    keys = (
        (keys_pre * cosine + turn(keys_pre) * sine)
        .astype(jnp.bfloat16)
        .reshape(count, rows_here, width)
    )
    values = project(normed, w_value).astype(jnp.bfloat16)
    keys_all, values_all = (
        lax.all_gather(keys, "seq", axis=1, tiled=True),
        lax.all_gather(values, "seq", axis=1, tiled=True),
    )
    scores = attention_scores(query, keys_all)
    top = jnp.max(scores, -1, keepdims=True)
    expo = jnp.exp(scores - top)
    summed = jnp.sum(expo, -1, keepdims=True)
    chance = expo / summed
    log_total = top + jnp.log(summed)
    mixed = (
        jnp.einsum(
            "ihrp,iphe->irhe",
            chance.astype(jnp.bfloat16),
            heads_of(values_all),
            preferred_element_type=jnp.float32,
        )
        .reshape(count, rows_here, width)
        .astype(jnp.bfloat16)
    )
    middle = source + project(mixed, w_out)
    scale_ffn = lax.rsqrt(jnp.mean(middle * middle, -1, keepdims=True) + epsilon)
    unit_ffn = middle * scale_ffn
    normed_ffn = (unit_ffn * gain_ffn).astype(jnp.bfloat16)
    gate = project(normed_ffn, w_gate)
    up = project(normed_ffn, w_up)
    sigma = jax.nn.sigmoid(gate)
    hidden = (gate * sigma * up).astype(jnp.bfloat16)
    block_out = (middle + project(hidden, w_down)).astype(jnp.bfloat16)
    incoming = cotangent.astype(jnp.float32)
    grad_w_down = weight_grad(hidden, cotangent)
    grad_hidden = back_project(cotangent, w_down)
    grad_gate = (grad_hidden * up * sigma * (1.0 + gate * (1.0 - sigma))).astype(jnp.bfloat16)
    grad_up = (grad_hidden * gate * sigma).astype(jnp.bfloat16)
    grad_w_gate = weight_grad(normed_ffn, grad_gate)
    grad_w_up = weight_grad(normed_ffn, grad_up)
    grad_normed_ffn = back_project(grad_gate, w_gate) + back_project(grad_up, w_up)
    grad_gain_ffn = jnp.sum(grad_normed_ffn * unit_ffn, axis=(0, 1))
    grad_middle = incoming + norm_back(grad_normed_ffn, unit_ffn, scale_ffn, gain_ffn)
    grad_branch = grad_middle.astype(jnp.bfloat16)
    grad_w_out = weight_grad(mixed, grad_branch)
    grad_mixed = heads_of(back_project(grad_branch, w_out)).astype(jnp.bfloat16)
    keys_back, values_back = (keys_all, values_all)
    chance_back = jnp.exp(attention_scores(query, keys_back) - log_total)
    grad_chance = jnp.einsum(
        "irhe,iphe->ihrp", grad_mixed, heads_of(values_back), preferred_element_type=jnp.float32
    )
    inner = jnp.sum(grad_chance * chance_back, -1, keepdims=True)
    grad_scores = (chance_back * (grad_chance - inner)).astype(jnp.bfloat16)
    grad_query = (
        jnp.einsum(
            "ihrp,iphe->irhe", grad_scores, heads_of(keys_back), preferred_element_type=jnp.float32
        )
        * factor
    )
    grad_values_sum = jnp.einsum(
        "ihrp,irhe->iphe",
        chance_back.astype(jnp.bfloat16),
        grad_mixed,
        preferred_element_type=jnp.float32,
    )
    grad_keys_sum = (
        jnp.einsum("ihrp,irhe->iphe", grad_scores, query, preferred_element_type=jnp.float32)
        * factor
    )
    grad_keys, grad_values = (
        lax.psum_scatter(
            grad_keys_sum.reshape(count, length_all, width).astype(jnp.bfloat16),
            "seq",
            scatter_dimension=1,
            tiled=True,
        ).astype(jnp.float32),
        lax.psum_scatter(
            grad_values_sum.reshape(count, length_all, width).astype(jnp.bfloat16),
            "seq",
            scatter_dimension=1,
            tiled=True,
        ).astype(jnp.float32),
    )
    grad_query_pre = (
        (grad_query * cosine - turn(grad_query * sine))
        .reshape(count, rows_here, width)
        .astype(jnp.bfloat16)
    )
    grad_keys_heads = heads_of(grad_keys)
    grad_keys_pre = (
        (grad_keys_heads * cosine - turn(grad_keys_heads * sine))
        .reshape(count, rows_here, width)
        .astype(jnp.bfloat16)
    )
    grad_values_pre = grad_values.astype(jnp.bfloat16)
    grad_w_query = weight_grad(normed, grad_query_pre)
    grad_w_key = weight_grad(normed, grad_keys_pre)
    grad_w_value = weight_grad(normed, grad_values_pre)
    grad_normed = (
        back_project(grad_query_pre, w_query)
        + back_project(grad_keys_pre, w_key)
        + back_project(grad_values_pre, w_value)
    )
    grad_gain_attn = jnp.sum(grad_normed * unit_attn, axis=(0, 1))
    grad_input = (grad_middle + norm_back(grad_normed, unit_attn, scale_attn, gain_attn)).astype(
        jnp.bfloat16
    )
    shares = (
        lax.psum_scatter(
            grad_gain_attn.astype(jnp.bfloat16), "items", scatter_dimension=0, tiled=True
        ).astype(jnp.float32),
        lax.psum_scatter(
            grad_w_query.astype(jnp.bfloat16), "items", scatter_dimension=0, tiled=True
        ).astype(jnp.float32),
        lax.psum_scatter(
            grad_w_key.astype(jnp.bfloat16), "items", scatter_dimension=0, tiled=True
        ).astype(jnp.float32),
        lax.psum_scatter(
            grad_w_value.astype(jnp.bfloat16), "items", scatter_dimension=0, tiled=True
        ).astype(jnp.float32),
        lax.psum_scatter(
            grad_w_out.astype(jnp.bfloat16), "items", scatter_dimension=0, tiled=True
        ).astype(jnp.float32),
        lax.psum_scatter(
            grad_gain_ffn.astype(jnp.bfloat16), "items", scatter_dimension=0, tiled=True
        ).astype(jnp.float32),
        lax.psum_scatter(
            grad_w_gate.astype(jnp.bfloat16), "items", scatter_dimension=0, tiled=True
        ).astype(jnp.float32),
        lax.psum_scatter(
            grad_w_up.astype(jnp.bfloat16), "items", scatter_dimension=0, tiled=True
        ).astype(jnp.float32),
        lax.psum_scatter(
            grad_w_down.astype(jnp.bfloat16), "items", scatter_dimension=0, tiled=True
        ).astype(jnp.float32),
    )
    summed = (
        lax.psum(shares[0].astype(jnp.bfloat16), "seq").astype(jnp.float32),
        lax.psum(shares[1].astype(jnp.bfloat16), "seq").astype(jnp.float32),
        lax.psum(shares[2].astype(jnp.bfloat16), "seq").astype(jnp.float32),
        lax.psum(shares[3].astype(jnp.bfloat16), "seq").astype(jnp.float32),
        lax.psum(shares[4].astype(jnp.bfloat16), "seq").astype(jnp.float32),
        lax.psum(shares[5].astype(jnp.bfloat16), "seq").astype(jnp.float32),
        lax.psum(shares[6].astype(jnp.bfloat16), "seq").astype(jnp.float32),
        lax.psum(shares[7].astype(jnp.bfloat16), "seq").astype(jnp.float32),
        lax.psum(shares[8].astype(jnp.bfloat16), "seq").astype(jnp.float32),
    )
    return (
        block_out,
        grad_input,
        summed[0],
        summed[1],
        summed[2],
        summed[3],
        summed[4],
        summed[5],
        summed[6],
        summed[7],
        summed[8],
    )


MESH = pl.DeviceIdType.MESH
SHORT = SIDE_S * SIDE_S + 1
WIDE = 256
LOW = jnp.bfloat16
F32 = jnp.float32
NEVER = -1e30

PLANS = "xyzyzxyyzxxyyxy"
ORDER = (
    (),
    (),
    (),
    (),
    (),
    (2, 42),
    (12,),
    (),
    (52, 22),
    (62,),
    (),
    (13,),
    (3,),
    (43,),
    (32,),
    (63, 53),
    (72,),
    (23,),
    (92,),
    (),
    (),
    (),
    (82,),
    (),
    (14, 102, 4, 44, 64, 33, 112, 54),
    (),
    (
        73, 24, 93, 122, 83, 15, 132, 103, 65, 34, 74, 113, 142, 152, 5, 45, 94, 55, 123, 84, 133,
        104, 35, 75, 143, 114, 25, 16, 66, 124, 153, 95, 134, 85, 144, 105, 115, 36, 76, 125, 154,
        135, 145, 116, 126, 155, 146,
    ),
)


def dot(left, right):
    return lax.dot_general(left, right, (((1,), (0,)), ((), ())), preferred_element_type=F32)


def dot_nt(left, right):
    return lax.dot_general(left, right, (((1,), (1,)), ((), ())), preferred_element_type=F32)


def dot_tn(left, right):
    return lax.dot_general(left, right, (((0,), (0,)), ((), ())), preferred_element_type=F32)


def rope_constants(rows):
    quarter = HD // 4
    freq = 10000.0 ** (-np.arange(quarter) / quarter)
    tables = []
    for side, length in ((SIDE_S, SIDE_S * SIDE_S + 1), (SIDE_L, SIDE_L * SIDE_L + 1)):
        place = np.arange(rows) - 1
        place = np.where((place >= 0) & (place < length - 1), place, 0)
        row = (place // side)[:, None] * freq
        col = (place % side)[:, None] * freq
        cosine = np.concatenate([np.cos(row), np.cos(row), np.cos(col), np.cos(col)], -1)
        sine = np.concatenate([-np.sin(row), np.sin(row), -np.sin(col), np.sin(col)], -1)
        tables += [np.concatenate([cosine, cosine], -1), np.concatenate([sine, sine], -1)]
    return np.stack(tables).astype(np.float32)


def swap_quarters(values):
    lane = lax.broadcasted_iota(jnp.int32, values.shape, 1)
    first = (lane % (HD // 2)) < HD // 4
    return jnp.where(
        first, pltpu.roll(values, 2 * HD - HD // 4, 1), pltpu.roll(values, HD // 4, 1)
    )


def fused(geo, *refs):
    rows_here, width, hidden_all = geo
    (
        lens, gain_a, gain_f, x_hbm, cot_hbm, tab_hbm,
        wq, wk, wv, wo, wg, wu, wd,
        bo_hbm, gi_hbm, fa_hbm, fd_hbm, fq_hbm, gain_hbm,
        x4, cot4, tab, wqkv_v, wo_v, wg_v, wu_v, wd_v,
        nrm, nrm_t, qkv, chance, mix_own, mix_in, mix, mix_t,
        mid, nf, nf_t, hid, hid_t, gg, gu, big,
        gnf_out, gnf_in, sb, rb, bo, bo_in, gb, gmx, ds_s, gqkv, sb2, rb2, gi, gi_in,
        gain_s, gain_x, gain_y, gain_z, gain_f_z, gain_c,
        pa, r1a, r2a, r3a, fa, pd, r1d, r2d, r3d, fd, pq, r1q, r2q, r3q, fq,
        sem_w, sem_in_s, sem_in_r, sem_core_s, sem_core_r, sem_gain_s, sem_gain_r, sem_o,
        sa_s, sa_r, sd_s, sd_r, sq_s, sq_r,
    ) = refs
    s = lax.axis_index("seq")
    i = lax.axis_index("items")
    y, c = s // 2, s % 2
    z, x = i // 2, i % 2
    rows = 4 * rows_here
    half = width // 2
    ff = hidden_all // 2
    pairs = half // 128
    step = rows_here
    fine = 32
    per = rows_here // step
    blocks = [(r0, min(256, rows - r0)) for r0 in range(0, rows, 256)]

    def device(y_to, c_to, z_to, x_to):
        return (y_to * 2 + c_to, z_to * 2 + x_to)

    sibling = device(y, 1 - c, z, x)
    y_dev = device(1 - y, c, z, x)
    x_dev = device(y, c, z, 1 - x)
    z_hi, z_lo = z // 2, z % 2
    near_z = device(y, c, z + 1 - 2 * z_lo, x)
    far_z = device(y, c, z + 2 - 4 * z_hi, x)

    started = []

    def send(src, dst, s_sem, r_sem, to):
        return pltpu.make_async_remote_copy(
            src_ref=src, dst_ref=dst, send_sem=s_sem, recv_sem=r_sem,
            device_id=to, device_id_type=MESH,
        )

    def weight_copies():
        copies = [pltpu.make_async_copy(tab_hbm, tab, sem_w.at[0])]
        mine = pl.ds(pl.multiple_of(c * half, half), half)
        for t, w in enumerate((wq, wk, wv)):
            copies.append(
                pltpu.make_async_copy(
                    w.at[:, mine], wqkv_v.at[:, pl.ds(t * half, half)], sem_w.at[1 + t]
                )
            )
        copies.append(pltpu.make_async_copy(wo, wo_v, sem_w.at[4]))
        for b in range(ff // 128):
            far = pl.ds(pl.multiple_of(256 * b + 128 * c, 128), 128)
            near = pl.ds(128 * b, 128)
            copies.append(pltpu.make_async_copy(wg.at[:, far], wg_v.at[:, near], sem_w.at[5 + 3 * b]))
            copies.append(pltpu.make_async_copy(wu.at[:, far], wu_v.at[:, near], sem_w.at[6 + 3 * b]))
            copies.append(pltpu.make_async_copy(wd.at[far], wd_v.at[near], sem_w.at[7 + 3 * b]))
        return copies

    weights = weight_copies()
    own_x = pltpu.make_async_copy(x_hbm.at[y], x4.at[s], sem_o.at[0])
    own_cot = pltpu.make_async_copy(cot_hbm.at[y], cot4.at[s], sem_o.at[1])
    own_x.start()
    for copy in weights[:4]:
        copy.start()

    barrier = pltpu.get_barrier_semaphore()
    for to in (sibling, y_dev, x_dev, near_z, far_z):
        pl.semaphore_signal(barrier, inc=1, device_id=to, device_id_type=MESH)
    pl.semaphore_wait(barrier, 5)

    s_y = (1 - y) * 2 + c
    part_rows = rows_here // 2
    across_x = [
        send(
            x_hbm.at[1 - y, pl.ds(n * part_rows, part_rows)], x4.at[s, pl.ds(n * part_rows, part_rows)],
            sem_in_s.at[8 + n], sem_in_r.at[8 + n], y_dev,
        )
        for n in range(2)
    ]
    beside_x = send(x_hbm.at[y], x4.at[s], sem_in_s.at[1], sem_in_r.at[1], sibling)
    for copy in across_x:
        copy.start()
    beside_x.start()
    across_c = send(cot_hbm.at[1 - y], cot4.at[s], sem_in_s.at[2], sem_in_r.at[2], y_dev)
    beside_c = send(cot_hbm.at[y], cot4.at[s], sem_in_s.at[3], sem_in_r.at[3], sibling)
    own_cot.start()
    for copy in weights[4:]:
        copy.start()
    relay_x = [
        send(
            x4.at[s_y, pl.ds(n * part_rows, part_rows)], x4.at[s_y, pl.ds(n * part_rows, part_rows)],
            sem_in_s.at[10 + n], sem_in_r.at[10 + n], sibling,
        )
        for n in range(2)
    ]
    relay_c = send(cot4.at[s_y], cot4.at[s_y], sem_in_s.at[5], sem_in_r.at[5], sibling)

    length = lens[y]

    def norm_rows(piece, n):
        here = pl.ds(n * part_rows, part_rows)
        values = x4[piece, here, :].astype(F32)
        scale = lax.rsqrt(jnp.mean(values * values, -1, keepdims=True) + epsilon)
        there = pl.ds(pl.multiple_of(piece * rows_here + n * part_rows, 16), part_rows)
        nrm[there, :] = (values * scale * gain_a[...]).astype(LOW)

    def project_rows(part):
        base = pl.multiple_of(part * 2 * rows_here, 32)
        here = pl.ds(base, 2 * rows_here)
        cosine = jnp.where(length == LONG, tab[2, here, :], tab[0, here, :])
        sine = jnp.where(length == LONG, tab[3, here, :], tab[1, here, :])
        for t in range(3):
            product = dot(nrm[here, :], wqkv_v[:, t * half : (t + 1) * half])
            for p in range(pairs):
                lanes = product[:, 128 * p : 128 * (p + 1)]
                if t < 2:
                    lanes = lanes * cosine + swap_quarters(lanes) * sine
                if t == 0:
                    lanes = lanes.astype(LOW).astype(F32) * HD ** (-0.5)
                qkv[t, here, 128 * p : 128 * (p + 1)] = lanes.astype(LOW)

    own_x.wait()
    for n in range(2):
        norm_rows(s, n)
    beside_x.wait_recv()
    for n in range(2):
        norm_rows(2 * y + 1 - c, n)
    for copy in weights[:4]:
        copy.wait()
    project_rows(y)
    for n in range(2):
        across_x[n].wait_recv()
        relay_x[n].start()
        norm_rows(s_y, n)
    across_c.start()
    beside_c.start()
    for n in range(2):
        relay_x[n].wait_recv()
        norm_rows(2 * (1 - y) + 1 - c, n)
    project_rows(1 - y)

    lane = lax.broadcasted_iota(jnp.int32, (1, 128), 1)
    left_head = lane < HD
    masks = [(lane // HD == n).astype(F32).astype(LOW) for n in range(2)]

    def mix_copy(pair):
        return send(
            mix_own.at[pair], mix_in.at[pair], sem_core_s.at[pair], sem_core_r.at[pair], sibling
        )

    tiles = blocks
    key = lax.broadcasted_iota(jnp.int32, (1, rows), 1)
    bias = jnp.where(key < length, 0.0, NEVER)

    def stacked(first, second):
        return jnp.concatenate([first, second], 0)

    def attend(pair, carry):
        lanes = pl.ds(pl.multiple_of(pair * 128, 128), 128)
        parts = []
        for k0, kb in tiles:
            query = qkv[0, k0:, lanes]
            part = dot_nt(stacked(query * masks[0], query * masks[1]), qkv[1, k0 : k0 + kb, lanes])
            parts.append(part + bias[:, k0 : k0 + kb] if k0 + kb > SHORT else part)
        for n in range(2):
            for r0, rb in blocks:
                scores = []
                for (k0, kb), part in zip(tiles, parts):
                    if k0 <= r0:
                        base = n * (rows - k0) + r0 - k0
                        here = part[base : base + rb]
                        if k0 == r0:
                            row = lax.broadcasted_iota(jnp.int32, here.shape, 0)
                            col = lax.broadcasted_iota(jnp.int32, here.shape, 1)
                            here = jnp.where(col <= row, here, NEVER)
                        scores.append((k0, kb, here))
                top = functools.reduce(jnp.maximum, [jnp.max(p, -1, keepdims=True) for _, _, p in scores])
                expo = [(k0, kb, jnp.exp(p - top)) for k0, kb, p in scores]
                inverse = 1.0 / sum(jnp.sum(p, -1, keepdims=True) for _, _, p in expo)
                for k0, kb, p in expo:
                    chance[pair * 2 + n, r0 : r0 + rb, k0 : k0 + kb] = (p * inverse).astype(LOW)
        outs = []
        for k0, kb in tiles:
            at = slice(k0, k0 + kb)
            low = stacked(chance[pair * 2, k0:, at], chance[pair * 2 + 1, k0:, at])
            outs.append(dot(low, qkv[2, at, lanes]))
        for r0, rb in blocks:
            both = []
            for n in range(2):
                at = [n * (rows - k0) + r0 - k0 for k0, _ in tiles if k0 <= r0]
                both.append(sum(out[b : b + rb] for b, out in zip(at, outs)))
            mix_own[pair, r0 : r0 + rb, :] = jnp.where(left_head, both[0], both[1]).astype(LOW)
        mix_copy(pair).start()
        return carry

    lax.fori_loop(0, pairs, attend, 0)

    across_c.wait_recv()
    relay_c.start()

    def turn_rows(src, dst):
        def one(b, carry):
            here = pl.ds(pl.multiple_of(b * 128, 128), 128)
            dst[:, here] = src[here, :].T
            return carry

        lax.fori_loop(0, rows // 128, one, 0)

    def place_mix(src, at):
        def one(p, carry):
            mix[:, pl.ds(pl.multiple_of(at * half + p * 128, 128), 128)] = src[p]
            return carry

        lax.fori_loop(0, pairs, one, 0)

    place_mix(mix_own, c)
    turn_rows(nrm, nrm_t)
    weights[4].wait()

    def chunk(n, wide=WIDE):
        return pl.ds(pl.multiple_of(n * wide, wide), wide)

    def heads_of_core(core):
        return pl.ds(pl.multiple_of(core * half, half), half)

    for n in range(width // WIDE):
        mid[:, chunk(n)] = (
            dot(mix[:, heads_of_core(c)], wo_v[heads_of_core(c), chunk(n)])
            + x4[:, :, chunk(n)].reshape(rows, WIDE).astype(F32)
        )
    for p in range(pairs):
        mix_copy(p).wait_recv()
    place_mix(mix_in, 1 - c)
    for n in range(width // WIDE):
        mid[:, chunk(n)] += dot(mix[:, heads_of_core(1 - c)], wo_v[heads_of_core(1 - c), chunk(n)])

    def second_norm(b, carry):
        here = pl.ds(pl.multiple_of(b * step, step), step)
        values = mid[here, :]
        scale = lax.rsqrt(jnp.mean(values * values, -1, keepdims=True) + epsilon)
        nf[here, :] = (values * scale * gain_f[...]).astype(LOW)
        return carry

    lax.fori_loop(0, rows // step, second_norm, 0)
    turn_rows(nf, nf_t)
    for copy in weights[5:]:
        copy.wait()
    own_cot.wait()
    beside_c.wait_recv()
    relay_c.wait_recv()

    class Group:
        def __init__(self, parts, r1, r2, r3, fin, s_sem, r_sem):
            self.parts, self.r1, self.r2, self.r3, self.fin = parts, r1, r2, r3, fin
            self.s_sem, self.r_sem = s_sem, r_sem

        def copy(self, k, n, src, dst, to):
            return send(src, dst, self.s_sem.at[k, n], self.r_sem.at[k, n], to)

        def step1(self, k):
            self.hop(k, 0).start()

        def to_core(self, k):
            return self.copy(k, 5, self.fin.at[k, c], self.fin.at[k, c], sibling)

        def finish(self, k, own, new):
            for h in range(2):
                total = self.r1[own + (h,)].astype(F32) + self.r3[k, new + h].astype(F32)
                self.fin[k, c, h] = total.astype(LOW)
            self.to_core(k).start()

        def end(self, k):
            self.to_core(k).wait_recv()

        def sent(self, k):
            for n in range(self.hops):
                self.hop(k, n).wait_send()
            self.to_core(k).wait_send()

    def add(ref, at, other, of):
        ref[at] = (ref[at].astype(F32) + other[of].astype(F32)).astype(LOW)

    class XZY(Group):
        hops = 4

        def hop(self, k, n):
            r1, r2, r3 = self.r1, self.r2, self.r3
            if n == 0:
                return self.copy(k, n, self.parts.at[k, :, :, 1 - x], r1.at[k], x_dev)
            if n == 1:
                return self.copy(k, n, r1.at[k, :, 1 - z_lo], r2.at[k], near_z)
            if n == 2:
                return self.copy(k, n, r1.at[k, 1 - z_hi, z_lo], r3.at[k, pl.ds(0, 2)], far_z)
            return self.copy(k, n, r1.at[k, z_hi, z_lo], r3.at[k, pl.ds(2, 2)], y_dev)

        def step2(self, k):
            self.hop(k, 0).wait_recv()
            for lo in (1 - z_lo, z_lo):
                for hi in range(2):
                    for h in range(2):
                        add(self.r1, (k, hi, lo, h), self.parts, (k, hi, lo, x, h))
                if lo is not z_lo:
                    self.hop(k, 1).start()

        def step3(self, k):
            self.hop(k, 1).wait_recv()
            for hi in (1 - z_hi, z_hi):
                for h in range(2):
                    add(self.r1, (k, hi, z_lo, h), self.r2, (k, hi, h))
                if hi is not z_hi:
                    self.hop(k, 2).start()

        def step4(self, k):
            self.hop(k, 2).wait_recv()
            for h in range(2):
                add(self.r1, (k, z_hi, z_lo, h), self.r3, (k, h))
            self.hop(k, 3).start()

        def step5(self, k):
            self.hop(k, 3).wait_recv()
            self.finish(k, (k, z_hi, z_lo), 2)

    class ZXY(Group):
        hops = 4

        def hop(self, k, n):
            r1, r2, r3 = self.r1, self.r2, self.r3
            if n == 0:
                return self.copy(k, n, self.parts.at[k, :, 1 - z_lo], r1.at[k], near_z)
            if n == 1:
                return self.copy(k, n, r1.at[k, 1 - z_hi], r2.at[k], far_z)
            if n == 2:
                return self.copy(k, n, r1.at[k, z_hi, 1 - x], r3.at[k, pl.ds(0, 2)], x_dev)
            return self.copy(k, n, r1.at[k, z_hi, x], r3.at[k, pl.ds(2, 2)], y_dev)

        def step2(self, k):
            self.hop(k, 0).wait_recv()
            for hi in (1 - z_hi, z_hi):
                for xx in range(2):
                    for h in range(2):
                        add(self.r1, (k, hi, xx, h), self.parts, (k, hi, z_lo, xx, h))
                if hi is not z_hi:
                    self.hop(k, 1).start()

        def step3(self, k):
            self.hop(k, 1).wait_recv()
            for xx in (1 - x, x):
                for h in range(2):
                    add(self.r1, (k, z_hi, xx, h), self.r2, (k, xx, h))
                if xx is not x:
                    self.hop(k, 2).start()

        def step4(self, k):
            self.hop(k, 2).wait_recv()
            for h in range(2):
                add(self.r1, (k, z_hi, x, h), self.r3, (k, h))
            self.hop(k, 3).start()

        def step5(self, k):
            self.hop(k, 3).wait_recv()
            self.finish(k, (k, z_hi, x), 2)

    class YXZ(Group):
        hops = 5

        def hop(self, k, n):
            r1, r2, r3 = self.r1, self.r2, self.r3
            if n == 0:
                return self.copy(k, n, self.parts.at[k, :, :, :, 1 - y], r1.at[k], y_dev)
            if n == 1:
                return self.copy(k, n, r1.at[k, :, :, 1 - x], r2.at[k], x_dev)
            if n == 2:
                return self.copy(k, n, r2.at[k, :, 1 - z_lo], r3.at[k, pl.ds(0, 2)], near_z)
            if n == 3:
                return self.copy(k, n, r2.at[k, 1 - z_hi, z_lo], r3.at[k, 2], far_z)
            return self.copy(k, n, self.fin.at[k, c, y], self.fin.at[k, c, y], y_dev)

        def beside(self, k, n):
            at = self.fin.at[k, c, y] if n == 0 else self.fin.at[k, c, 1 - y]
            return self.copy(k, 5 + n, at, at, sibling)

        def step2(self, k):
            self.hop(k, 0).wait_recv()
            for xx in (1 - x, x):
                for hi in range(2):
                    for lo in range(2):
                        add(self.r1, (k, hi, lo, xx), self.parts, (k, hi, lo, xx, y))
                if xx is not x:
                    self.hop(k, 1).start()

        def step3(self, k):
            self.hop(k, 1).wait_recv()
            for lo in (1 - z_lo, z_lo):
                for hi in range(2):
                    add(self.r2, (k, hi, lo), self.r1, (k, hi, lo, x))
                if lo is not z_lo:
                    self.hop(k, 2).start()

        def step4(self, k):
            self.hop(k, 2).wait_recv()
            for hi in (1 - z_hi, z_hi):
                add(self.r2, (k, hi, z_lo), self.r3, (k, hi))
                if hi is not z_hi:
                    self.hop(k, 3).start()

        def step5(self, k):
            self.hop(k, 3).wait_recv()
            total = self.r2[k, z_hi, z_lo].astype(F32) + self.r3[k, 2].astype(F32)
            self.fin[k, c, y] = total.astype(LOW)
            self.hop(k, 4).start()
            self.beside(k, 0).start()

        def step6(self, k):
            self.hop(k, 4).wait_recv()
            self.beside(k, 1).start()

        def end(self, k):
            for n in range(2):
                self.beside(k, n).wait_recv()

        def sent(self, k):
            for n in range(self.hops):
                self.hop(k, n).wait_send()
            for n in range(2):
                self.beside(k, n).wait_send()

    class Gains:
        def hop(self, k, n):
            src = (gain_s, gain_x, gain_y, gain_z, gain_s)[n]
            dst = (gain_x, gain_y, gain_z, gain_f_z, gain_c)[n]
            to = (x_dev, y_dev, near_z, far_z, sibling)[n]
            return send(src, dst, sem_gain_s.at[n], sem_gain_r.at[n], to)

        def step1(self, k):
            self.hop(k, 0).start()

        def step2(self, k):
            self.hop(k, 0).wait()
            gain_x[...] = gain_s[...] + gain_x[...]
            self.hop(k, 1).start()

        def step3(self, k):
            self.hop(k, 1).wait()
            gain_y[...] = gain_x[...] + gain_y[...]
            self.hop(k, 2).start()

        def step4(self, k):
            self.hop(k, 2).wait()
            gain_z[...] = gain_y[...] + gain_z[...]
            self.hop(k, 3).start()

        def step5(self, k):
            self.hop(k, 3).wait()
            gain_s[...] = gain_z[...] + gain_f_z[...]
            self.hop(k, 4).start()

        def end(self, k):
            self.hop(k, 4).wait()
            top = lax.broadcasted_iota(jnp.int32, gain_s.shape, 0) == 0
            total = gain_s[...] + jnp.where(top, gain_c[...], 0.0)
            gain_c[...] = pltpu.roll(total, lax.rem(8 - i, 8) * (width // 8), 1)

        def sent(self, k):
            pass

    buffers_a = (pa, r1a, r2a, r3a, fa, sa_s, sa_r)
    buffers_d = (pd, r1d, r2d, r3d, fd, sd_s, sd_r)
    buffers_q = (pq, r1q, r2q, r3q, fq, sq_s, sq_r)
    kinds = {"x": XZY, "y": YXZ, "z": ZXY}
    chunks = [(kinds[kind](*buffers_a), n) for n, kind in enumerate(PLANS[:8])]
    chunks += [(kinds[kind](*buffers_d), n) for n, kind in enumerate(PLANS[8:11])]
    chunks += [(kinds[kind](*buffers_q), n) for n, kind in enumerate(PLANS[11:])]
    chunks += [(Gains(), 0)]
    slots = iter(ORDER)

    def first(chunk):
        group, k = chunks[chunk]
        group.step1(k)

    def turn():
        for code in next(slots):
            group, k = chunks[code // 10]
            getattr(group, f"step{code % 10}")(k)

    chunks_f = ff // WIDE
    chunks_w = width // WIDE

    def feed(n, carry):
        at = chunk(n)
        big[:, 0:WIDE] = dot(nf[...], wg_v[:, at])
        big[:, WIDE : 2 * WIDE] = dot(nf[...], wu_v[:, at])
        big[:, 2 * WIDE : 3 * WIDE] = dot_nt(cot4[...].reshape(rows, width), wd_v[at, :])

        def one(b, inner):
            here = pl.ds(pl.multiple_of(b * fine, fine), fine)
            gate = big[here, 0:WIDE]
            up = big[here, WIDE : 2 * WIDE]
            back = big[here, 2 * WIDE : 3 * WIDE]
            sigma = 0.5 * jnp.tanh(0.5 * gate) + 0.5
            silu = gate * sigma
            hid[here, at] = (silu * up).astype(LOW)
            gg[here, at] = (back * up * (sigma + silu * (1.0 - sigma))).astype(LOW)
            gu[here, at] = (back * silu).astype(LOW)
            return inner

        lax.fori_loop(0, rows // fine, one, 0, unroll=5)
        shape = pa.shape[1:]
        pa[n] = dot(nf_t[...], gg[:, at]).reshape(shape).astype(LOW)
        first(n)
        pa[n + chunks_f] = dot(nf_t[...], gu[:, at]).reshape(shape).astype(LOW)
        first(n + chunks_f)
        hid_t[at, :] = hid[:, at].T
        return carry

    for n in range(chunks_f):
        turn()
        feed(n, 0)
    turn()

    def gnf_copy(n):
        return send(
            gnf_out.at[n], gnf_in.at[n], sem_core_s.at[pairs + n], sem_core_r.at[pairs + n], sibling
        )

    def back_ffn(n, carry):
        partial = dot_nt(gg[...], wg_v[chunk(n), :]) + dot_nt(gu[...], wu_v[chunk(n), :])
        big[:, chunk(n)] = partial
        gnf_out[n] = partial.astype(LOW)
        gnf_copy(n).start()
        return carry

    for n in range(chunks_w):
        back_ffn(n, 0)
        turn()

    def down(n, carry):
        big[:, chunk(n + chunks_w)] = dot(hid[...], wd_v[:, chunk(n)])
        return carry

    lax.fori_loop(0, chunks_w, down, 0)
    n_core = pairs + chunks_w
    bo_copy = send(sb, rb, sem_core_s.at[n_core], sem_core_r.at[n_core], sibling)
    far = slice(width, 2 * width)

    def for_rows(core, fn):
        for yy in range(2):
            def one(b, carry, yy=yy):
                base = pl.multiple_of((2 * yy + core) * rows_here + b * step, step)
                fn(yy, b, pl.ds(base, step), pl.ds(pl.multiple_of(b * step, step), step))
                return carry

            lax.fori_loop(0, per, one, 0)

    def pack_bo(yy, b, here, there):
        sb[yy, there, :] = big[here, far].astype(LOW)

    for_rows(1 - c, pack_bo)
    bo_copy.start()

    for n in range(chunks_w):
        turn()
        at = slice(n * WIDE, (n + 1) * WIDE)
        pd[n] = (
            dot(hid_t[...], cot4[:, :, at].reshape(rows, WIDE)).reshape(pd.shape[1:]).astype(LOW)
        )
        first(8 + n)

    turn()
    bo_copy.wait_recv()

    def finish_bo(yy, b, here, there):
        bo[yy, there, :] = (mid[here, :] + big[here, far] + rb[yy, there, :].astype(F32)).astype(LOW)

    for_rows(c, finish_bo)
    bo_across = send(bo.at[1 - y], bo_in, sem_in_s.at[6], sem_in_r.at[6], y_dev)
    bo_across.start()

    turn()
    for n in range(chunks_w):
        gnf_copy(n).wait_recv()

    def middle_back(b, total):
        here = pl.ds(pl.multiple_of(b * step, step), step)
        values = mid[here, :]
        grad = big[here, 0:width] + jnp.concatenate(
            [gnf_in[n, here, :].astype(F32) for n in range(chunks_w)], -1
        )
        scale = lax.rsqrt(jnp.mean(values * values, -1, keepdims=True) + epsilon)
        unit = values * scale
        total = total + (grad * unit).reshape(step // 8, 8, width).sum(0)
        scaled = grad * gain_f[...]
        inner = jnp.mean(scaled * unit, -1, keepdims=True)
        out = cot4[b // per, pl.ds(pl.multiple_of(lax.rem(b, per) * step, step), step), :].astype(F32)
        out = out + scale * (scaled - unit * inner)
        mid[here, :] = out
        gb[here, :] = out.astype(LOW)
        return total

    total_f = lax.fori_loop(0, rows // step, middle_back, jnp.zeros((8, width), F32))

    turn()
    turn_rows(mix, mix_t)
    mine = pl.ds(pl.multiple_of(c * half, half), half)
    pq[0] = dot(mix_t[...], gb[:, mine]).reshape(pq.shape[1:]).astype(LOW)
    first(11)
    gmx[...] = dot_nt(gb[...], wo_v[mine, :]).astype(LOW)

    def query_back(pair):
        lanes = slice(pair * 128, pair * 128 + 128)
        grads = []
        for k0, kb in tiles:
            grad = gmx[k0:, lanes]
            grads.append(
                dot_nt(stacked(grad * masks[0], grad * masks[1]), qkv[2, k0 : k0 + kb, lanes])
            )
        for n in range(2):
            for r0, rb in blocks:
                both = []
                for (k0, kb), grad in zip(tiles, grads):
                    if k0 <= r0:
                        base = n * (rows - k0) + r0 - k0
                        prob = chance[pair * 2 + n, r0 : r0 + rb, k0 : k0 + kb].astype(F32)
                        both.append((slice(k0, k0 + kb), prob, grad[base : base + rb] * prob))
                inner = sum(jnp.sum(each, -1, keepdims=True) for _, _, each in both)
                for at, prob, each in both:
                    ds_s[n, r0 : r0 + rb, at] = (each - prob * inner).astype(LOW)
        outs = []
        for k0, kb in tiles:
            at = slice(k0, k0 + kb)
            outs.append(dot(stacked(ds_s[0, k0:, at], ds_s[1, k0:, at]), qkv[1, at, lanes]))
        for r0, rb in blocks:
            both = []
            for n in range(2):
                at = [n * (rows - k0) + r0 - k0 for k0, _ in tiles if k0 <= r0]
                both.append(sum(out[b : b + rb] for b, out in zip(at, outs)))
            big[r0 : r0 + rb, 0:128] = jnp.where(left_head, both[0], both[1])

    def keys_back(pair):
        lanes = slice(pair * 128, pair * 128 + 128)

        def beside(first, second):
            return jnp.concatenate([first, second], 1)

        for k0, kb in tiles:
            at = slice(k0, k0 + kb)
            out = dot_tn(beside(ds_s[0, k0:, at], ds_s[1, k0:, at]), qkv[0, k0:, lanes])
            big[at, 128:256] = jnp.where(left_head, out[:kb], out[kb:])
            low = beside(chance[pair * 2, k0:, at], chance[pair * 2 + 1, k0:, at])
            out = dot_tn(low, gmx[k0:, lanes])
            big[at, 256:384] = jnp.where(left_head, out[:kb], out[kb:])

        def one(b, inner):
            here = pl.ds(pl.multiple_of(b * 64, 64), 64)
            cosine = jnp.where(length == LONG, tab[2, here, :], tab[0, here, :])
            sine = jnp.where(length == LONG, tab[3, here, :], tab[1, here, :])
            for t in range(3):
                values = big[here, 128 * t : 128 * (t + 1)]
                if t == 0:
                    values = values * HD ** (-0.5)
                if t < 2:
                    values = values * cosine - swap_quarters(values) * sine
                gqkv[here, t * half + pair * 128 : t * half + pair * 128 + 128] = values.astype(LOW)
            return inner

        lax.fori_loop(0, rows // 64, one, 0, unroll=5)

    for pair in range(pairs):
        turn()
        query_back(pair)
        turn()
        keys_back(pair)

    for t in range(3):
        turn()
        pq[1 + t] = (
            dot(nrm_t[...], gqkv[:, t * half : (t + 1) * half]).reshape(pq.shape[1:]).astype(LOW)
        )
        first(12 + t)

    turn()

    def back_attn(n, carry):
        big[:, chunk(n)] = dot_nt(gqkv[...], wqkv_v[chunk(n), :])
        return carry

    lax.fori_loop(0, chunks_w, back_attn, 0)
    turn()

    def pack_gi(yy, b, here, there):
        sb2[yy, there, :] = big[here, 0:width].astype(LOW)

    for_rows(1 - c, pack_gi)
    gi_copy = send(sb2, rb2, sem_core_s.at[n_core + 1], sem_core_r.at[n_core + 1], sibling)
    gi_copy.start()

    def gain_back(b, total):
        here = pl.ds(pl.multiple_of(b * step, step), step)
        values = x4[b // per, pl.ds(pl.multiple_of(lax.rem(b, per) * step, step), step), :].astype(F32)
        scale = lax.rsqrt(jnp.mean(values * values, -1, keepdims=True) + epsilon)
        return total + (big[here, 0:width] * (values * scale)).reshape(step // 8, 8, width).sum(0)

    total_a = lax.fori_loop(0, rows // step, gain_back, jnp.zeros((8, width), F32))
    row = lax.broadcasted_iota(jnp.int32, (8, width), 0)
    gain_s[...] = jnp.where(
        row == 0, jnp.sum(total_a, 0, keepdims=True), jnp.sum(total_f, 0, keepdims=True)
    )
    first(15)
    turn()
    gi_copy.wait_recv()

    def finish_gi(yy, b, here, there):
        values = x4[2 * yy + c, there, :].astype(F32)
        scale = lax.rsqrt(jnp.mean(values * values, -1, keepdims=True) + epsilon)
        unit = values * scale
        scaled = (big[here, 0:width] + rb2[yy, there, :].astype(F32)) * gain_a[...]
        inner = jnp.mean(scaled * unit, -1, keepdims=True)
        gi[yy, there, :] = (mid[here, :] + scale * (scaled - unit * inner)).astype(LOW)

    for_rows(c, finish_gi)
    gi_across = send(gi.at[1 - y], gi_in, sem_in_s.at[7], sem_in_r.at[7], y_dev)
    gi_across.start()

    outs = [
        pltpu.make_async_copy(bo.at[y], bo_hbm.at[y], sem_o.at[6]),
        pltpu.make_async_copy(gi.at[y], gi_hbm.at[y], sem_o.at[7]),
        pltpu.make_async_copy(bo_in, bo_hbm.at[1 - y], sem_o.at[8]),
        pltpu.make_async_copy(gi_in, gi_hbm.at[1 - y], sem_o.at[9]),
        pltpu.make_async_copy(fa, fa_hbm, sem_o.at[2]),
        pltpu.make_async_copy(fd, fd_hbm, sem_o.at[3]),
        pltpu.make_async_copy(fq, fq_hbm, sem_o.at[4]),
        pltpu.make_async_copy(gain_c, gain_hbm, sem_o.at[5]),
    ]
    outs[0].start()
    outs[1].start()
    turn()
    bo_across.wait_recv()
    outs[2].start()
    gi_across.wait_recv()
    outs[3].start()
    for n, part in enumerate((chunks[:8], chunks[8:11], chunks[11:15], chunks[15:])):
        for group, k in part:
            group.end(k)
        outs[4 + n].start()
    for copy in outs:
        copy.wait()

    for copy in (*across_x, beside_x, across_c, beside_c, *relay_x, relay_c, bo_across, gi_across):
        copy.wait_send()
    for p in range(pairs):
        mix_copy(p).wait_send()
    for n in range(chunks_w):
        gnf_copy(n).wait_send()
    bo_copy.wait_send()
    gi_copy.wait_send()
    for group, k in chunks:
        group.sent(k)


def spread(chunks_f, share, *refs):
    fa_far, fd_far, fq_far, bo, gi, gains_far = refs[:6]
    outs, (fa, fd, fq, gains), stage, sem_in, sem_out = refs[6:17], refs[17:21], refs[21:28], *refs[28:]
    bo_out, gi_out, da, df = outs[0], outs[1], outs[2], outs[7]
    ends = outs[3:7] + outs[8:]
    dq, dk, dv, do, dg, du, dd = stage
    near = [
        pltpu.make_async_copy(a, b, sem_in.at[n])
        for n, (a, b) in enumerate(
            [(fa_far.at[:chunks_f], fa.at[:chunks_f]), (fa_far.at[chunks_f:], fa.at[chunks_f:])]
            + [(fd_far, fd), (fq_far, fq), (gains_far, gains), (bo, bo_out), (gi, gi_out)]
        )
    ]
    for copy in near:
        copy.start()
    done = [pltpu.make_async_copy(a, b, sem_out.at[n]) for n, (a, b) in enumerate(zip(stage, ends))]
    rows, half, deep = fa.shape[3], fq.shape[4], fd.shape[3]
    halves = [(core, h, slice(h * rows, (h + 1) * rows)) for core in range(2) for h in range(2)]

    for first, ref, copy in ((0, dg, 0), (chunks_f, du, 1)):
        near[copy].wait()
        for core, h, at in halves:
            for n in range(chunks_f):
                for b in range(WIDE // 128):
                    far = 256 * (n * (WIDE // 128) + b) + 128 * core
                    ref[at, far : far + 128] = fa[
                        n + first, core, h, :, 128 * b : 128 * (b + 1)
                    ].astype(F32)
        done[4 + copy].start()
    near[2].wait()
    for core, h, _ in halves:
        at = slice((2 * core + h) * deep, (2 * core + h + 1) * deep)
        for n in range(fd.shape[0]):
            dd[at, WIDE * n : WIDE * (n + 1)] = fd[n, core, h].astype(F32)
    done[6].start()
    near[3].wait()
    for n, (ref, end) in enumerate(((do, 3), (dq, 0), (dk, 1), (dv, 2))):
        for core, h, at in halves:
            ref[at, core * half : (core + 1) * half] = fq[n, core, h].astype(F32)
        done[end].start()
    near[4].wait()
    da[...] = gains[0, 0:share]
    df[...] = gains[1, 0:share]
    near[5].wait()
    near[6].wait()
    for copy in done:
        copy.wait()


def item_per_chip(
    block_in, lengths, gain_attn, w_query, w_key, w_value, w_out, gain_ffn, w_gate, w_up, w_down,
    cotangent,
):
    _, rows_here, width = block_in.shape
    hidden_all = w_gate.shape[1]
    rows = rows_here * lax.axis_size("seq")
    shares = lax.axis_size("items")
    half, ff = width // 2, hidden_all // 2
    pairs = half // 128
    chunks_f, chunks_w = ff // WIDE, width // WIDE
    thin, deep = width // shares // 2, ff // shares // 2
    tables = jnp.asarray(rope_constants(rows))
    any_ = pl.BlockSpec(memory_space=pl.ANY)
    vmem = pl.BlockSpec(memory_space=pltpu.VMEM)

    def group(n, r, w):
        return [
            pltpu.VMEM((n, 2, 2, 2, 2, r, w), LOW),
            pltpu.VMEM((n, 2, 2, 2, r, w), LOW),
            pltpu.VMEM((n, 2, 2, r, w), LOW),
            pltpu.VMEM((n, 4, r, w), LOW),
            pltpu.VMEM((n, 2, 2, r, w), LOW),
        ]

    def low(*shape):
        return pltpu.VMEM(shape, LOW)

    def full(*shape):
        return pltpu.VMEM(shape, F32)

    dma = pltpu.SemaphoreType.DMA
    scratch = [
        low(4, rows_here, width), low(4, rows_here, width), full(4, rows, 128),
        low(width, 3 * half), low(width, width), low(width, ff), low(width, ff), low(ff, width),
        low(rows, width), low(width, rows), low(3, rows, half), low(2 * pairs, rows, rows),
        low(pairs, rows, 128), low(pairs, rows, 128), low(rows, width), low(width, rows),
        full(rows, width), low(rows, width), low(width, rows), low(rows, ff), low(ff, rows),
        low(rows, ff), low(rows, ff), full(rows, 2 * width),
        low(chunks_w, rows, WIDE), low(chunks_w, rows, WIDE),
        low(2, rows_here, width), low(2, rows_here, width),
        low(2, rows_here, width), low(rows_here, width),
        low(rows, width), low(rows, half), low(2, rows, rows), low(rows, 3 * half),
        low(2, rows_here, width), low(2, rows_here, width),
        low(2, rows_here, width), low(rows_here, width),
        full(8, width), full(8, width), full(8, width), full(8, width), full(8, width), full(8, width),
    ]
    scratch += group(2 * chunks_f, thin, WIDE) + group(chunks_w, deep, WIDE) + group(4, thin, half)
    scratch += [
        dma((5 + 3 * (ff // 128),)), dma((12,)), dma((12,)),
        dma((pairs + chunks_w + 2,)), dma((pairs + chunks_w + 2,)), dma((6,)), dma((6,)), dma((10,)),
        dma((2 * chunks_f, 8)), dma((2 * chunks_f, 8)), dma((chunks_w, 8)), dma((chunks_w, 8)),
        dma((4, 8)), dma((4, 8)),
    ]
    shape = jax.ShapeDtypeStruct
    bo, gi, fa, fd, fq, gains = pl.pallas_call(
        functools.partial(fused, (rows_here, width, hidden_all)),
        out_shape=(
            shape(block_in.shape, LOW), shape(block_in.shape, LOW),
            shape((2 * chunks_f, 2, 2, thin, WIDE), LOW), shape((chunks_w, 2, 2, deep, WIDE), LOW),
            shape((4, 2, 2, thin, half), LOW), shape((8, width), F32),
        ),
        in_specs=[pl.BlockSpec(memory_space=pltpu.SMEM), vmem, vmem] + [any_] * 10,
        out_specs=(any_,) * 6,
        scratch_shapes=scratch,
        compiler_params=pltpu.CompilerParams(
            collective_id=0, has_side_effects=True, vmem_limit_bytes=63 * 2**20
        ),
        name="block",
    )(
        lengths, gain_attn, gain_ffn, block_in, cotangent, tables,
        w_query, w_key, w_value, w_out, w_gate, w_up, w_down,
    )
    thick = (width // shares, width)
    made = (fa, fd, fq, bo, gi, gains)
    share = width // shares
    bo, gi, da, dq, dk, dv, do, df, dg, du, dd = pl.pallas_call(
        functools.partial(spread, chunks_f, share),
        out_shape=(
            shape(block_in.shape, LOW), shape(block_in.shape, LOW), shape((share,), F32),
            shape(thick, F32), shape(thick, F32), shape(thick, F32), shape(thick, F32),
            shape((share,), F32),
            shape((width // shares, hidden_all), F32), shape((width // shares, hidden_all), F32),
            shape((hidden_all // shares, width), F32),
        ),
        in_specs=[any_] * 6,
        out_specs=(vmem,) * 3 + (any_,) * 4 + (vmem,) + (any_,) * 3,
        scratch_shapes=[pltpu.VMEM(a.shape, a.dtype) for a in (fa, fd, fq, gains)]
        + [pltpu.VMEM(thick, F32)] * 4
        + [pltpu.VMEM((width // shares, hidden_all), F32)] * 2
        + [pltpu.VMEM((hidden_all // shares, width), F32), dma((7,)), dma((7,))],
        compiler_params=pltpu.CompilerParams(vmem_limit_bytes=60 * 2**20),
        name="spread",
    )(*made)
    return bo, gi, da, dq, dk, dv, do, df, dg, du, dd


def solution(mesh):
    fits = mesh.shape["seq"] == 4 and mesh.shape["items"] == 8
    return jax.shard_map(
        item_per_chip if fits else body,
        mesh=mesh,
        in_specs=(P("items", "seq", None), P("items")) + (P(),) * 9 + (P("items", "seq", None),),
        out_specs=(
            (P("items", "seq", None),) * 2
            + (P("items"),) + (P("items", None),) * 4
            + (P("items"),) + (P("items", None),) * 3
        ),
        check_vma=False,
    )
```
